32 devices in a mesh: pool: 16 (over z, y, core), tp: 2 (over x).
Axes of the slice: x: 2, y: 2, z: 4, core: 2. Of those that a mesh axis runs over, the one named last changes fastest.
Arguments:
- queries: bfloat16 [4096, 4096], P('pool', 'tp'), may hold values from -8 to 8
- new_key_values: bfloat16 [4096, 2048], P('pool', 'tp'), may hold values from -6 to 6
- key_value_store: bfloat16 [384, 256, 2048], P('pool', None, 'tp'), may hold values from -6 to 6
- o_weight: bfloat16 [4096, 8192], P('tp'), may hold values from -0.09375 to 0.09375
- residual: bfloat16 [4096, 8192], P(('pool', 'tp')), may hold values from -6 to 6
- hit_dev: int32 [32, 16], replicated, may hold values from 0 to 15, as said below
- hit_blk: int32 [32, 16], replicated, may hold values from 0 to 23
- prefix_len: int32 [32], replicated, may hold values from 3072 to 4096, as said below
Outputs:
- layer_out: bfloat16 [4096, 8192], P(('pool', 'tp'))
The draws below stay inside these ranges and needn't reach their ends.
Inputs may be any that keep to these rules, and one draw needn't show every extreme that they name: `hit_dev`: within one request the 16 pool indices are distinct. So one pool index sends at most one used block to each request, and at most 2 to the 2 requests held by any one pool index. `prefix_len`: some request has the full 16 * 256 tokens.
All inputs are finite; a program needn't handle non-finite values.
Results may differ from the reference program's by a relative error of at most 0.0085.
Values may be sent and summed in bfloat16 or wider, within the bound.
No kernel may reach another device: no remote copies, remote signals or barrier semaphores. Data moves between devices by JAX's collectives and lax.ppermute only.
A program may use at most 192 MiB of HBM per device.

```python
import jax
import jax.numpy as jnp
from jax import lax

D = 8192
HEAD_SIZE = 128
QUERY_HEADS = 32
KEY_VALUE_HEADS = 8
NEW_TOKEN_COUNT = 128
PREFIX_BLOCK_LEN = 256
MAXB = 16
POOL_BLK = 24
REQ_DEV = 2
REQ = 32
ALL_NEW_TOKENS = 4096
STORED_BLOCK_NUM = 384
N_TP = 2


def draw_queries(key, part):
    key = jax.random.fold_in(key, 1)
    first = jax.random.fold_in(key, 0)
    array_shape = (ALL_NEW_TOKENS, QUERY_HEADS * HEAD_SIZE)
    values = jnp.clip(2.0 * jax.random.normal(first, array_shape, jnp.float32), -8.0, 8.0)
    return values.astype(jnp.bfloat16)


def draw_key_value_store(key, part):
    key = jax.random.fold_in(key, 2)
    first = jax.random.fold_in(key, 0)
    array_shape = (STORED_BLOCK_NUM, PREFIX_BLOCK_LEN, KEY_VALUE_HEADS * 2 * HEAD_SIZE)
    values = jnp.clip(jax.random.normal(first, array_shape, jnp.float32), -6.0, 6.0)
    return values.astype(jnp.bfloat16)


def draw_hit_dev(key, part):
    key = jax.random.fold_in(key, 3)
    first, second = jax.random.split(key, 2)
    npool = REQ // REQ_DEV
    keys = jax.random.split(first, REQ)
    perms = jax.vmap(lambda k: jax.random.permutation(k, npool))(keys).astype(jnp.int32)
    perms = perms.reshape(npool, REQ_DEV, npool)
    target = perms[:, 0, 0]
    where_at = jnp.argmax(perms == target[:, None, None], axis=2)
    leading = perms[:, :, 0]
    places = jnp.arange(npool, dtype=jnp.int32)
    moved = jnp.where(places[None, None, :] == where_at[:, :, None], leading[:, :, None], perms)
    moved = jnp.where(places[None, None, :] == 0, target[:, None, None], moved)
    chosen = jax.random.randint(second, (), 0, npool)
    flag = (jnp.arange(npool) == chosen)[:, None, None]
    result = jnp.where(flag, moved, perms)
    return result[:, :, :MAXB].reshape(REQ, MAXB).astype(jnp.int32)


def draw_prefix_len(key, part):
    key = jax.random.fold_in(key, 4)
    first, second = jax.random.split(key, 2)
    lengths = jax.random.randint(first, (REQ,), 3 * MAXB * PREFIX_BLOCK_LEN // 4, MAXB * PREFIX_BLOCK_LEN + 1)
    longest = jax.random.randint(second, (), 0, REQ)
    lengths = jnp.where(jnp.arange(REQ) == longest, MAXB * PREFIX_BLOCK_LEN, lengths)
    return lengths.astype(jnp.int32)


def touch_ends(entries, stream_key, smallest, high):
    spot = [jax.random.randint(jax.random.fold_in(stream_key, axis), (), 0, length) for axis, length in enumerate(entries.shape)]
    widest = entries.shape.index(max(entries.shape))
    next_to = spot[:widest] + [(spot[widest] + 1) % entries.shape[widest]] + spot[widest + 1:]
    return entries.at[tuple(spot)].set(smallest).at[tuple(next_to)].set(high)


def shard_levels(key, shape, pieces, low, largest):
    def one(axis_at, parts):
        steps = jax.random.uniform(jax.random.fold_in(jax.random.fold_in(key, 6), axis_at), (parts,), jnp.float32, low / len(pieces), largest / len(pieces))
        return jnp.repeat(jnp.exp(steps), shape[axis_at] // parts).reshape((-1,) + (1,) * (len(shape) - axis_at - 1))

    gain = one(*pieces[0])
    for cut in pieces[1:]:
        gain = gain * one(*cut)
    return gain


def normal_values(stream_key, extent, scale, bound, shards=(), kind=jnp.bfloat16):
    gain = shard_levels(stream_key, extent, shards, -0.22, 0.18) if shards else 1.0
    values = jax.random.normal(stream_key, extent, jnp.float32) * scale * gain
    return jnp.minimum(jnp.maximum(values, -bound), bound).astype(kind)


def setup_inputs(seed: int = 0) -> dict:
    key_of = jax.random.split(jax.random.key(seed), 9)
    queries = draw_queries(jax.random.fold_in(key_of[8], 71), 0)
    new_key_values = normal_values(key_of[1], (ALL_NEW_TOKENS, KEY_VALUE_HEADS * 2 * HEAD_SIZE), 1.0, 6.0, ((0, 16), (1, 2)))
    key_value_store = draw_key_value_store(jax.random.fold_in(key_of[8], 71), 0)
    o_weight = normal_values(key_of[3], (QUERY_HEADS * HEAD_SIZE, D), (QUERY_HEADS * HEAD_SIZE) ** -0.5, 0.09375, ((0, 2),))
    residual = normal_values(key_of[4], (ALL_NEW_TOKENS, D), 1.0, 6.0, ((0, 32),))
    hit_dev = draw_hit_dev(jax.random.fold_in(key_of[8], 71), 0)
    hit_blk = touch_ends(jax.random.randint(key_of[6], (REQ, MAXB), 0, POOL_BLK), jax.random.fold_in(key_of[6], 1), 0, POOL_BLK - 1).astype(jnp.int32)
    prefix_len = draw_prefix_len(jax.random.fold_in(key_of[8], 71), 0)
    return {"queries": queries, "new_key_values": new_key_values, "key_value_store": key_value_store, "o_weight": o_weight, "residual": residual, "hit_dev": hit_dev, "hit_blk": hit_blk, "prefix_len": prefix_len}


def reference(queries, new_key_values, key_value_store, o_weight, residual, hit_dev, hit_blk, prefix_len):
    query_group = QUERY_HEADS // KEY_VALUE_HEADS
    token_span = MAXB * PREFIX_BLOCK_LEN

    def one(request_index):
        block_index = hit_dev[request_index] * POOL_BLK + hit_blk[request_index]
        prefix_blocks = jnp.take(key_value_store, block_index, axis=0).reshape(token_span, KEY_VALUE_HEADS, 2, HEAD_SIZE)
        fresh_tokens = lax.dynamic_slice_in_dim(new_key_values, request_index * NEW_TOKEN_COUNT, NEW_TOKEN_COUNT, 0).reshape(NEW_TOKEN_COUNT, KEY_VALUE_HEADS, 2, HEAD_SIZE)
        keys = jnp.concatenate([prefix_blocks[:, :, 0], fresh_tokens[:, :, 0]], 0).astype(jnp.float32)
        values = jnp.concatenate([prefix_blocks[:, :, 1], fresh_tokens[:, :, 1]], 0).astype(jnp.float32)
        query_rows = lax.dynamic_slice_in_dim(queries, request_index * NEW_TOKEN_COUNT, NEW_TOKEN_COUNT, 0).reshape(NEW_TOKEN_COUNT, KEY_VALUE_HEADS, query_group, HEAD_SIZE).astype(jnp.float32)
        scores = jnp.einsum("ihgd,jhd->hgij", query_rows, keys) * (HEAD_SIZE ** -0.5)
        valid = jnp.arange(token_span, dtype=jnp.int32) < prefix_len[request_index]
        causal = jnp.arange(NEW_TOKEN_COUNT, dtype=jnp.int32)[None, :] <= jnp.arange(NEW_TOKEN_COUNT, dtype=jnp.int32)[:, None]
        allowed = jnp.concatenate([jnp.broadcast_to(valid[None, :], (NEW_TOKEN_COUNT, token_span)), causal], 1)
        scores = jnp.where(allowed, scores, -jnp.inf)
        rowmax = jnp.max(scores, axis=-1, keepdims=True)
        expo = jnp.exp(scores - rowmax)
        denom = jnp.sum(expo, axis=-1)
        probs = expo.astype(jnp.bfloat16).astype(jnp.float32)
        mixed = jnp.einsum("hgij,jhd->ihgd", probs, values)
        mixed = mixed / jnp.transpose(denom, (2, 0, 1))[..., None]
        return mixed.reshape(NEW_TOKEN_COUNT, QUERY_HEADS * HEAD_SIZE).astype(jnp.bfloat16)

    attn = lax.map(one, jnp.arange(REQ, dtype=jnp.int32)).reshape(ALL_NEW_TOKENS, QUERY_HEADS * HEAD_SIZE)
    width = QUERY_HEADS * HEAD_SIZE // N_TP

    def add_group(g, total):
        left = lax.dynamic_slice_in_dim(attn, g * width, width, 1)
        right = lax.dynamic_slice_in_dim(o_weight, g * width, width, 0)
        part = jnp.dot(left, right, preferred_element_type=jnp.float32).astype(jnp.bfloat16)
        part = lax.optimization_barrier(part)
        return total + part.astype(jnp.float32)

    total = lax.fori_loop(0, N_TP, add_group, jnp.zeros((ALL_NEW_TOKENS, D), jnp.float32))
    return (total + residual.astype(jnp.float32)).astype(jnp.bfloat16)
```

```python
import functools

import jax
import jax.numpy as jnp
from jax import lax
from jax.experimental import pallas as pl
from jax.experimental.pallas import tpu as pltpu
from jax.sharding import PartitionSpec as P

HEAD_SIZE = 128
NEW_TOKEN_COUNT = 128
PREFIX_BLOCK_LEN = 256
MAXB = 16
LOG2E = 1.4426950408889634
SCALE2 = HEAD_SIZE ** (-0.5) * LOG2E
NEG = -1e30
F32 = jnp.float32
BF16 = jnp.bfloat16
TOK = NEW_TOKEN_COUNT
STAT = 128


def dot_nt(a, b):
    return lax.dot_general(a, b, (((1,), (1,)), ((), ())), preferred_element_type=F32)


def chip_ring(nchips):
    if nchips % 2:
        return list(range(nchips))
    up = list(range(0, nchips, 2))
    return up + [chip + 1 for chip in reversed(up)]


def pack_kernel(idx_ref, src_ref, dst_ref):
    dst_ref[...] = src_ref[...]


def pack_blocks(indices, store):
    count = indices.shape[0]
    _, rows, cols = store.shape
    return pl.pallas_call(
        pack_kernel,
        out_shape=jax.ShapeDtypeStruct((count, rows, cols), store.dtype),
        grid_spec=pltpu.PrefetchScalarGridSpec(
            num_scalar_prefetch=1,
            grid=(count,),
            in_specs=[pl.BlockSpec((1, rows, cols), lambda i, idx: (idx[i], 0, 0))],
            out_specs=pl.BlockSpec((1, rows, cols), lambda i, idx: (i, 0, 0)),
        ),
        cost_estimate=pl.CostEstimate(
            flops=0, bytes_accessed=4 * count * rows * cols, transcendentals=0
        ),
        name="pack_blocks",
    )(indices, store)


def attend_kernel(call, group, heads, has_carry, has_fresh, plan_ref, *refs):
    refs = list(refs)
    q_ref, own_ref, sib_ref = refs[:3]
    rest = refs[3:]
    fresh_ref = rest.pop(0) if has_fresh else None
    carry_ref = rest.pop(0) if has_carry else None
    out_ref = rest.pop(0)
    h = pl.program_id(0)
    width = group * HEAD_SIZE
    rows = group * TOK
    n_own = plan_ref[4 * call + 2]
    n_sib = plan_ref[4 * call + 3]

    q = jnp.concatenate(
        [q_ref[:, g * HEAD_SIZE : (g + 1) * HEAD_SIZE] for g in range(group)], axis=0
    )
    parts = [own_ref[0], sib_ref[0]]
    if has_fresh:
        parts.append(fresh_ref[...])
    keys = jnp.concatenate([x[:, :HEAD_SIZE] for x in parts], axis=0)
    values = jnp.concatenate([x[:, HEAD_SIZE:] for x in parts], axis=0)
    span = keys.shape[0]
    values = jnp.concatenate([values, jnp.ones((span, HEAD_SIZE), BF16)], axis=1)
    scores = dot_nt(q, keys)
    col = lax.broadcasted_iota(jnp.int32, (1, 2 * PREFIX_BLOCK_LEN), 1)
    limit = jnp.where(col < PREFIX_BLOCK_LEN, n_own, n_sib + PREFIX_BLOCK_LEN)
    bias = jnp.where(col < limit, 0.0, NEG).astype(F32)
    if has_fresh:
        tok = lax.broadcasted_iota(jnp.int32, (TOK, TOK), 0)
        new = lax.broadcasted_iota(jnp.int32, (TOK, TOK), 1)
        causal = jnp.where(new <= tok, 0.0, NEG).astype(F32)
        causal = jnp.concatenate([causal] * group, axis=0)
        scores = jnp.concatenate(
            [
                scores[:, : 2 * PREFIX_BLOCK_LEN] + bias,
                scores[:, 2 * PREFIX_BLOCK_LEN :] + causal,
            ],
            axis=1,
        )
    else:
        scores = scores + bias
    top = jnp.max(scores, axis=1, keepdims=True)
    probs = jnp.exp2((scores - top) * SCALE2).astype(BF16)
    mixed = jnp.dot(probs, values, preferred_element_type=F32)
    total = mixed[:, HEAD_SIZE:]
    out = mixed[:, :HEAD_SIZE] / total
    lse = top * SCALE2 + jnp.log2(total)

    lane = lax.broadcasted_iota(jnp.int32, (TOK, STAT), 1)
    stat_at = heads * HEAD_SIZE
    if has_carry:
        stat_in = carry_ref[:, stat_at : stat_at + STAT].astype(F32)
    old = out_ref[:, stat_at : stat_at + STAT].astype(F32)
    stat = jnp.where(h == 0, 0.0, old)
    pieces = []
    for g in range(group):
        head = h * group + g
        o_g = out[g * TOK : (g + 1) * TOK]
        lse_g = lse[g * TOK : (g + 1) * TOK]
        if has_carry:
            mine = (lax.rem(lane, heads) == head) & (lane < 3 * heads)
            lse_c = jnp.sum(jnp.where(mine, stat_in, 0.0), axis=1, keepdims=True)
            at = pl.multiple_of(head * HEAD_SIZE, HEAD_SIZE)
            o_c = carry_ref[:, pl.ds(at, HEAD_SIZE)].astype(F32)
            high = jnp.maximum(lse_g, lse_c)
            w_c = jnp.exp2(lse_c - high)
            w_g = jnp.exp2(lse_g - high)
            w = w_c + w_g
            o_g = (o_c * w_c + o_g * w_g) / w
            lse_g = high + jnp.log2(w)
        first = lse_g.astype(BF16).astype(F32)
        second = (lse_g - first).astype(BF16).astype(F32)
        third = lse_g - first - second
        stat = jnp.where(lane == head, first, stat)
        stat = jnp.where(lane == head + heads, second, stat)
        stat = jnp.where(lane == head + 2 * heads, third, stat)
        pieces.append(o_g.astype(BF16))
    at = pl.multiple_of(h * width, width)
    out_ref[:, pl.ds(at, width)] = jnp.concatenate(pieces, axis=1)
    out_ref[:, stat_at : stat_at + STAT] = stat.astype(BF16)


def attend(call, plan, q, store, sib, kv_local, fresh=None, carry=None):
    heads = q.shape[1] // HEAD_SIZE
    group = heads // kv_local
    width = group * HEAD_SIZE
    pair = 2 * HEAD_SIZE
    cols = heads * HEAD_SIZE + STAT
    span = 2 * PREFIX_BLOCK_LEN + (TOK if fresh is not None else 0)
    in_specs = [
        pl.BlockSpec((TOK, width), lambda h, plan: (0, h)),
        pl.BlockSpec((1, PREFIX_BLOCK_LEN, pair), lambda h, plan: (plan[4 * call], 0, h)),
        pl.BlockSpec((1, PREFIX_BLOCK_LEN, pair), lambda h, plan: (plan[4 * call + 1], 0, h)),
    ]
    args = [q, store, sib]
    if fresh is not None:
        in_specs.append(pl.BlockSpec((TOK, pair), lambda h, plan: (0, h)))
        args.append(fresh)
    if carry is not None:
        in_specs.append(pl.BlockSpec((TOK, cols), lambda h, plan: (0, 0)))
        args.append(carry)
    body = functools.partial(
        attend_kernel, call, group, heads, carry is not None, fresh is not None
    )
    return pl.pallas_call(
        body,
        out_shape=jax.ShapeDtypeStruct((TOK, cols), BF16),
        grid_spec=pltpu.PrefetchScalarGridSpec(
            num_scalar_prefetch=1,
            grid=(kv_local,),
            in_specs=in_specs,
            out_specs=pl.BlockSpec((TOK, cols), lambda h, plan: (0, 0)),
        ),
        compiler_params=pltpu.CompilerParams(vmem_limit_bytes=40 * 1024 * 1024),
        cost_estimate=pl.CostEstimate(
            flops=8 * heads * TOK * span * HEAD_SIZE,
            bytes_accessed=4 * TOK * cols + 4 * kv_local * span * pair,
            transcendentals=heads * TOK * span,
        ),
        name="attend",
    )(plan, *args)


def merge_parts(heads, part_refs, attn_ref):
    stat_at = heads * HEAD_SIZE
    stats = [ref[:, stat_at : stat_at + STAT].astype(F32) for ref in part_refs]
    for head in range(heads):
        lses = [
            s[:, head : head + 1]
            + s[:, head + heads : head + heads + 1]
            + s[:, head + 2 * heads : head + 2 * heads + 1]
            for s in stats
        ]
        high = functools.reduce(jnp.maximum, lses)
        weights = [jnp.exp2(x - high) for x in lses]
        norm = 1.0 / functools.reduce(jnp.add, weights)
        cols = slice(head * HEAD_SIZE, (head + 1) * HEAD_SIZE)
        mixed = functools.reduce(
            jnp.add, [w * ref[:, cols].astype(F32) for w, ref in zip(weights, part_refs)]
        )
        attn_ref[:, cols] = (mixed * norm).astype(BF16)


def project_kernel(heads, nparts, nadd, *refs):
    part_refs = refs[:nparts]
    w_ref = refs[nparts]
    add_refs = refs[nparts + 1 : nparts + 1 + nadd]
    out_ref, attn_ref = refs[nparts + 1 + nadd :]

    @pl.when(pl.program_id(0) == 0)
    def _():
        merge_parts(heads, part_refs, attn_ref)

    got = jnp.dot(attn_ref[...], w_ref[...], preferred_element_type=F32).astype(BF16)
    if nadd:
        total = got.astype(F32)
        for ref in add_refs:
            total = total + ref[...].astype(F32)
        got = total.astype(BF16)
    out_ref[...] = got


def project(parts, weight, adds=()):
    depth, model = weight.shape
    heads = depth // HEAD_SIZE
    cols = parts[0].shape[1]
    tile = 512
    in_specs = [pl.BlockSpec((TOK, cols), lambda j: (0, 0)) for _ in parts]
    in_specs.append(pl.BlockSpec((depth, tile), lambda j: (0, j)))
    in_specs += [pl.BlockSpec((TOK, tile), lambda j: (0, j)) for _ in adds]
    return pl.pallas_call(
        functools.partial(project_kernel, heads, len(parts), len(adds)),
        out_shape=jax.ShapeDtypeStruct((TOK, model), BF16),
        grid=(model // tile,),
        in_specs=in_specs,
        out_specs=pl.BlockSpec((TOK, tile), lambda j: (0, j)),
        scratch_shapes=[pltpu.VMEM((TOK, depth), BF16)],
        compiler_params=pltpu.CompilerParams(vmem_limit_bytes=40 * 1024 * 1024),
        cost_estimate=pl.CostEstimate(
            flops=2 * TOK * depth * model,
            bytes_accessed=2 * depth * model + 4 * TOK * model,
            transcendentals=0,
        ),
        name="project",
    )(*parts, weight, *adds)


def shards(
    queries, new_key_values, key_value_store, o_weight, residual, hit_dev, hit_blk, prefix_len
):
    npool = lax.axis_size("pool")
    ntp = lax.axis_size("tp")
    me = lax.axis_index("pool")
    tp = lax.axis_index("tp")
    rdev = queries.shape[0] // TOK
    kv_local = key_value_store.shape[2] // (2 * HEAD_SIZE)
    nchips = npool // 2
    core = lax.rem(me, 2)
    chip = lax.div(me, 2)
    sibling = me + 1 - 2 * core
    ring = chip_ring(nchips)
    place = [ring.index(i) for i in range(nchips)]
    split_rows = ntp == rdev and rdev == 2

    swap_perm = [(p, p + 1 - 2 * (p % 2)) for p in range(npool)]
    cw_perm, ccw_perm = [], []
    for k in range(nchips):
        a, b = ring[k], ring[(k + 1) % nchips]
        for c in range(2):
            cw_perm.append((2 * a + c, 2 * b + c))
            ccw_perm.append((2 * b + c, 2 * a + c))

    starts = jnp.arange(MAXB, dtype=jnp.int32)[None, :] * PREFIX_BLOCK_LEN
    left = jnp.clip(prefix_len[:, None] - starts, 0, PREFIX_BLOCK_LEN)
    here = hit_dev == me
    n_own = jnp.sum(jnp.where(here, left, 0), axis=1)
    blk_own = jnp.sum(jnp.where(here, hit_blk, 0), axis=1)
    n_sib = jnp.sum(jnp.where(hit_dev == sibling, left, 0), axis=1)

    def of_core(x, which):
        x = x.reshape(nchips, 2, rdev)
        return lax.dynamic_index_in_dim(x, which, 1, keepdims=False)

    blk_mine, blk_theirs = of_core(blk_own, core), of_core(blk_own, 1 - core)
    n_own, n_sib = of_core(n_own, core), of_core(n_sib, core)
    spot = jnp.asarray(place, jnp.int32)[chip]
    ring_at = jnp.asarray(ring, jnp.int32)
    steps = list(range(-(nchips // 2), nchips // 2 + 1))
    chips_at = ring_at[lax.rem(spot + nchips - jnp.asarray(steps, jnp.int32), nchips)]

    half = nchips // 2
    outs = []
    slots = [1 - tp, tp] if split_rows else list(range(rdev))
    state = []
    for order, slot in enumerate(slots):
        pick = lambda x: lax.dynamic_index_in_dim(x, slot, 1, keepdims=False)
        plan = jnp.stack(
            [pick(blk_mine)[chips_at], chips_at, pick(n_own)[chips_at], pick(n_sib)[chips_at]],
            axis=1,
        ).reshape(-1)
        q = lax.dynamic_slice_in_dim(queries, slot * TOK, TOK, 0)
        fresh = lax.dynamic_slice_in_dim(new_key_values, slot * TOK, TOK, 0)
        packed = pack_blocks(pick(blk_theirs), key_value_store)
        sib = lax.ppermute(packed, "pool", swap_perm)
        if nchips % 2:
            reach = (half, half)
        else:
            reach = (half, half - 1) if order % 2 == 0 else (half - 1, half)
        held = {}
        for sign, perm, hops in ((1, cw_perm, reach[0]), (-1, ccw_perm, reach[1])):
            moving = q
            for s in range(1, hops + 1):
                moving = lax.ppermute(moving, "pool", perm)
                held[sign * s] = moving
        state.append((plan, q, fresh, sib, reach, held))

    parts_of = []
    for plan, q, fresh, sib, reach, held in state:
        run = functools.partial(attend, store=key_value_store, sib=sib, kv_local=kv_local)
        call = lambda s: steps.index(s)
        own = run(call(0), plan, q, fresh=fresh)
        parts = [own]
        for sign, back, hops in ((1, ccw_perm, reach[0]), (-1, cw_perm, reach[1])):
            carry = None
            for s in range(hops, 0, -1):
                carry = run(call(sign * s), plan, held[sign * s], carry=carry)
                carry = lax.ppermute(carry, "pool", back)
            if carry is not None:
                parts.append(carry)
        parts_of.append(parts)

    if split_rows:
        away = project(parts_of[0], o_weight)
        got = lax.ppermute(away, "tp", [(0, 1), (1, 0)])
        return project(parts_of[1], o_weight, (got, residual))
    rows = jnp.concatenate([project(parts, o_weight) for parts in parts_of], axis=0)
    mine = lax.psum_scatter(rows, "tp", scatter_dimension=0, tiled=True)
    return (mine.astype(F32) + residual.astype(F32)).astype(BF16)


def solution(mesh):
    placed = (
        P("pool", "tp"),
        P("pool", "tp"),
        P("pool", None, "tp"),
        P("tp", None),
        P(("pool", "tp"), None),
        P(),
        P(),
        P(),
    )
    return jax.shard_map(
        shards, mesh=mesh, in_specs=placed, out_specs=P(("pool", "tp"), None), check_vma=False
    )
```

```python
import functools

import jax
import jax.numpy as jnp
from jax import lax
from jax.experimental import pallas as pl
from jax.experimental.pallas import tpu as pltpu
from jax.sharding import PartitionSpec as P

HEAD_SIZE = 128
NEW_TOKEN_COUNT = 128
PREFIX_BLOCK_LEN = 256
MAXB = 16
LOG2E = 1.4426950408889634
SCALE2 = HEAD_SIZE ** (-0.5) * LOG2E
NEG = -1e30
F32 = jnp.float32
BF16 = jnp.bfloat16
TOK = NEW_TOKEN_COUNT
STAT = 128


def dot_nt(a, b):
    return lax.dot_general(a, b, (((1,), (1,)), ((), ())), preferred_element_type=F32)


def chip_ring(nchips):
    if nchips % 2:
        return list(range(nchips))
    up = list(range(0, nchips, 2))
    return up + [chip + 1 for chip in reversed(up)]


def attend_kernel(call, group, heads, unroll, has_carry, has_fresh, plan_ref, *refs):
    refs = list(refs)
    q_ref, own_ref, sib_ref = refs[:3]
    rest = refs[3:]
    fresh_ref = rest.pop(0) if has_fresh else None
    carry_ref, carry_stat_ref = (rest.pop(0), rest.pop(0)) if has_carry else (None, None)
    out_ref, stat_ref = rest
    step = pl.program_id(0)
    width = group * HEAD_SIZE
    pair = 2 * HEAD_SIZE
    stat_at = heads * HEAD_SIZE
    n_own = plan_ref[4 * call + 2]
    n_sib = plan_ref[4 * call + 3]

    col = lax.broadcasted_iota(jnp.int32, (1, PREFIX_BLOCK_LEN), 1)
    biases = [
        jnp.where(col < n_own, 0.0, NEG).astype(F32),
        jnp.where(col < n_sib, 0.0, NEG).astype(F32),
    ]
    if has_fresh:
        tok = lax.broadcasted_iota(jnp.int32, (TOK, TOK), 0)
        new = lax.broadcasted_iota(jnp.int32, (TOK, TOK), 1)
        causal = jnp.where(new <= tok, 0.0, NEG).astype(F32)
        biases.append(jnp.concatenate([causal] * group, axis=0))
    lane = lax.rem(lax.broadcasted_iota(jnp.int32, (TOK, STAT), 1), heads)
    if has_carry:
        full_lane = lax.broadcasted_iota(jnp.int32, (TOK, STAT), 1)
        stat_in = jnp.where(full_lane < 3 * heads, carry_stat_ref[...].astype(F32), 0.0)
    stat = stat_ref[...]

    for u in range(unroll):
        q = jnp.concatenate(
            [
                q_ref[:, u * width + g * HEAD_SIZE : u * width + (g + 1) * HEAD_SIZE]
                for g in range(group)
            ],
            axis=0,
        )
        blocks = [own_ref[0, :, u * pair : (u + 1) * pair], sib_ref[0, :, u * pair : (u + 1) * pair]]
        if has_fresh:
            blocks.append(fresh_ref[:, u * pair : (u + 1) * pair])
        scores = [dot_nt(q, x[:, :HEAD_SIZE]) + bias for x, bias in zip(blocks, biases)]
        top = functools.reduce(
            jnp.maximum, [jnp.max(x, axis=1, keepdims=True) for x in scores]
        )
        probs = jnp.concatenate(
            [jnp.exp2((x - top) * SCALE2).astype(BF16) for x in scores], axis=1
        )
        values = jnp.concatenate([x[:, HEAD_SIZE:] for x in blocks], axis=0)
        values = jnp.concatenate([values, jnp.ones_like(values)], axis=1)
        mixed = jnp.dot(probs, values, preferred_element_type=F32)
        base = top * SCALE2
        for g in range(group):
            rows = slice(g * TOK, (g + 1) * TOK)
            head = (step * unroll + u) * group + g
            o_g, total, base_g = mixed[rows, :HEAD_SIZE], mixed[rows, HEAD_SIZE:], base[rows]
            if has_carry:
                lse_c = jnp.sum(jnp.where(lane == head, stat_in, 0.0), axis=1, keepdims=True)
                at = u * width + g * HEAD_SIZE
                o_c = carry_ref[:, at : at + HEAD_SIZE].astype(F32)
                high = jnp.maximum(base_g, lse_c)
                w_c = jnp.exp2(lse_c - high)
                w_g = jnp.exp2(base_g - high)
                total = w_c + total * w_g
                o_g = o_c * w_c + o_g * w_g
                base_g = high
            stat = jnp.where(lane == head, base_g + jnp.log2(total), stat)
            at = pl.multiple_of(step * unroll * width, width) + (u * width + g * HEAD_SIZE)
            at = pl.multiple_of(at, HEAD_SIZE)
            out_ref[:, pl.ds(at, HEAD_SIZE)] = (o_g / total).astype(BF16)
    stat_ref[...] = stat

    @pl.when(step == pl.num_programs(0) - 1)
    def _():
        full = lax.broadcasted_iota(jnp.int32, (TOK, STAT), 1)
        first = stat.astype(BF16).astype(F32)
        second = (stat - first).astype(BF16).astype(F32)
        third = stat - first - second
        split = jnp.where(full < heads, first, jnp.where(full < 2 * heads, second, third))
        out_ref[:, stat_at : stat_at + STAT] = split.astype(BF16)


def attend(call, plan, q, store, sib, kv_local, fresh=None, carry=None):
    heads = q.shape[1] // HEAD_SIZE
    group = heads // kv_local
    unroll = 2 if kv_local % 2 == 0 else 1
    width = unroll * group * HEAD_SIZE
    pair = unroll * 2 * HEAD_SIZE
    cols = heads * HEAD_SIZE + STAT
    span = 2 * PREFIX_BLOCK_LEN + (TOK if fresh is not None else 0)
    in_specs = [
        pl.BlockSpec((TOK, width), lambda h, plan: (0, h)),
        pl.BlockSpec((1, PREFIX_BLOCK_LEN, pair), lambda h, plan: (plan[4 * call], 0, h)),
        pl.BlockSpec((1, PREFIX_BLOCK_LEN, pair), lambda h, plan: (plan[4 * call + 1], 0, h)),
    ]
    args = [q, store, sib]
    if fresh is not None:
        in_specs.append(pl.BlockSpec((TOK, pair), lambda h, plan: (0, h)))
        args.append(fresh)
    if carry is not None:
        in_specs.append(pl.BlockSpec((TOK, width), lambda h, plan: (0, h)))
        in_specs.append(pl.BlockSpec((TOK, STAT), lambda h, plan: (0, heads)))
        args += [carry, carry]
    body = functools.partial(
        attend_kernel, call, group, heads, unroll, carry is not None, fresh is not None
    )
    return pl.pallas_call(
        body,
        out_shape=jax.ShapeDtypeStruct((TOK, cols), BF16),
        grid_spec=pltpu.PrefetchScalarGridSpec(
            num_scalar_prefetch=1,
            grid=(kv_local // unroll,),
            in_specs=in_specs,
            out_specs=pl.BlockSpec((TOK, cols), lambda h, plan: (0, 0)),
            scratch_shapes=[pltpu.VMEM((TOK, STAT), F32)],
        ),
        compiler_params=pltpu.CompilerParams(vmem_limit_bytes=40 * 1024 * 1024),
        cost_estimate=pl.CostEstimate(
            flops=8 * heads * TOK * span * HEAD_SIZE,
            bytes_accessed=4 * TOK * cols + 4 * kv_local * span * 2 * HEAD_SIZE,
            transcendentals=heads * TOK * span,
        ),
        name="attend",
    )(plan, *args)


def merge_parts(heads, part_refs, attn_ref):
    stat_at = heads * HEAD_SIZE
    lses = []
    for ref in part_refs:
        s = ref[:, stat_at : stat_at + STAT].astype(F32)
        lses.append(s[:, :heads] + s[:, heads : 2 * heads] + s[:, 2 * heads : 3 * heads])
    high = functools.reduce(jnp.maximum, lses)
    weights = [jnp.exp2(x - high) for x in lses]
    norm = 1.0 / functools.reduce(jnp.add, weights)
    weights = [w * norm for w in weights]
    for head in range(heads):
        cols = slice(head * HEAD_SIZE, (head + 1) * HEAD_SIZE)
        mixed = functools.reduce(
            jnp.add,
            [w[:, head : head + 1] * ref[:, cols].astype(F32) for w, ref in zip(weights, part_refs)],
        )
        attn_ref[:, cols] = mixed.astype(BF16)


def project_kernel(heads, nparts, nweight, nadd, *refs):
    part_refs = refs[:nparts]
    w_refs = refs[nparts : nparts + nweight]
    add_refs = refs[nparts + nweight : nparts + nweight + nadd]
    out_ref, attn_ref = refs[nparts + nweight + nadd :]

    @pl.when(pl.program_id(0) == 0)
    def _():
        merge_parts(heads, part_refs, attn_ref)

    depth = w_refs[0].shape[0]
    got = functools.reduce(
        jnp.add,
        [
            jnp.dot(
                attn_ref[:, i * depth : (i + 1) * depth], ref[...], preferred_element_type=F32
            )
            for i, ref in enumerate(w_refs)
        ],
    ).astype(BF16)
    if nadd:
        total = got.astype(F32)
        for ref in add_refs:
            total = total + ref[...].astype(F32)
        got = total.astype(BF16)
    out_ref[...] = got


def project(parts, weight, adds=()):
    depth, model = weight.shape
    heads = depth // HEAD_SIZE
    cols = parts[0].shape[1]
    tile = 1024
    streams = 4 if depth % (4 * HEAD_SIZE) == 0 else 1
    in_specs = [pl.BlockSpec((TOK, cols), lambda j: (0, 0)) for _ in parts]
    for i in range(streams):
        in_specs.append(pl.BlockSpec((depth // streams, tile), lambda j, i=i: (i, j)))
    in_specs += [pl.BlockSpec((TOK, tile), lambda j: (0, j)) for _ in adds]
    return pl.pallas_call(
        functools.partial(project_kernel, heads, len(parts), streams, len(adds)),
        out_shape=jax.ShapeDtypeStruct((TOK, model), BF16),
        grid=(model // tile,),
        in_specs=in_specs,
        out_specs=pl.BlockSpec((TOK, tile), lambda j: (0, j)),
        scratch_shapes=[pltpu.VMEM((TOK, depth), BF16)],
        compiler_params=pltpu.CompilerParams(vmem_limit_bytes=40 * 1024 * 1024),
        cost_estimate=pl.CostEstimate(
            flops=2 * TOK * depth * model,
            bytes_accessed=2 * depth * model + 4 * TOK * model,
            transcendentals=0,
        ),
        name="project",
    )(*parts, *([weight] * streams), *adds)


def shards(
    queries, new_key_values, key_value_store, o_weight, residual, hit_dev, hit_blk, prefix_len
):
    npool = lax.axis_size("pool")
    ntp = lax.axis_size("tp")
    me = lax.axis_index("pool")
    tp = lax.axis_index("tp")
    rdev = queries.shape[0] // TOK
    kv_local = key_value_store.shape[2] // (2 * HEAD_SIZE)
    nchips = npool // 2
    core = lax.rem(me, 2)
    chip = lax.div(me, 2)
    sibling = me + 1 - 2 * core
    ring = chip_ring(nchips)
    place = [ring.index(i) for i in range(nchips)]
    split_rows = ntp == rdev and rdev == 2

    swap_perm = [(p, p + 1 - 2 * (p % 2)) for p in range(npool)]
    cw_perm, ccw_perm = [], []
    for k in range(nchips):
        a, b = ring[k], ring[(k + 1) % nchips]
        for c in range(2):
            cw_perm.append((2 * a + c, 2 * b + c))
            ccw_perm.append((2 * b + c, 2 * a + c))

    starts = jnp.arange(MAXB, dtype=jnp.int32)[None, :] * PREFIX_BLOCK_LEN
    left = jnp.clip(prefix_len[:, None] - starts, 0, PREFIX_BLOCK_LEN)
    here, beside = hit_dev == me, hit_dev == sibling
    table = jnp.stack(
        [
            jnp.sum(jnp.where(at, x, 0), axis=1)
            for x, at in ((hit_blk, here), (hit_blk, beside), (left, here), (left, beside))
        ],
        axis=1,
    )
    half = nchips // 2
    steps = list(range(-half, half + 1))
    spot = jnp.asarray(place, jnp.int32)[chip]
    chips_at = jnp.asarray(ring, jnp.int32)[
        lax.rem(spot + nchips - jnp.asarray(steps, jnp.int32), nchips)
    ]
    slots = [1 - tp, tp] if split_rows else [jnp.int32(i) for i in range(rdev)]
    wanted = ((chips_at * 2 + core) * rdev)[None, :] + jnp.stack(slots)[:, None]
    plans = jnp.take(table, wanted.reshape(-1), axis=0, mode="clip").reshape(rdev, -1)
    sib = lax.ppermute(key_value_store, "pool", swap_perm)

    state = []
    for order, slot in enumerate(slots):
        plan = plans[order]
        q = lax.dynamic_slice_in_dim(queries, slot * TOK, TOK, 0)
        fresh = lax.dynamic_slice_in_dim(new_key_values, slot * TOK, TOK, 0)
        if nchips % 2:
            reach = (half, half)
        else:
            reach = (half, half - 1) if order % 2 == 0 else (half - 1, half)
        held = {}
        for sign, perm, hops in ((1, cw_perm, reach[0]), (-1, ccw_perm, reach[1])):
            moving = q
            for s in range(1, hops + 1):
                moving = lax.ppermute(moving, "pool", perm)
                held[sign * s] = moving
        state.append((plan, q, fresh, reach, held))

    parts_of = []
    for plan, q, fresh, reach, held in state:
        run = functools.partial(attend, store=key_value_store, sib=sib, kv_local=kv_local)
        call = lambda s: steps.index(s)
        own = run(call(0), plan, q, fresh=fresh)
        parts = [own]
        for sign, back, hops in ((1, ccw_perm, reach[0]), (-1, cw_perm, reach[1])):
            carry = None
            for s in range(hops, 0, -1):
                carry = run(call(sign * s), plan, held[sign * s], carry=carry)
                carry = lax.ppermute(carry, "pool", back)
            if carry is not None:
                parts.append(carry)
        parts_of.append(parts)

    if split_rows:
        away = project(parts_of[0], o_weight)
        got = lax.ppermute(away, "tp", [(0, 1), (1, 0)])
        return project(parts_of[1], o_weight, (got, residual))
    rows = jnp.concatenate([project(parts, o_weight) for parts in parts_of], axis=0)
    mine = lax.psum_scatter(rows, "tp", scatter_dimension=0, tiled=True)
    return (mine.astype(F32) + residual.astype(F32)).astype(BF16)


def solution(mesh):
    placed = (
        P("pool", "tp"),
        P("pool", "tp"),
        P("pool", None, "tp"),
        P("tp", None),
        P(("pool", "tp"), None),
        P(),
        P(),
        P(),
    )
    return jax.shard_map(
        shards, mesh=mesh, in_specs=placed, out_specs=P(("pool", "tp"), None), check_vma=False
    )
```

```python
import functools

import jax
import jax.numpy as jnp
from jax import lax
from jax.experimental import pallas as pl
from jax.experimental.pallas import tpu as pltpu
from jax.sharding import PartitionSpec as P

HEAD_SIZE = 128
NEW_TOKEN_COUNT = 128
PREFIX_BLOCK_LEN = 256
MAXB = 16
LOG2E = 1.4426950408889634
SCALE2 = HEAD_SIZE ** (-0.5) * LOG2E
NEG = -1e30
F32 = jnp.float32
BF16 = jnp.bfloat16
TOK = NEW_TOKEN_COUNT
VMEM_LIMIT = 60 * 1024 * 1024


def dot_nt(a, b):
    return lax.dot_general(a, b, (((1,), (1,)), ((), ())), preferred_element_type=F32)


def chip_ring(nchips):
    if nchips % 2:
        return list(range(nchips))
    up = list(range(0, nchips, 2))
    return up + [chip + 1 for chip in reversed(up)]


def stat_rows(heads):
    return -(-3 * heads // 16) * 16


def read_stat(ref, heads):
    s = ref[heads * HEAD_SIZE :, :].astype(F32)
    return s[:heads] + s[heads : 2 * heads] + s[2 * heads : 3 * heads]


def write_stat(ref, stat, heads):
    first = stat.astype(BF16).astype(F32)
    second = (stat - first).astype(BF16).astype(F32)
    third = stat - first - second
    terms = [first, second, third]
    extra = stat_rows(heads) - 3 * heads
    if extra:
        terms.append(jnp.zeros((extra, TOK), F32))
    ref[heads * HEAD_SIZE :, :] = jnp.concatenate(terms, axis=0).astype(BF16)


def attend_kernel(call, group, heads, nq, has_carry, has_fresh, plan_ref, *refs):
    refs = list(refs)
    q_refs, refs = refs[:nq], refs[nq:]
    own_ref, sib_ref = refs[:2]
    rest = refs[2:]
    fresh_ref = rest.pop(0) if has_fresh else None
    carry_ref = rest.pop(0) if has_carry else None
    (out_ref,) = rest
    kv = heads // group
    per_q = heads // nq
    pair = 2 * HEAD_SIZE
    rows = group * TOK

    def bias_of(count):
        at = lax.broadcasted_iota(jnp.int32, (PREFIX_BLOCK_LEN, rows), 0)
        return jnp.where(at < count, 0.0, NEG).astype(F32)

    biases = [bias_of(plan_ref[4 * call + 2]), bias_of(plan_ref[4 * call + 3])]
    if has_fresh:
        new = lax.broadcasted_iota(jnp.int32, (TOK, TOK), 0)
        tok = lax.broadcasted_iota(jnp.int32, (TOK, TOK), 1)
        causal = jnp.where(new <= tok, 0.0, NEG).astype(F32)
        biases.append(jnp.concatenate([causal] * group, axis=1))
    if has_carry:
        stat_in = read_stat(carry_ref, heads)
    stats = []
    for u in range(kv):
        queries = []
        for g in range(group):
            part, at = divmod(u * group + g, per_q)
            queries.append(q_refs[part][:, at * HEAD_SIZE : (at + 1) * HEAD_SIZE])
        q = jnp.concatenate(queries, axis=0)
        blocks = [ref[0, :, u * pair : (u + 1) * pair] for ref in (own_ref, sib_ref)]
        if has_fresh:
            blocks.append(fresh_ref[:, u * pair : (u + 1) * pair])
        scores = [dot_nt(x[:, :HEAD_SIZE], q) + bias for x, bias in zip(blocks, biases)]
        top = functools.reduce(
            jnp.maximum, [jnp.max(x, axis=0, keepdims=True) for x in scores]
        )
        probs = [jnp.exp2((x - top) * SCALE2) for x in scores]
        total = functools.reduce(jnp.add, [jnp.sum(x, axis=0, keepdims=True) for x in probs])
        probs = jnp.concatenate([x.astype(BF16) for x in probs], axis=0)
        values = jnp.concatenate([x[:, HEAD_SIZE:] for x in blocks], axis=0)
        mixed = lax.dot_general(
            values, probs, (((0,), (0,)), ((), ())), preferred_element_type=F32
        )
        base = top * SCALE2
        for g in range(group):
            head = u * group + g
            cols = slice(g * TOK, (g + 1) * TOK)
            at = slice(head * HEAD_SIZE, (head + 1) * HEAD_SIZE)
            o_g, sum_g, base_g = mixed[:, cols], total[:, cols], base[:, cols]
            if has_carry:
                lse_c = stat_in[head : head + 1]
                high = jnp.maximum(base_g, lse_c)
                w_c = jnp.exp2(lse_c - high)
                w_g = jnp.exp2(base_g - high)
                sum_g = w_c + sum_g * w_g
                norm = 1.0 / sum_g
                out = carry_ref[at, :].astype(F32) * (w_c * norm) + o_g * (w_g * norm)
                base_g = high
            else:
                out = o_g * (1.0 / sum_g)
            out_ref[at, :] = out.astype(BF16)
            stats.append(base_g + jnp.log2(sum_g))
    write_stat(out_ref, jnp.concatenate(stats, axis=0), heads)


def attend(call, plan, q_parts, store, sib, kv_local, fresh=None, carry=None):
    nq = len(q_parts)
    width = q_parts[0][2]
    heads = nq * width // HEAD_SIZE
    group = heads // kv_local
    cols = kv_local * 2 * HEAD_SIZE
    rows = heads * HEAD_SIZE + stat_rows(heads)
    span = 2 * PREFIX_BLOCK_LEN + (TOK if fresh is not None else 0)
    in_specs = [
        pl.BlockSpec((TOK, width), lambda i, plan, block=block: (0, block))
        for _, block, _ in q_parts
    ]
    in_specs += [
        pl.BlockSpec((1, PREFIX_BLOCK_LEN, cols), lambda i, plan: (plan[4 * call], 0, 0)),
        pl.BlockSpec((1, PREFIX_BLOCK_LEN, cols), lambda i, plan: (plan[4 * call + 1], 0, 0)),
    ]
    args = [array for array, _, _ in q_parts] + [store, sib]
    if fresh is not None:
        in_specs.append(pl.BlockSpec((TOK, cols), lambda i, plan: (0, 0)))
        args.append(fresh)
    if carry is not None:
        in_specs.append(pl.BlockSpec((rows, TOK), lambda i, plan: (0, 0)))
        args.append(carry)
    body = functools.partial(
        attend_kernel, call, group, heads, nq, carry is not None, fresh is not None
    )
    return pl.pallas_call(
        body,
        out_shape=jax.ShapeDtypeStruct((rows, TOK), BF16),
        grid_spec=pltpu.PrefetchScalarGridSpec(
            num_scalar_prefetch=1,
            grid=(1,),
            in_specs=in_specs,
            out_specs=pl.BlockSpec((rows, TOK), lambda i, plan: (0, 0)),
        ),
        compiler_params=pltpu.CompilerParams(vmem_limit_bytes=VMEM_LIMIT),
        cost_estimate=pl.CostEstimate(
            flops=8 * heads * TOK * span * HEAD_SIZE,
            bytes_accessed=4 * TOK * rows + 4 * kv_local * span * 2 * HEAD_SIZE,
            transcendentals=heads * TOK * span,
        ),
        name="attend",
    )(plan, *args)


def merged_heads(heads, part_refs, emit):
    lses = [read_stat(ref, heads) for ref in part_refs]
    high = functools.reduce(jnp.maximum, lses)
    weights = [jnp.exp2(x - high) for x in lses]
    total = functools.reduce(jnp.add, weights)
    norm = 1.0 / total
    weights = [w * norm for w in weights]
    for head in range(heads):
        at = slice(head * HEAD_SIZE, (head + 1) * HEAD_SIZE)
        emit(
            head,
            functools.reduce(
                jnp.add,
                [w[head : head + 1] * ref[at, :].astype(F32) for w, ref in zip(weights, part_refs)],
            ),
        )
    return high + jnp.log2(total)


def merge_kernel(heads, a_ref, b_ref, out_ref):
    def emit(head, value):
        out_ref[head * HEAD_SIZE : (head + 1) * HEAD_SIZE, :] = value.astype(BF16)

    write_stat(out_ref, merged_heads(heads, (a_ref, b_ref), emit), heads)


def merge(a, b, heads):
    spec = pl.BlockSpec(a.shape, lambda: (0, 0))
    return pl.pallas_call(
        functools.partial(merge_kernel, heads),
        out_shape=jax.ShapeDtypeStruct(a.shape, BF16),
        in_specs=[spec, spec],
        out_specs=spec,
        compiler_params=pltpu.CompilerParams(vmem_limit_bytes=VMEM_LIMIT),
        cost_estimate=pl.CostEstimate(flops=0, bytes_accessed=6 * a.size, transcendentals=0),
        name="merge",
    )(a, b)


def project_kernel(heads, nparts, nadd, streams, tile, *refs):
    part_refs = refs[:nparts]
    w_ref = refs[nparts]
    add_refs = refs[nparts + 1 : nparts + 1 + nadd]
    out_ref, attn_ref, parts_ref, w_buf, part_sem, w_sem = refs[nparts + 1 + nadd :]
    j = pl.program_id(0)
    count = pl.num_programs(0)
    ahead = w_buf.shape[0]
    depth = w_buf.shape[1] // streams

    def weight_copies(t):
        slot = lax.rem(t, ahead)
        cols = pl.ds(pl.multiple_of(t * tile, tile), tile)
        return [
            pltpu.make_async_copy(
                w_ref.at[pl.ds(i * depth, depth), cols],
                w_buf.at[slot, pl.ds(i * depth, depth)],
                w_sem.at[slot, i],
            )
            for i in range(streams)
        ]

    @pl.when(j == 0)
    def _():
        copies = [
            pltpu.make_async_copy(ref, parts_ref.at[i], part_sem.at[i])
            for i, ref in enumerate(part_refs)
        ]
        for copy in copies:
            copy.start()
        for t in range(ahead - 1):
            for copy in weight_copies(t):
                copy.start()
        for copy in copies:
            copy.wait()

        def emit(head, value):
            cols = slice(head * HEAD_SIZE, (head + 1) * HEAD_SIZE)
            attn_ref[:, cols] = value.T.astype(BF16)

        merged_heads(heads, [parts_ref.at[i] for i in range(nparts)], emit)

    @pl.when(j + ahead - 1 < count)
    def _():
        for copy in weight_copies(j + ahead - 1):
            copy.start()

    for copy in weight_copies(j):
        copy.wait()
    got = jnp.dot(
        attn_ref[...], w_buf[lax.rem(j, ahead)], preferred_element_type=F32
    ).astype(BF16)
    if nadd:
        total = got.astype(F32)
        for ref in add_refs:
            total = total + ref[...].astype(F32)
        got = total.astype(BF16)
    out_ref[...] = got


def project(parts, weight, adds=()):
    depth, model = weight.shape
    heads = depth // HEAD_SIZE
    tile = 1024
    ahead = min(3, model // tile)
    streams = 4
    in_specs = [pl.BlockSpec(memory_space=pl.ANY) for _ in parts]
    in_specs.append(pl.BlockSpec(memory_space=pl.ANY))
    in_specs += [pl.BlockSpec((TOK, tile), lambda j: (0, j)) for _ in adds]
    return pl.pallas_call(
        functools.partial(project_kernel, heads, len(parts), len(adds), streams, tile),
        out_shape=jax.ShapeDtypeStruct((TOK, model), BF16),
        grid=(model // tile,),
        in_specs=in_specs,
        out_specs=pl.BlockSpec((TOK, tile), lambda j: (0, j)),
        scratch_shapes=[
            pltpu.VMEM((TOK, depth), BF16),
            pltpu.VMEM((len(parts),) + parts[0].shape, BF16),
            pltpu.VMEM((ahead, depth, tile), BF16),
            pltpu.SemaphoreType.DMA((len(parts),)),
            pltpu.SemaphoreType.DMA((ahead, streams)),
        ],
        compiler_params=pltpu.CompilerParams(vmem_limit_bytes=VMEM_LIMIT),
        cost_estimate=pl.CostEstimate(
            flops=2 * TOK * depth * model,
            bytes_accessed=2 * depth * model + 4 * TOK * model,
            transcendentals=0,
        ),
        name="project",
    )(*parts, weight, *adds)


def shards(
    queries, new_key_values, key_value_store, o_weight, residual, hit_dev, hit_blk, prefix_len
):
    npool = lax.axis_size("pool")
    ntp = lax.axis_size("tp")
    me = lax.axis_index("pool")
    tp = lax.axis_index("tp")
    rdev = queries.shape[0] // TOK
    kv_local = key_value_store.shape[2] // (2 * HEAD_SIZE)
    nchips = npool // 2
    core = lax.rem(me, 2)
    chip = lax.div(me, 2)
    sibling = me + 1 - 2 * core
    ring = chip_ring(nchips)
    place = [ring.index(i) for i in range(nchips)]
    split_rows = ntp == rdev and rdev == 2

    swap_perm = [(p, p + 1 - 2 * (p % 2)) for p in range(npool)]
    cw_perm, ccw_perm = [], []
    for k in range(nchips):
        a, b = ring[k], ring[(k + 1) % nchips]
        for c in range(2):
            cw_perm.append((2 * a + c, 2 * b + c))
            ccw_perm.append((2 * b + c, 2 * a + c))

    starts = jnp.arange(MAXB, dtype=jnp.int32)[None, :] * PREFIX_BLOCK_LEN
    left = jnp.clip(prefix_len[:, None] - starts, 0, PREFIX_BLOCK_LEN)
    here, beside = hit_dev == me, hit_dev == sibling
    table = jnp.stack(
        [
            jnp.sum(jnp.where(at, x, 0), axis=1)
            for x, at in ((hit_blk, here), (hit_blk, beside), (left, here), (left, beside))
        ],
        axis=1,
    )
    half = nchips // 2
    steps = list(range(-half, half + 1))
    spot = jnp.asarray(place, jnp.int32)[chip]
    chips_at = jnp.asarray(ring, jnp.int32)[
        lax.rem(spot + nchips - jnp.asarray(steps, jnp.int32), nchips)
    ]
    slots = [1 - tp, tp] if split_rows else [jnp.int32(i) for i in range(rdev)]
    wanted = ((chips_at * 2 + core) * rdev)[None, :] + jnp.stack(slots)[:, None]
    plans = jnp.take(table, wanted.reshape(-1), axis=0, mode="clip").reshape(rdev, -1)
    sib = lax.ppermute(key_value_store, "pool", swap_perm)

    heads = queries.shape[1] // HEAD_SIZE
    nq = 2 if kv_local % 2 == 0 else 1
    width = heads // nq * HEAD_SIZE

    def travel(x, hops_cw, hops_ccw, held, key):
        for sign, perm, hops in ((1, cw_perm, hops_cw), (-1, ccw_perm, hops_ccw)):
            moving = x
            for t in range(1, hops + 1):
                moving = lax.ppermute(moving, "pool", perm)
                held[sign * t, key] = moving

    def after(x, *others):
        return lax.optimization_barrier((x,) + others)[0]

    def reach(flip):
        if nchips % 2:
            return half, half
        return (half - 1, half) if flip else (half, half - 1)

    q_of, fresh_of = [], []
    for order, slot in enumerate(slots):
        held = {}
        fresh_of.append(lax.dynamic_slice_in_dim(new_key_values, slot * TOK, TOK, 0))
        if order == 0:
            for part in range(nq):
                q = lax.dynamic_slice(queries, (slot * TOK, part * width), (TOK, width))
                held[0, part] = q
                travel(q, *reach(part % 2), held, part)
            opposite = {}
            for part in range(nq):
                for t in (half, -half):
                    if (t, part) in held:
                        opposite[part] = held[t, part]
            for part in range(nq):
                for t in (half, -half):
                    held.setdefault((t, part), opposite.get(part))
            q_of.append(
                {t: [(held[t, part], 0, width) for part in range(nq)] for t in steps}
            )
        else:
            q = lax.dynamic_slice_in_dim(queries, slot * TOK, TOK, 0)
            held[0, 0] = q
            travel(q, *reach(order % 2), held, 0)
            q_of.append(
                {t: [(x, part, width) for part in range(nq)] for (t, _), x in held.items()}
            )

    last = [None]

    def run(order, t, **more):
        plan = plans[order]
        if last[0] is not None:
            plan = after(plan, last[0])
        last[0] = attend(
            steps.index(t), plan, q_of[order][t], key_value_store, sib, kv_local, **more
        )
        return last[0]

    parts_of = [[run(order, 0, fresh=fresh_of[order])] for order in range(rdev)]
    carry = {1: None, -1: None}
    hops = dict(zip((1, -1), reach(0)))
    back = {1: ccw_perm, -1: cw_perm}
    early = {}
    for i in range(half):
        for sign in (1, -1):
            t = hops[sign] - i
            if t > 0:
                x = run(0, sign * t, carry=carry[sign])
                carry[sign] = lax.ppermute(x, "pool", back[sign])
        for order in range(1, rdev):
            for t in (i + 1, -i - 1):
                if t in q_of[order]:
                    early[order, t] = run(order, t)
    parts_of[0] += [x for x in carry.values() if x is not None]
    for order in range(1, rdev):
        for sign, count in zip((1, -1), reach(order % 2)):
            moving = None
            for t in range(count, 0, -1):
                x = early[order, sign * t]
                x = x if moving is None else merge(x, moving, heads)
                moving = lax.ppermute(x, "pool", back[sign])
            if moving is not None:
                parts_of[order].append(moving)

    if split_rows:
        away = project(parts_of[0], o_weight)
        got = lax.ppermute(away, "tp", [(0, 1), (1, 0)])
        return project(parts_of[1], o_weight, (got, residual))
    rows = jnp.concatenate([project(parts, o_weight) for parts in parts_of], axis=0)
    mine = lax.psum_scatter(rows, "tp", scatter_dimension=0, tiled=True)
    return (mine.astype(F32) + residual.astype(F32)).astype(BF16)


def solution(mesh):
    placed = (
        P("pool", "tp"),
        P("pool", "tp"),
        P("pool", None, "tp"),
        P("tp", None),
        P(("pool", "tp"), None),
        P(),
        P(),
        P(),
    )
    return jax.shard_map(
        shards, mesh=mesh, in_specs=placed, out_specs=P(("pool", "tp"), None), check_vma=False
    )
```

```python
import functools

import jax
import jax.numpy as jnp
from jax import lax
from jax.experimental import pallas as pl
from jax.experimental.pallas import tpu as pltpu
from jax.sharding import PartitionSpec as P

HEAD_SIZE = 128
NEW_TOKEN_COUNT = 128
PREFIX_BLOCK_LEN = 256
MAXB = 16
LOG2E = 1.4426950408889634
SCALE2 = HEAD_SIZE ** (-0.5) * LOG2E
NEG = -1e30
F32 = jnp.float32
BF16 = jnp.bfloat16
TOK = NEW_TOKEN_COUNT
VMEM_LIMIT = 64 * 1024 * 1024
CHUNK = 64


def dot_nt(a, b):
    return lax.dot_general(a, b, (((1,), (1,)), ((), ())), preferred_element_type=F32)


def chip_ring(nchips):
    if nchips % 2:
        return list(range(nchips))
    up = list(range(0, nchips, 2))
    return up + [chip + 1 for chip in reversed(up)]


def stat_rows(heads):
    return -(-3 * heads // 16) * 16


def read_stat(ref, heads):
    s = ref[heads * HEAD_SIZE :, :].astype(F32)
    return s[:heads] + s[heads : 2 * heads] + s[2 * heads : 3 * heads]


def write_stat(ref, stat, heads):
    first = stat.astype(BF16).astype(F32)
    second = (stat - first).astype(BF16).astype(F32)
    third = stat - first - second
    terms = [first, second, third]
    extra = stat_rows(heads) - 3 * heads
    if extra:
        terms.append(jnp.zeros((extra, TOK), F32))
    ref[heads * HEAD_SIZE :, :] = jnp.concatenate(terms, axis=0).astype(BF16)


def attend_kernel(calls, group, heads, nq, has_carry, has_fresh, plan_ref, *refs):
    refs = list(refs)
    count = len(calls)
    kv = heads // group
    per_q = kv // nq
    pair = 2 * HEAD_SIZE
    width = group * HEAD_SIZE
    cols = group * TOK
    stat_at = heads * HEAD_SIZE
    span = 2 * PREFIX_BLOCK_LEN + (TOK if has_fresh else 0)

    store_ref, sib_ref = refs.pop(0), refs.pop(0)
    q_refs = [[refs.pop(0) for _ in range(nq)] for _ in range(count)]
    fresh_refs = [refs.pop(0) for _ in range(count)] if has_fresh else None
    carry_refs = [refs.pop(0) for _ in range(count)] if has_carry else None
    out_refs = [refs.pop(0) for _ in range(count)]
    q_buf, kv_buf, carry_buf, out_buf, bias_buf, s_buf, p_buf, in_sem, carry_sem, out_sem = refs

    def copies_in(r, u):
        at = slice(u * pair, (u + 1) * pair)
        part, inner = divmod(u, per_q)
        block, other = plan_ref[4 * calls[r]], plan_ref[4 * calls[r] + 1]
        moves = [
            (q_refs[r][part].at[:, inner * width : (inner + 1) * width], q_buf.at[r, u]),
            (store_ref.at[block, :, at], kv_buf.at[r, u, 0:PREFIX_BLOCK_LEN]),
            (sib_ref.at[other, :, at], kv_buf.at[r, u, PREFIX_BLOCK_LEN : 2 * PREFIX_BLOCK_LEN]),
        ]
        if has_fresh:
            moves.append((fresh_refs[r].at[:, at], kv_buf.at[r, u, 2 * PREFIX_BLOCK_LEN : span]))
        return [
            pltpu.make_async_copy(a, b, in_sem.at[r, u, i]) for i, (a, b) in enumerate(moves)
        ]

    def copy_carry(r):
        return pltpu.make_async_copy(carry_refs[r], carry_buf.at[r], carry_sem.at[r])

    def copy_out(r, u):
        at = slice(u * width, (u + 1) * width) if u < kv else slice(stat_at, out_buf.shape[1])
        return pltpu.make_async_copy(out_buf.at[r, at], out_refs[r].at[at], out_sem.at[r, u])

    for r in range(count):
        for u in range(kv):
            for copy in copies_in(r, u):
                copy.start()
            if u == 0 and has_carry:
                copy_carry(r).start()

    for r in range(count):
        at = lax.broadcasted_iota(jnp.int32, (PREFIX_BLOCK_LEN, TOK), 0)
        for i in range(2):
            valid = at < plan_ref[4 * calls[r] + 2 + i]
            bias_buf[r, i * PREFIX_BLOCK_LEN : (i + 1) * PREFIX_BLOCK_LEN] = jnp.where(
                valid, 0.0, NEG
            ).astype(F32)
        if has_fresh:
            new = lax.broadcasted_iota(jnp.int32, (TOK, TOK), 0)
            tok = lax.broadcasted_iota(jnp.int32, (TOK, TOK), 1)
            bias_buf[r, 2 * PREFIX_BLOCK_LEN : span] = jnp.where(new <= tok, 0.0, NEG).astype(F32)

    jobs = [(r, u) for r in range(count) for u in range(kv)]
    slots = s_buf.shape[0]
    stats = [[] for _ in range(count)]

    def score(n):
        r, u = jobs[n]
        for copy in copies_in(r, u):
            copy.wait()
        q = jnp.concatenate(
            [q_buf[r, u, :, g * HEAD_SIZE : (g + 1) * HEAD_SIZE] for g in range(group)], axis=0
        )
        for at in range(0, span, PREFIX_BLOCK_LEN):
            rows = slice(at, min(at + PREFIX_BLOCK_LEN, span))
            s_buf[n % slots, rows] = dot_nt(kv_buf[r, u, rows, :HEAD_SIZE], q)

    def soften(n):
        r, u = jobs[n]
        slot = n % slots

        def piece(at):
            bias = bias_buf[r, at : at + CHUNK]
            return s_buf[slot, at : at + CHUNK] + jnp.concatenate([bias] * group, axis=1)

        top = None
        for at in range(0, span, CHUNK):
            high = jnp.max(piece(at).reshape(CHUNK // 8, 8, cols), axis=0)
            top = high if top is None else jnp.maximum(top, high)
        top = jnp.max(top, axis=0, keepdims=True)
        total = None
        for at in range(0, span, CHUNK):
            ex = jnp.exp2((piece(at) - top) * SCALE2)
            p_buf[slot, at : at + CHUNK] = ex.astype(BF16)
            part = jnp.sum(ex.reshape(CHUNK // 8, 8, cols), axis=0)
            total = part if total is None else total + part
        return top * SCALE2, jnp.sum(total, axis=0, keepdims=True)

    def mix(n, base, total):
        r, u = jobs[n]
        mixed = lax.dot_general(
            kv_buf[r, u, :, HEAD_SIZE:],
            p_buf[n % slots],
            (((0,), (0,)), ((), ())),
            preferred_element_type=F32,
        )
        if has_carry and u == 0:
            copy_carry(r).wait()
        if has_carry:
            stat_in = read_stat(carry_buf.at[r], heads)
        for g in range(group):
            head = u * group + g
            at = slice(head * HEAD_SIZE, (head + 1) * HEAD_SIZE)
            part = slice(g * TOK, (g + 1) * TOK)
            o_g, sum_g, base_g = mixed[:, part], total[:, part], base[:, part]
            if has_carry:
                lse_c = stat_in[head : head + 1]
                high = jnp.maximum(base_g, lse_c)
                w_c = jnp.exp2(lse_c - high)
                w_g = jnp.exp2(base_g - high)
                sum_g = w_c + sum_g * w_g
                norm = 1.0 / sum_g
                out = carry_buf[r, at].astype(F32) * (w_c * norm) + o_g * (w_g * norm)
                base_g = high
            else:
                out = o_g * (1.0 / sum_g)
            out_buf[r, at] = out.astype(BF16)
            stats[r].append(base_g + jnp.log2(sum_g))
        copy_out(r, u).start()
        if u == kv - 1:
            write_stat(out_buf.at[r], jnp.concatenate(stats[r], axis=0), heads)
            copy_out(r, kv).start()

    score(0)
    for n in range(len(jobs)):
        if n + 1 < len(jobs):
            score(n + 1)
        mix(n, *soften(n))
    for r in range(count):
        for u in range(kv + 1):
            copy_out(r, u).wait()


def attend(calls, plan, q_parts, store, sib, kv_local, fresh=None, carry=None):
    count = len(calls)
    nq = len(q_parts[0])
    width = q_parts[0][0].shape[1]
    heads = nq * width // HEAD_SIZE
    group = heads // kv_local
    rows = heads * HEAD_SIZE + stat_rows(heads)
    span = 2 * PREFIX_BLOCK_LEN + (TOK if fresh is not None else 0)
    args = [store, sib] + [x for parts in q_parts for x in parts]
    args += list(fresh or ()) + list(carry or ())
    body = functools.partial(
        attend_kernel, calls, group, heads, nq, carry is not None, fresh is not None
    )
    any_spec = pl.BlockSpec(memory_space=pl.ANY)
    slots = 3
    out = pl.pallas_call(
        body,
        out_shape=[jax.ShapeDtypeStruct((rows, TOK), BF16)] * count,
        in_specs=[pl.BlockSpec(memory_space=pltpu.SMEM)] + [any_spec] * len(args),
        out_specs=[any_spec] * count,
        scratch_shapes=[
            pltpu.VMEM((count, kv_local, TOK, group * HEAD_SIZE), BF16),
            pltpu.VMEM((count, kv_local, span, 2 * HEAD_SIZE), BF16),
            pltpu.VMEM((count, rows, TOK), BF16),
            pltpu.VMEM((count, rows, TOK), BF16),
            pltpu.VMEM((count, span, TOK), F32),
            pltpu.VMEM((slots, span, group * TOK), F32),
            pltpu.VMEM((slots, span, group * TOK), BF16),
            pltpu.SemaphoreType.DMA((count, kv_local, 4)),
            pltpu.SemaphoreType.DMA((count,)),
            pltpu.SemaphoreType.DMA((count, kv_local + 1)),
        ],
        compiler_params=pltpu.CompilerParams(vmem_limit_bytes=VMEM_LIMIT),
        cost_estimate=pl.CostEstimate(
            flops=8 * heads * TOK * span * HEAD_SIZE * count,
            bytes_accessed=(4 * TOK * rows + 4 * kv_local * span * 2 * HEAD_SIZE) * count,
            transcendentals=heads * TOK * span * count,
        ),
        name="attend",
    )(plan, *args)
    return list(out)


def merged_heads(heads, part_refs, emit):
    lses = [read_stat(ref, heads) for ref in part_refs]
    high = functools.reduce(jnp.maximum, lses)
    weights = [jnp.exp2(x - high) for x in lses]
    total = functools.reduce(jnp.add, weights)
    norm = 1.0 / total
    weights = [w * norm for w in weights]
    for head in range(heads):
        at = slice(head * HEAD_SIZE, (head + 1) * HEAD_SIZE)
        emit(
            head,
            functools.reduce(
                jnp.add,
                [w[head : head + 1] * ref[at, :].astype(F32) for w, ref in zip(weights, part_refs)],
            ),
        )
    return high + jnp.log2(total)


def merge_kernel(heads, a_ref, b_ref, out_ref):
    def emit(head, value):
        out_ref[head * HEAD_SIZE : (head + 1) * HEAD_SIZE, :] = value.astype(BF16)

    write_stat(out_ref, merged_heads(heads, (a_ref, b_ref), emit), heads)


def merge(a, b, heads):
    spec = pl.BlockSpec(a.shape, lambda: (0, 0))
    return pl.pallas_call(
        functools.partial(merge_kernel, heads),
        out_shape=jax.ShapeDtypeStruct(a.shape, BF16),
        in_specs=[spec, spec],
        out_specs=spec,
        compiler_params=pltpu.CompilerParams(vmem_limit_bytes=VMEM_LIMIT),
        cost_estimate=pl.CostEstimate(flops=0, bytes_accessed=6 * a.size, transcendentals=0),
        name="merge",
    )(a, b)


def project_kernel(heads, nparts, nadd, streams, tile, *refs):
    part_refs = refs[:nparts]
    w_ref = refs[nparts]
    add_refs = refs[nparts + 1 : nparts + 1 + nadd]
    out_ref, attn_ref, parts_ref, w_buf, part_sem, w_sem = refs[nparts + 1 + nadd :]
    j = pl.program_id(0)
    count = pl.num_programs(0)
    ahead = w_buf.shape[0]
    depth = w_buf.shape[1] // streams

    def weight_copies(t):
        slot = lax.rem(t, ahead)
        cols = pl.ds(pl.multiple_of(t * tile, tile), tile)
        return [
            pltpu.make_async_copy(
                w_ref.at[pl.ds(i * depth, depth), cols],
                w_buf.at[slot, pl.ds(i * depth, depth)],
                w_sem.at[slot, i],
            )
            for i in range(streams)
        ]

    @pl.when(j == 0)
    def _():
        copies = [
            pltpu.make_async_copy(ref, parts_ref.at[i], part_sem.at[i])
            for i, ref in enumerate(part_refs)
        ]
        for copy in copies:
            copy.start()
        for t in range(ahead - 1):
            for copy in weight_copies(t):
                copy.start()
        for copy in copies:
            copy.wait()

        def emit(head, value):
            cols = slice(head * HEAD_SIZE, (head + 1) * HEAD_SIZE)
            attn_ref[:, cols] = value.T.astype(BF16)

        merged_heads(heads, [parts_ref.at[i] for i in range(nparts)], emit)

    @pl.when(j + ahead - 1 < count)
    def _():
        for copy in weight_copies(j + ahead - 1):
            copy.start()

    for copy in weight_copies(j):
        copy.wait()
    got = jnp.dot(
        attn_ref[...], w_buf[lax.rem(j, ahead)], preferred_element_type=F32
    ).astype(BF16)
    if nadd:
        total = got.astype(F32)
        for ref in add_refs:
            total = total + ref[...].astype(F32)
        got = total.astype(BF16)
    out_ref[...] = got


def project(parts, weight, adds=()):
    depth, model = weight.shape
    heads = depth // HEAD_SIZE
    tile = 1024
    ahead = min(3, model // tile)
    streams = 4
    in_specs = [pl.BlockSpec(memory_space=pl.ANY) for _ in parts]
    in_specs.append(pl.BlockSpec(memory_space=pl.ANY))
    in_specs += [pl.BlockSpec((TOK, tile), lambda j: (0, j)) for _ in adds]
    return pl.pallas_call(
        functools.partial(project_kernel, heads, len(parts), len(adds), streams, tile),
        out_shape=jax.ShapeDtypeStruct((TOK, model), BF16),
        grid=(model // tile,),
        in_specs=in_specs,
        out_specs=pl.BlockSpec((TOK, tile), lambda j: (0, j)),
        scratch_shapes=[
            pltpu.VMEM((TOK, depth), BF16),
            pltpu.VMEM((len(parts),) + parts[0].shape, BF16),
            pltpu.VMEM((ahead, depth, tile), BF16),
            pltpu.SemaphoreType.DMA((len(parts),)),
            pltpu.SemaphoreType.DMA((ahead, streams)),
        ],
        compiler_params=pltpu.CompilerParams(vmem_limit_bytes=VMEM_LIMIT),
        cost_estimate=pl.CostEstimate(
            flops=2 * TOK * depth * model,
            bytes_accessed=2 * depth * model + 4 * TOK * model,
            transcendentals=0,
        ),
        name="project",
    )(*parts, weight, *adds)


def shards(
    queries, new_key_values, key_value_store, o_weight, residual, hit_dev, hit_blk, prefix_len
):
    npool = lax.axis_size("pool")
    ntp = lax.axis_size("tp")
    me = lax.axis_index("pool")
    tp = lax.axis_index("tp")
    rdev = queries.shape[0] // TOK
    kv_local = key_value_store.shape[2] // (2 * HEAD_SIZE)
    nchips = npool // 2
    core = lax.rem(me, 2)
    chip = lax.div(me, 2)
    sibling = me + 1 - 2 * core
    ring = chip_ring(nchips)
    place = [ring.index(i) for i in range(nchips)]
    split_rows = ntp == rdev and rdev == 2

    swap_perm = [(p, p + 1 - 2 * (p % 2)) for p in range(npool)]
    cw_perm, ccw_perm = [], []
    for k in range(nchips):
        a, b = ring[k], ring[(k + 1) % nchips]
        for c in range(2):
            cw_perm.append((2 * a + c, 2 * b + c))
            ccw_perm.append((2 * b + c, 2 * a + c))

    starts = jnp.arange(MAXB, dtype=jnp.int32)[None, :] * PREFIX_BLOCK_LEN
    left = jnp.clip(prefix_len[:, None] - starts, 0, PREFIX_BLOCK_LEN)
    here, beside = hit_dev == me, hit_dev == sibling
    table = jnp.stack(
        [
            jnp.sum(jnp.where(at, x, 0), axis=1)
            for x, at in ((hit_blk, here), (hit_blk, beside), (left, here), (left, beside))
        ],
        axis=1,
    )
    half = nchips // 2
    steps = list(range(-half, half + 1))
    spot = jnp.asarray(place, jnp.int32)[chip]
    chips_at = jnp.asarray(ring, jnp.int32)[
        lax.rem(spot + nchips - jnp.asarray(steps, jnp.int32), nchips)
    ]
    slots = [1 - tp, tp] if split_rows else [jnp.int32(i) for i in range(rdev)]
    wanted = ((chips_at * 2 + core) * rdev)[None, :] + jnp.stack(slots)[:, None]
    plan = jnp.take(table, wanted.reshape(-1), axis=0, mode="clip").reshape(-1)
    sib = lax.ppermute(key_value_store, "pool", swap_perm)

    heads = queries.shape[1] // HEAD_SIZE
    nq = 2 if kv_local % 2 == 0 else 1
    width = heads // nq * HEAD_SIZE

    def travel(x, hops_cw, hops_ccw, held, key):
        for sign, perm, hops in ((1, cw_perm, hops_cw), (-1, ccw_perm, hops_ccw)):
            moving = x
            for t in range(1, hops + 1):
                moving = lax.ppermute(moving, "pool", perm)
                held[sign * t, key] = moving

    def after(x, *others):
        return lax.optimization_barrier((x,) + others)[0]

    def reach(flip):
        if nchips % 2:
            return half, half
        return (half - 1, half) if flip else (half, half - 1)

    q_of, fresh_of = [], []
    for order, slot in enumerate(slots):
        held = {}
        fresh_of.append(lax.dynamic_slice_in_dim(new_key_values, slot * TOK, TOK, 0))
        if order == 0:
            for part in range(nq):
                q = lax.dynamic_slice(queries, (slot * TOK, part * width), (TOK, width))
                held[0, part] = q
                travel(q, *reach(part % 2), held, part)
            opposite = {}
            for part in range(nq):
                for t in (half, -half):
                    if (t, part) in held:
                        opposite[part] = held[t, part]
            for part in range(nq):
                for t in (half, -half):
                    held.setdefault((t, part), opposite.get(part))
            q_of.append({t: [held[t, part] for part in range(nq)] for t in steps})
        else:
            q = lax.dynamic_slice_in_dim(queries, slot * TOK, TOK, 0)
            held[0, 0] = q
            travel(q, *reach(order % 2), held, 0)
            q_of.append({t: [x] for (t, _), x in held.items()})
            q_of[order][0] = [q[:, part * width : (part + 1) * width] for part in range(nq)]

    last = [None]

    def run(wanted, **more):
        calls = [order * len(steps) + steps.index(t) for order, t in wanted]
        table = plan if last[0] is None else after(plan, last[0])
        out = attend(
            calls, table, [q_of[order][t] for order, t in wanted], key_value_store, sib, kv_local,
            **more,
        )
        last[0] = out[0]
        return out

    own = run([(order, 0) for order in range(rdev)], fresh=fresh_of)
    parts_of = [[x] for x in own]
    carry = {1: None, -1: None}
    hops = dict(zip((1, -1), reach(0)))
    back = {1: ccw_perm, -1: cw_perm}
    early = {}
    for i in range(half):
        for sign in (1, -1):
            t = hops[sign] - i
            if t > 0:
                more = {} if carry[sign] is None else {"carry": [carry[sign]]}
                (x,) = run([(0, sign * t)], **more)
                carry[sign] = lax.ppermute(x, "pool", back[sign])
        wanted = [
            (order, t) for order in range(1, rdev) for t in (i + 1, -i - 1) if t in q_of[order]
        ]
        if wanted:
            early.update(zip(wanted, run(wanted)))
    parts_of[0] += [x for x in carry.values() if x is not None]
    for order in range(1, rdev):
        for sign, count in zip((1, -1), reach(order % 2)):
            moving = None
            for t in range(count, 0, -1):
                x = early[order, sign * t]
                x = x if moving is None else merge(x, moving, heads)
                moving = lax.ppermute(x, "pool", back[sign])
            if moving is not None:
                parts_of[order].append(moving)

    if split_rows:
        away = project(parts_of[0], o_weight)
        got = lax.ppermute(away, "tp", [(0, 1), (1, 0)])
        return project(parts_of[1], o_weight, (got, residual))
    rows = jnp.concatenate([project(parts, o_weight) for parts in parts_of], axis=0)
    mine = lax.psum_scatter(rows, "tp", scatter_dimension=0, tiled=True)
    return (mine.astype(F32) + residual.astype(F32)).astype(BF16)


def solution(mesh):
    placed = (
        P("pool", "tp"),
        P("pool", "tp"),
        P("pool", None, "tp"),
        P("tp", None),
        P(("pool", "tp"), None),
        P(),
        P(),
        P(),
    )
    return jax.shard_map(
        shards, mesh=mesh, in_specs=placed, out_specs=P(("pool", "tp"), None), check_vma=False
    )
```

```python
import functools

import jax
import jax.numpy as jnp
from jax import lax
from jax.experimental import pallas as pl
from jax.experimental.pallas import tpu as pltpu
from jax.sharding import PartitionSpec as P

HEAD_SIZE = 128
NEW_TOKEN_COUNT = 128
PREFIX_BLOCK_LEN = 256
MAXB = 16
LOG2E = 1.4426950408889634
SCALE2 = HEAD_SIZE ** (-0.5) * LOG2E
NEG = -1e30
F32 = jnp.float32
BF16 = jnp.bfloat16
TOK = NEW_TOKEN_COUNT
VMEM_LIMIT = 64 * 1024 * 1024
CHUNK = 64


def dot_nt(a, b):
    return lax.dot_general(a, b, (((1,), (1,)), ((), ())), preferred_element_type=F32)


def chip_ring(nchips):
    if nchips % 2:
        return list(range(nchips))
    up = list(range(0, nchips, 2))
    return up + [chip + 1 for chip in reversed(up)]


def stat_rows(heads):
    return -(-3 * heads // 16) * 16


def part_rows(heads):
    return heads * HEAD_SIZE + stat_rows(heads)


def read_stat(ref, heads):
    s = ref[heads * HEAD_SIZE :, :].astype(F32)
    return s[:heads] + s[heads : 2 * heads] + s[2 * heads : 3 * heads]


def write_stat(ref, stat, heads):
    first = stat.astype(BF16).astype(F32)
    second = (stat - first).astype(BF16).astype(F32)
    third = stat - first - second
    terms = [first, second, third]
    extra = stat_rows(heads) - 3 * heads
    if extra:
        terms.append(jnp.zeros((extra, TOK), F32))
    ref[heads * HEAD_SIZE :, :] = jnp.concatenate(terms, axis=0).astype(BF16)


def attend_kernel(calls, nouts, group, heads, nq, has_carry, has_fresh, plan_ref, *refs):
    refs = list(refs)
    count = len(calls)
    kv = heads // group
    per_q = kv // nq
    pair = 2 * HEAD_SIZE
    width = group * HEAD_SIZE
    cols = group * TOK
    span = 2 * PREFIX_BLOCK_LEN + (TOK if has_fresh else 0)

    store_ref, sib_ref = refs.pop(0), refs.pop(0)
    q_refs = [[refs.pop(0) for _ in range(nq)] for _ in range(count)]
    fresh_refs = [refs.pop(0) for _ in range(count)] if has_fresh else None
    carry_refs = [refs.pop(0) for _ in range(count)] if has_carry else None
    out_refs = [[refs.pop(0) for _ in range(n)] for n in nouts]
    q_buf, kv_buf, carry_buf, out_buf, bias_buf, s_buf, p_buf, in_sem, carry_sem, out_sem = refs

    def copies_in(r, u):
        at = slice(u * pair, (u + 1) * pair)
        part, inner = divmod(u, per_q)
        block, other = plan_ref[4 * calls[r]], plan_ref[4 * calls[r] + 1]
        moves = [
            (q_refs[r][part].at[:, inner * width : (inner + 1) * width], q_buf.at[r, u]),
            (store_ref.at[block, :, at], kv_buf.at[r, u, 0:PREFIX_BLOCK_LEN]),
            (sib_ref.at[other, :, at], kv_buf.at[r, u, PREFIX_BLOCK_LEN : 2 * PREFIX_BLOCK_LEN]),
        ]
        if has_fresh:
            moves.append((fresh_refs[r].at[:, at], kv_buf.at[r, u, 2 * PREFIX_BLOCK_LEN : span]))
        return [
            pltpu.make_async_copy(a, b, in_sem.at[r, u, i]) for i, (a, b) in enumerate(moves)
        ]

    def copy_carry(r):
        return pltpu.make_async_copy(carry_refs[r], carry_buf.at[r], carry_sem.at[r])

    def spot(r, head):
        share = heads // nouts[r]
        return head // share, head % share * HEAD_SIZE, head // share * part_rows(share)

    def copy_out(r, u):
        if u < kv:
            part, inner, base = spot(r, u * group)
            n = group * HEAD_SIZE
        else:
            part, share = u - kv, heads // nouts[r]
            inner, base, n = share * HEAD_SIZE, part * part_rows(share), stat_rows(share)
        return pltpu.make_async_copy(
            out_buf.at[r, base + inner : base + inner + n],
            out_refs[r][part].at[inner : inner + n],
            out_sem.at[r, u],
        )

    for r in range(count):
        for u in range(kv):
            for copy in copies_in(r, u):
                copy.start()
            if u == 0 and has_carry:
                copy_carry(r).start()

    for r in range(count):
        at = lax.broadcasted_iota(jnp.int32, (PREFIX_BLOCK_LEN, TOK), 0)
        for i in range(2):
            valid = at < plan_ref[4 * calls[r] + 2 + i]
            bias_buf[r, i * PREFIX_BLOCK_LEN : (i + 1) * PREFIX_BLOCK_LEN] = jnp.where(
                valid, 0.0, NEG
            ).astype(F32)
        if has_fresh:
            new = lax.broadcasted_iota(jnp.int32, (TOK, TOK), 0)
            tok = lax.broadcasted_iota(jnp.int32, (TOK, TOK), 1)
            bias_buf[r, 2 * PREFIX_BLOCK_LEN : span] = jnp.where(new <= tok, 0.0, NEG).astype(F32)

    jobs = [(r, u) for r in range(count) for u in range(kv)]
    slots = s_buf.shape[0]
    stats = [[] for _ in range(count)]

    def score(n):
        r, u = jobs[n]
        for copy in copies_in(r, u):
            copy.wait()
        q = jnp.concatenate(
            [q_buf[r, u, :, g * HEAD_SIZE : (g + 1) * HEAD_SIZE] for g in range(group)], axis=0
        )
        for at in range(0, span, PREFIX_BLOCK_LEN):
            rows = slice(at, min(at + PREFIX_BLOCK_LEN, span))
            s_buf[n % slots, rows] = dot_nt(kv_buf[r, u, rows, :HEAD_SIZE], q)

    def soften(n):
        r, u = jobs[n]
        slot = n % slots

        def piece(at):
            bias = bias_buf[r, at : at + CHUNK]
            return s_buf[slot, at : at + CHUNK] + jnp.concatenate([bias] * group, axis=1)

        top = None
        for at in range(0, span, CHUNK):
            high = jnp.max(piece(at).reshape(CHUNK // 8, 8, cols), axis=0)
            top = high if top is None else jnp.maximum(top, high)
        top = jnp.max(top, axis=0, keepdims=True)
        total = None
        for at in range(0, span, CHUNK):
            ex = jnp.exp2((piece(at) - top) * SCALE2)
            p_buf[slot, at : at + CHUNK] = ex.astype(BF16)
            part = jnp.sum(ex.reshape(CHUNK // 8, 8, cols), axis=0)
            total = part if total is None else total + part
        return top * SCALE2, jnp.sum(total, axis=0, keepdims=True)

    def mix(n, base, total):
        r, u = jobs[n]
        mixed = lax.dot_general(
            kv_buf[r, u, :, HEAD_SIZE:],
            p_buf[n % slots],
            (((0,), (0,)), ((), ())),
            preferred_element_type=F32,
        )
        if has_carry and u == 0:
            copy_carry(r).wait()
        if has_carry:
            stat_in = read_stat(carry_buf.at[r], heads)
        for g in range(group):
            head = u * group + g
            at = slice(head * HEAD_SIZE, (head + 1) * HEAD_SIZE)
            part = slice(g * TOK, (g + 1) * TOK)
            o_g, sum_g, base_g = mixed[:, part], total[:, part], base[:, part]
            if has_carry:
                lse_c = stat_in[head : head + 1]
                high = jnp.maximum(base_g, lse_c)
                w_c = jnp.exp2(lse_c - high)
                w_g = jnp.exp2(base_g - high)
                sum_g = w_c + sum_g * w_g
                norm = 1.0 / sum_g
                out = carry_buf[r, at].astype(F32) * (w_c * norm) + o_g * (w_g * norm)
                base_g = high
            else:
                out = o_g * (1.0 / sum_g)
            _, inner, first = spot(r, head)
            out_buf[r, first + inner : first + inner + HEAD_SIZE] = out.astype(BF16)
            stats[r].append(base_g + jnp.log2(sum_g))
        copy_out(r, u).start()
        share = heads // nouts[r]
        if len(stats[r]) == share:
            part, _, first = spot(r, u * group)
            write_stat(
                out_buf.at[r, first : first + part_rows(share)],
                jnp.concatenate(stats[r], axis=0),
                share,
            )
            stats[r].clear()
            copy_out(r, kv + part).start()

    score(0)
    for n in range(len(jobs)):
        if n + 1 < len(jobs):
            score(n + 1)
        mix(n, *soften(n))
    for r in range(count):
        for u in range(kv + nouts[r]):
            copy_out(r, u).wait()


def attend(calls, nouts, plan, q_parts, store, sib, kv_local, fresh=None, carry=None):
    count = len(calls)
    nq = len(q_parts[0])
    width = q_parts[0][0].shape[1]
    heads = nq * width // HEAD_SIZE
    group = heads // kv_local
    rows = part_rows(heads)
    shares = [part_rows(heads // n) for n in nouts for _ in range(n)]
    room = max(n * part_rows(heads // n) for n in nouts)
    span = 2 * PREFIX_BLOCK_LEN + (TOK if fresh is not None else 0)
    args = [store, sib] + [x for parts in q_parts for x in parts]
    args += list(fresh or ()) + list(carry or ())
    body = functools.partial(
        attend_kernel, calls, nouts, group, heads, nq, carry is not None, fresh is not None
    )
    any_spec = pl.BlockSpec(memory_space=pl.ANY)
    slots = 3
    out = pl.pallas_call(
        body,
        out_shape=[jax.ShapeDtypeStruct((n, TOK), BF16) for n in shares],
        in_specs=[pl.BlockSpec(memory_space=pltpu.SMEM)] + [any_spec] * len(args),
        out_specs=[any_spec] * len(shares),
        scratch_shapes=[
            pltpu.VMEM((count, kv_local, TOK, group * HEAD_SIZE), BF16),
            pltpu.VMEM((count, kv_local, span, 2 * HEAD_SIZE), BF16),
            pltpu.VMEM((count, rows, TOK), BF16),
            pltpu.VMEM((count, room, TOK), BF16),
            pltpu.VMEM((count, span, TOK), F32),
            pltpu.VMEM((slots, span, group * TOK), F32),
            pltpu.VMEM((slots, span, group * TOK), BF16),
            pltpu.SemaphoreType.DMA((count, kv_local, 4)),
            pltpu.SemaphoreType.DMA((count,)),
            pltpu.SemaphoreType.DMA((count, kv_local + max(nouts))),
        ],
        compiler_params=pltpu.CompilerParams(vmem_limit_bytes=VMEM_LIMIT),
        cost_estimate=pl.CostEstimate(
            flops=8 * heads * TOK * span * HEAD_SIZE * count,
            bytes_accessed=(4 * TOK * rows + 4 * kv_local * span * 2 * HEAD_SIZE) * count,
            transcendentals=heads * TOK * span * count,
        ),
        name="attend",
    )(plan, *args)
    out = list(out)
    return [[out.pop(0) for _ in range(n)] for n in nouts]


def merged_heads(heads, part_refs, emit):
    lses = [read_stat(ref, heads) for ref in part_refs]
    high = functools.reduce(jnp.maximum, lses)
    weights = [jnp.exp2(x - high) for x in lses]
    total = functools.reduce(jnp.add, weights)
    norm = 1.0 / total
    weights = [w * norm for w in weights]
    for head in range(heads):
        at = slice(head * HEAD_SIZE, (head + 1) * HEAD_SIZE)
        emit(
            head,
            functools.reduce(
                jnp.add,
                [w[head : head + 1] * ref[at, :].astype(F32) for w, ref in zip(weights, part_refs)],
            ),
        )
    return high + jnp.log2(total)


def merge_kernel(heads, *refs):
    count = len(refs) // 3
    for i in range(count):
        a_ref, b_ref, out_ref = refs[2 * i], refs[2 * i + 1], refs[2 * count + i]

        def emit(head, value, out_ref=out_ref):
            out_ref[head * HEAD_SIZE : (head + 1) * HEAD_SIZE, :] = value.astype(BF16)

        write_stat(out_ref, merged_heads(heads, (a_ref, b_ref), emit), heads)


def merge(pairs, heads):
    shape = pairs[0][0].shape
    spec = pl.BlockSpec(shape, lambda: (0, 0))
    args = [x for pair in pairs for x in pair]
    return pl.pallas_call(
        functools.partial(merge_kernel, heads),
        out_shape=[jax.ShapeDtypeStruct(shape, BF16)] * len(pairs),
        in_specs=[spec] * len(args),
        out_specs=[spec] * len(pairs),
        compiler_params=pltpu.CompilerParams(vmem_limit_bytes=VMEM_LIMIT),
        cost_estimate=pl.CostEstimate(
            flops=0, bytes_accessed=6 * pairs[0][0].size * len(pairs), transcendentals=0
        ),
        name="merge",
    )(*args)


def project_kernel(heads, nparts, has_acc, spans, streams, tile, at, *refs):
    part_refs = refs[:nparts]
    w_ref = refs[nparts]
    refs = list(refs[nparts + 1 :])
    acc_ref = refs.pop(0) if has_acc else None
    add_refs = [refs.pop(0) for _ in spans]
    out_ref, attn_ref, parts_ref, w_buf, part_sem, w_sem = refs
    j = pl.program_id(0)
    count = pl.num_programs(0)
    ahead = w_buf.shape[0]
    depth = w_buf.shape[1] // streams
    row0, col0 = at

    def weight_copies(t):
        slot = lax.rem(t, ahead)
        cols = pl.ds(pl.multiple_of(col0 + t * tile, tile), tile)
        return [
            pltpu.make_async_copy(
                w_ref.at[pl.ds(row0 + i * depth, depth), cols],
                w_buf.at[slot, pl.ds(i * depth, depth)],
                w_sem.at[slot, i],
            )
            for i in range(streams)
        ]

    @pl.when(j == 0)
    def _():
        copies = [
            pltpu.make_async_copy(ref, parts_ref.at[i], part_sem.at[i])
            for i, ref in enumerate(part_refs)
        ]
        for copy in copies:
            copy.start()
        for t in range(ahead - 1):
            for copy in weight_copies(t):
                copy.start()
        for copy in copies:
            copy.wait()

        def emit(head, value):
            cols = slice(head * HEAD_SIZE, (head + 1) * HEAD_SIZE)
            attn_ref[:, cols] = value.T.astype(BF16)

        merged_heads(heads, [parts_ref.at[i] for i in range(nparts)], emit)

    @pl.when(j + ahead - 1 < count)
    def _():
        for copy in weight_copies(j + ahead - 1):
            copy.start()

    for copy in weight_copies(j):
        copy.wait()
    got = jnp.dot(attn_ref[...], w_buf[lax.rem(j, ahead)], preferred_element_type=F32)
    if has_acc:
        got = got + acc_ref[...]
    if out_ref.dtype == F32:
        out_ref[...] = got
    else:
        got = got.astype(BF16)
        if spans:
            total = got.astype(F32)
            for ref, (low, high) in zip(add_refs, spans):
                here = (j >= low) & (j < high)
                total = total + jnp.where(here, ref[...].astype(F32), 0.0)
            got = total.astype(BF16)
        out_ref[...] = got


def project(parts, weight, row0=0, col0=0, cols=None, acc=None, adds=(), dtype=BF16):
    heads = next(h for h in range(1, 1000) if part_rows(h) == parts[0].shape[0])
    depth = heads * HEAD_SIZE
    cols = weight.shape[1] if cols is None else cols
    tile = 1024
    count = cols // tile
    ahead = min(4, count)
    streams = 4
    in_specs = [pl.BlockSpec(memory_space=pl.ANY)] * (len(parts) + 1)
    args = list(parts) + [weight]
    if acc is not None:
        in_specs.append(pl.BlockSpec((TOK, tile), lambda j: (0, j)))
        args.append(acc)
    spans = []
    for x, first in adds:
        low, n = first // tile, x.shape[1] // tile
        spans.append((low, low + n))
        in_specs.append(
            pl.BlockSpec((TOK, tile), lambda j, low=low, n=n: (0, jnp.clip(j - low, 0, n - 1)))
        )
        args.append(x)
    return pl.pallas_call(
        functools.partial(
            project_kernel, heads, len(parts), acc is not None, spans, streams, tile, (row0, col0)
        ),
        out_shape=jax.ShapeDtypeStruct((TOK, cols), dtype),
        grid=(count,),
        in_specs=in_specs,
        out_specs=pl.BlockSpec((TOK, tile), lambda j: (0, j)),
        scratch_shapes=[
            pltpu.VMEM((TOK, depth), BF16),
            pltpu.VMEM((len(parts),) + parts[0].shape, BF16),
            pltpu.VMEM((ahead, depth, tile), BF16),
            pltpu.SemaphoreType.DMA((len(parts),)),
            pltpu.SemaphoreType.DMA((ahead, streams)),
        ],
        compiler_params=pltpu.CompilerParams(vmem_limit_bytes=VMEM_LIMIT),
        cost_estimate=pl.CostEstimate(
            flops=2 * TOK * depth * cols,
            bytes_accessed=2 * depth * cols + 4 * TOK * cols,
            transcendentals=0,
        ),
        name="project",
    )(*args)


def shards(
    queries, new_key_values, key_value_store, o_weight, residual, hit_dev, hit_blk, prefix_len
):
    npool = lax.axis_size("pool")
    ntp = lax.axis_size("tp")
    me = lax.axis_index("pool")
    tp = lax.axis_index("tp")
    rdev = queries.shape[0] // TOK
    kv_local = key_value_store.shape[2] // (2 * HEAD_SIZE)
    nchips = npool // 2
    core = lax.rem(me, 2)
    chip = lax.div(me, 2)
    sibling = me + 1 - 2 * core
    ring = chip_ring(nchips)
    place = [ring.index(i) for i in range(nchips)]
    split_rows = ntp == rdev and rdev == 2

    swap_perm = [(p, p + 1 - 2 * (p % 2)) for p in range(npool)]
    cw_perm, ccw_perm = [], []
    for k in range(nchips):
        a, b = ring[k], ring[(k + 1) % nchips]
        for c in range(2):
            cw_perm.append((2 * a + c, 2 * b + c))
            ccw_perm.append((2 * b + c, 2 * a + c))

    starts = jnp.arange(MAXB, dtype=jnp.int32)[None, :] * PREFIX_BLOCK_LEN
    left = jnp.clip(prefix_len[:, None] - starts, 0, PREFIX_BLOCK_LEN)
    here, beside = hit_dev == me, hit_dev == sibling
    table = jnp.stack(
        [
            jnp.sum(jnp.where(at, x, 0), axis=1)
            for x, at in ((hit_blk, here), (hit_blk, beside), (left, here), (left, beside))
        ],
        axis=1,
    )
    half = nchips // 2
    steps = list(range(-half, half + 1))
    spot = jnp.asarray(place, jnp.int32)[chip]
    chips_at = jnp.asarray(ring, jnp.int32)[
        lax.rem(spot + nchips - jnp.asarray(steps, jnp.int32), nchips)
    ]
    slots = [1 - tp, tp] if split_rows else [jnp.int32(i) for i in range(rdev)]
    wanted = ((chips_at * 2 + core) * rdev)[None, :] + jnp.stack(slots)[:, None]
    plan = jnp.take(table, wanted.reshape(-1), axis=0, mode="clip").reshape(-1)
    sib = lax.ppermute(key_value_store, "pool", swap_perm)

    heads = queries.shape[1] // HEAD_SIZE
    nq = 2 if kv_local % 2 == 0 else 1
    width = heads // nq * HEAD_SIZE

    def travel(x, hops_cw, hops_ccw, held, key):
        for sign, perm, hops in ((1, cw_perm, hops_cw), (-1, ccw_perm, hops_ccw)):
            moving = x
            for t in range(1, hops + 1):
                moving = lax.ppermute(moving, "pool", perm)
                held[sign * t, key] = moving

    def after(x, *others):
        return lax.optimization_barrier((x,) + others)[0]

    def reach(flip):
        if nchips % 2:
            return half, half
        return (half - 1, half) if flip else (half, half - 1)

    q_of, fresh_of = [], []
    for order, slot in enumerate(slots):
        held = {}
        fresh_of.append(lax.dynamic_slice_in_dim(new_key_values, slot * TOK, TOK, 0))
        if order == 0:
            for part in range(nq):
                q = lax.dynamic_slice(queries, (slot * TOK, part * width), (TOK, width))
                held[0, part] = q
                travel(q, *reach(part % 2), held, part)
            for part in range(nq):
                far = [held[t, part] for t in (half, -half) if (t, part) in held]
                for t in (half, -half):
                    if far:
                        held.setdefault((t, part), far[0])
            q_of.append({t: [held.get((t, part)) for part in range(nq)] for t in steps})
        else:
            q = lax.dynamic_slice_in_dim(queries, slot * TOK, TOK, 0)
            travel(q, *reach(False), held, 0)
            q_of.append({t: [x] for (t, _), x in held.items()})
            q_of[order][0] = [q[:, part * width : (part + 1) * width] for part in range(nq)]

    last = [None]
    nouts = [1] + [nq] * (rdev - 1)

    def run(wanted, **more):
        calls = [order * len(steps) + steps.index(t) for order, t in wanted]
        table = plan if last[0] is None else after(plan, last[0])
        out = attend(
            calls, [nouts[order] for order, _ in wanted], table,
            [q_of[order][t] for order, t in wanted], key_value_store, sib, kv_local, **more,
        )
        last[0] = out[0][0]
        return out

    carry = {}
    hops = dict(zip((1, -1), reach(False)))
    back = {1: ccw_perm, -1: cw_perm}
    early = {}
    own = []
    for i in range(half):
        wanted = [(sign, hops[sign] - i) for sign in (1, -1) if hops[sign] > i]
        more = {"carry": [carry[sign] for sign, _ in wanted]} if i else {}
        got = run([(0, sign * t) for sign, t in wanted], **more)
        for (sign, _), (x,) in zip(wanted, got):
            carry[sign] = lax.ppermute(x, "pool", back[sign])
        if i == 0:
            own = run([(order, 0) for order in range(rdev)], fresh=fresh_of)
        reached = [i] if i < half - 1 else [half - 1, half]
        fill = [
            (order, sign * t)
            for order in range(1, rdev) for t in reached for sign in (1, -1)
            if t > 0 and sign * t in q_of[order]
        ]
        if fill:
            early.update(zip(fill, run(fill)))
    parts = [[own[0][0]] + list(carry.values())]
    parts[0][0] = after(parts[0][0], last[0])

    shares = heads // nq
    ends = []
    for order in range(1, rdev):
        for t in (half, -half):
            if (order, t) not in early and (order, -t) in early:
                early[order, t] = early[order, -t]
        ends.append([])
        for part in range(nq):
            counts = dict(zip((1, -1), reach(part % 2)))
            moving = {}
            for i in range(half):
                signs = [sign for sign in (1, -1) if counts[sign] > i]
                local = [early[order, sign * (counts[sign] - i)][part] for sign in signs]
                if i:
                    local = merge([(x, moving[sign]) for x, sign in zip(local, signs)], shares)
                for sign, x in zip(signs, local):
                    moving[sign] = lax.ppermute(x, "pool", back[sign])
            ends[-1].append([own[order][part]] + list(moving.values()))

    def project_shares(shared, adds=()):
        total = None
        for part, group in enumerate(shared):
            final = part == len(shared) - 1
            total = project(
                group, o_weight, row0=part * shares * HEAD_SIZE, acc=total,
                adds=adds if final else (), dtype=BF16 if final else F32,
            )
        return total

    if split_rows:
        model = o_weight.shape[1]
        got = []
        for col0 in (0, model // 2):
            away = project(parts[0], o_weight, col0=col0, cols=model // 2)
            got.append((lax.ppermute(away, "tp", [(0, 1), (1, 0)]), col0))
        return project_shares(ends[0], got + [(residual, 0)])
    rows = [project(parts[0], o_weight)] + [project_shares(x) for x in ends]
    mine = lax.psum_scatter(
        jnp.concatenate(rows, axis=0), "tp", scatter_dimension=0, tiled=True
    )
    return (mine.astype(F32) + residual.astype(F32)).astype(BF16)


def solution(mesh):
    placed = (
        P("pool", "tp"),
        P("pool", "tp"),
        P("pool", None, "tp"),
        P("tp", None),
        P(("pool", "tp"), None),
        P(),
        P(),
        P(),
    )
    return jax.shard_map(
        shards, mesh=mesh, in_specs=placed, out_specs=P(("pool", "tp"), None), check_vma=False
    )
```

```python
import functools

import jax
import jax.numpy as jnp
from jax import lax
from jax.experimental import pallas as pl
from jax.experimental.pallas import tpu as pltpu
from jax.sharding import PartitionSpec as P

HEAD_SIZE = 128
NEW_TOKEN_COUNT = 128
PREFIX_BLOCK_LEN = 256
MAXB = 16
LOG2E = 1.4426950408889634
SCALE2 = HEAD_SIZE ** (-0.5) * LOG2E
NEG = -1e30
F32 = jnp.float32
BF16 = jnp.bfloat16
TOK = NEW_TOKEN_COUNT
VMEM_LIMIT = 64 * 1024 * 1024
CHUNK = 64


def dot_nt(a, b):
    return lax.dot_general(a, b, (((1,), (1,)), ((), ())), preferred_element_type=F32)


def chip_ring(nchips):
    if nchips % 2:
        return list(range(nchips))
    up = list(range(0, nchips, 2))
    return up + [chip + 1 for chip in reversed(up)]


def stat_rows(heads):
    return -(-3 * heads // 16) * 16


def part_rows(heads):
    return heads * HEAD_SIZE + stat_rows(heads)


def read_stat(ref, heads):
    s = ref[heads * HEAD_SIZE :, :].astype(F32)
    return s[:heads] + s[heads : 2 * heads] + s[2 * heads : 3 * heads]


def write_stat(ref, stat, heads):
    first = stat.astype(BF16).astype(F32)
    second = (stat - first).astype(BF16).astype(F32)
    third = stat - first - second
    terms = [first, second, third]
    extra = stat_rows(heads) - 3 * heads
    if extra:
        terms.append(jnp.zeros((extra, TOK), F32))
    ref[heads * HEAD_SIZE :, :] = jnp.concatenate(terms, axis=0).astype(BF16)


def attend_kernel(calls, nouts, nqs, shares, group, heads, has_carry, has_fresh, plan_ref, *refs):
    refs = list(refs)
    count = len(calls)
    kv = heads // group
    per_q = kv // shares
    pair = 2 * HEAD_SIZE
    width = group * HEAD_SIZE
    cols = group * TOK
    span = 2 * PREFIX_BLOCK_LEN + (TOK if has_fresh else 0)

    store_ref, sib_ref = refs.pop(0), refs.pop(0)
    q_refs = [[refs.pop(0) for _ in range(n)] for n in nqs]
    fresh_refs = [refs.pop(0) for _ in range(count)] if has_fresh else None
    carry_refs = [refs.pop(0) for _ in range(count)] if has_carry else None
    out_refs = [[refs.pop(0) for _ in range(n)] for n in nouts]
    q_buf, kv_buf, carry_buf, out_buf, bias_buf, s_buf, p_buf, in_sem, carry_sem, out_sem = refs

    def copies_in(r, part):
        at = slice(part * per_q * pair, (part + 1) * per_q * pair)
        cols = slice(part * per_q * width, (part + 1) * per_q * width)
        block, other = plan_ref[4 * calls[r]], plan_ref[4 * calls[r] + 1]
        q = q_refs[r][part] if len(q_refs[r]) > 1 else q_refs[r][0].at[:, cols]
        moves = [
            (q, q_buf.at[r, :, cols]),
            (store_ref.at[block, :, at], kv_buf.at[r, 0:PREFIX_BLOCK_LEN, at]),
            (sib_ref.at[other, :, at], kv_buf.at[r, PREFIX_BLOCK_LEN : 2 * PREFIX_BLOCK_LEN, at]),
        ]
        if has_fresh:
            moves.append((fresh_refs[r].at[:, at], kv_buf.at[r, 2 * PREFIX_BLOCK_LEN : span, at]))
        return [
            pltpu.make_async_copy(a, b, in_sem.at[r, part, i]) for i, (a, b) in enumerate(moves)
        ]

    def copy_carry(r):
        return pltpu.make_async_copy(carry_refs[r], carry_buf.at[r], carry_sem.at[r])

    def spot(r, head):
        share = heads // nouts[r]
        return head // share, head % share * HEAD_SIZE, head // share * part_rows(share)

    def copy_out(r, u):
        if u < kv:
            part, inner, base = spot(r, u * group)
            n = group * HEAD_SIZE
        else:
            part, share = u - kv, heads // nouts[r]
            inner, base, n = share * HEAD_SIZE, part * part_rows(share), stat_rows(share)
        return pltpu.make_async_copy(
            out_buf.at[r, base + inner : base + inner + n],
            out_refs[r][part].at[inner : inner + n],
            out_sem.at[r, u],
        )

    for r in range(count):
        for part in range(shares):
            for copy in copies_in(r, part):
                copy.start()
            if part == 0 and has_carry:
                copy_carry(r).start()

    for r in range(count):
        at = lax.broadcasted_iota(jnp.int32, (PREFIX_BLOCK_LEN, TOK), 0)
        for i in range(2):
            valid = at < plan_ref[4 * calls[r] + 2 + i]
            bias_buf[r, i * PREFIX_BLOCK_LEN : (i + 1) * PREFIX_BLOCK_LEN] = jnp.where(
                valid, 0.0, NEG
            ).astype(F32)
        if has_fresh:
            new = lax.broadcasted_iota(jnp.int32, (TOK, TOK), 0)
            tok = lax.broadcasted_iota(jnp.int32, (TOK, TOK), 1)
            bias_buf[r, 2 * PREFIX_BLOCK_LEN : span] = jnp.where(new <= tok, 0.0, NEG).astype(F32)

    jobs = [(r, u) for r in range(count) for u in range(kv)]
    slots = s_buf.shape[0]
    stats = [[] for _ in range(count)]

    def score(n):
        r, u = jobs[n]
        if u % per_q == 0:
            for copy in copies_in(r, u // per_q):
                copy.wait()
        at = u * width
        q = jnp.concatenate(
            [q_buf[r, :, at + g * HEAD_SIZE : at + (g + 1) * HEAD_SIZE] for g in range(group)],
            axis=0,
        )
        at = u * pair
        for low in range(0, span, PREFIX_BLOCK_LEN):
            rows = slice(low, min(low + PREFIX_BLOCK_LEN, span))
            s_buf[n % slots, rows] = dot_nt(kv_buf[r, rows, at : at + HEAD_SIZE], q)

    def soften(n):
        r, u = jobs[n]
        slot = n % slots

        def piece(at):
            bias = bias_buf[r, at : at + CHUNK]
            return s_buf[slot, at : at + CHUNK] + jnp.concatenate([bias] * group, axis=1)

        top = None
        for at in range(0, span, CHUNK):
            high = jnp.max(piece(at).reshape(CHUNK // 8, 8, cols), axis=0)
            top = high if top is None else jnp.maximum(top, high)
        top = jnp.max(top, axis=0, keepdims=True)
        total = None
        for at in range(0, span, CHUNK):
            ex = jnp.exp2((piece(at) - top) * SCALE2)
            p_buf[slot, at : at + CHUNK] = ex.astype(BF16)
            part = jnp.sum(ex.reshape(CHUNK // 8, 8, cols), axis=0)
            total = part if total is None else total + part
        return top * SCALE2, jnp.sum(total, axis=0, keepdims=True)

    def mix(n, base, total):
        r, u = jobs[n]
        mixed = lax.dot_general(
            kv_buf[r, :, u * pair + HEAD_SIZE : (u + 1) * pair],
            p_buf[n % slots],
            (((0,), (0,)), ((), ())),
            preferred_element_type=F32,
        )
        if has_carry and u == 0:
            copy_carry(r).wait()
        if has_carry:
            stat_in = read_stat(carry_buf.at[r], heads)
        for g in range(group):
            head = u * group + g
            at = slice(head * HEAD_SIZE, (head + 1) * HEAD_SIZE)
            part = slice(g * TOK, (g + 1) * TOK)
            o_g, sum_g, base_g = mixed[:, part], total[:, part], base[:, part]
            if has_carry:
                lse_c = stat_in[head : head + 1]
                high = jnp.maximum(base_g, lse_c)
                w_c = jnp.exp2(lse_c - high)
                w_g = jnp.exp2(base_g - high)
                sum_g = w_c + sum_g * w_g
                norm = 1.0 / sum_g
                out = carry_buf[r, at].astype(F32) * (w_c * norm) + o_g * (w_g * norm)
                base_g = high
            else:
                out = o_g * (1.0 / sum_g)
            _, inner, first = spot(r, head)
            out_buf[r, first + inner : first + inner + HEAD_SIZE] = out.astype(BF16)
            stats[r].append(base_g + jnp.log2(sum_g))
        copy_out(r, u).start()
        share = heads // nouts[r]
        if len(stats[r]) == share:
            part, _, first = spot(r, u * group)
            write_stat(
                out_buf.at[r, first : first + part_rows(share)],
                jnp.concatenate(stats[r], axis=0),
                share,
            )
            stats[r].clear()
            copy_out(r, kv + part).start()

    score(0)
    for n in range(len(jobs)):
        if n + 1 < len(jobs):
            score(n + 1)
        mix(n, *soften(n))
    for r in range(count):
        for u in range(kv + nouts[r]):
            copy_out(r, u).wait()


def attend(calls, nouts, shares, plan, q_parts, store, sib, kv_local, fresh=None, carry=None):
    count = len(calls)
    nqs = [len(parts) for parts in q_parts]
    heads = nqs[0] * q_parts[0][0].shape[1] // HEAD_SIZE
    group = heads // kv_local
    rows = part_rows(heads)
    sizes = [part_rows(heads // n) for n in nouts for _ in range(n)]
    room = max(n * part_rows(heads // n) for n in nouts)
    span = 2 * PREFIX_BLOCK_LEN + (TOK if fresh is not None else 0)
    args = [store, sib] + [x for parts in q_parts for x in parts]
    args += list(fresh or ()) + list(carry or ())
    body = functools.partial(
        attend_kernel, calls, nouts, nqs, shares, group, heads, carry is not None, fresh is not None
    )
    any_spec = pl.BlockSpec(memory_space=pl.ANY)
    slots = 3
    out = pl.pallas_call(
        body,
        out_shape=[jax.ShapeDtypeStruct((n, TOK), BF16) for n in sizes],
        in_specs=[pl.BlockSpec(memory_space=pltpu.SMEM)] + [any_spec] * len(args),
        out_specs=[any_spec] * len(sizes),
        scratch_shapes=[
            pltpu.VMEM((count, TOK, heads * HEAD_SIZE), BF16),
            pltpu.VMEM((count, span, kv_local * 2 * HEAD_SIZE), BF16),
            pltpu.VMEM((count, rows, TOK), BF16),
            pltpu.VMEM((count, room, TOK), BF16),
            pltpu.VMEM((count, span, TOK), F32),
            pltpu.VMEM((slots, span, group * TOK), F32),
            pltpu.VMEM((slots, span, group * TOK), BF16),
            pltpu.SemaphoreType.DMA((count, shares, 4)),
            pltpu.SemaphoreType.DMA((count,)),
            pltpu.SemaphoreType.DMA((count, kv_local + max(nouts))),
        ],
        compiler_params=pltpu.CompilerParams(vmem_limit_bytes=VMEM_LIMIT),
        cost_estimate=pl.CostEstimate(
            flops=8 * heads * TOK * span * HEAD_SIZE * count,
            bytes_accessed=(4 * TOK * rows + 4 * kv_local * span * 2 * HEAD_SIZE) * count,
            transcendentals=heads * TOK * span * count,
        ),
        name="attend",
    )(plan, *args)
    out = list(out)
    return [[out.pop(0) for _ in range(n)] for n in nouts]


def merged_heads(heads, part_refs, emit):
    lses = [read_stat(ref, heads) for ref in part_refs]
    high = functools.reduce(jnp.maximum, lses)
    weights = [jnp.exp2(x - high) for x in lses]
    total = functools.reduce(jnp.add, weights)
    norm = 1.0 / total
    weights = [w * norm for w in weights]
    for head in range(heads):
        at = slice(head * HEAD_SIZE, (head + 1) * HEAD_SIZE)
        emit(
            head,
            functools.reduce(
                jnp.add,
                [w[head : head + 1] * ref[at, :].astype(F32) for w, ref in zip(weights, part_refs)],
            ),
        )
    return high + jnp.log2(total)


def merge_kernel(heads, *refs):
    count = len(refs) // 3
    for i in range(count):
        a_ref, b_ref, out_ref = refs[2 * i], refs[2 * i + 1], refs[2 * count + i]

        def emit(head, value, out_ref=out_ref):
            out_ref[head * HEAD_SIZE : (head + 1) * HEAD_SIZE, :] = value.astype(BF16)

        write_stat(out_ref, merged_heads(heads, (a_ref, b_ref), emit), heads)


def merge(pairs, heads):
    shape = pairs[0][0].shape
    spec = pl.BlockSpec(shape, lambda: (0, 0))
    args = [x for pair in pairs for x in pair]
    return pl.pallas_call(
        functools.partial(merge_kernel, heads),
        out_shape=[jax.ShapeDtypeStruct(shape, BF16)] * len(pairs),
        in_specs=[spec] * len(args),
        out_specs=[spec] * len(pairs),
        compiler_params=pltpu.CompilerParams(vmem_limit_bytes=VMEM_LIMIT),
        cost_estimate=pl.CostEstimate(
            flops=0, bytes_accessed=6 * pairs[0][0].size * len(pairs), transcendentals=0
        ),
        name="merge",
    )(*args)


def project_kernel(heads, counts, spans, streams, tile, *refs):
    refs = list(refs)
    part_refs = [refs.pop(0) for _ in range(sum(counts))]
    w_ref = refs.pop(0)
    add_refs = [refs.pop(0) for _ in spans]
    out_ref, attn_ref, parts_ref, w_buf, part_sem, w_sem = refs
    j = pl.program_id(0)
    count = pl.num_programs(0)
    ahead = w_buf.shape[0]
    depth = w_buf.shape[1] // streams

    def weight_copies(t):
        slot = lax.rem(t, ahead)
        cols = pl.ds(pl.multiple_of(t * tile, tile), tile)
        return [
            pltpu.make_async_copy(
                w_ref.at[pl.ds(i * depth, depth), cols],
                w_buf.at[slot, pl.ds(i * depth, depth)],
                w_sem.at[slot, i],
            )
            for i in range(streams)
        ]

    @pl.when(j == 0)
    def _():
        copies = [
            pltpu.make_async_copy(ref, parts_ref.at[i], part_sem.at[i])
            for i, ref in enumerate(part_refs)
        ]
        for copy in copies:
            copy.start()
        for t in range(ahead - 1):
            for copy in weight_copies(t):
                copy.start()
        for copy in copies:
            copy.wait()

        first = 0
        for share, n in enumerate(counts):

            def emit(head, value, base=share * heads):
                cols = slice((base + head) * HEAD_SIZE, (base + head + 1) * HEAD_SIZE)
                attn_ref[:, cols] = value.T.astype(BF16)

            merged_heads(heads, [parts_ref.at[i] for i in range(first, first + n)], emit)
            first += n

    @pl.when(j + ahead - 1 < count)
    def _():
        for copy in weight_copies(j + ahead - 1):
            copy.start()

    for copy in weight_copies(j):
        copy.wait()
    got = jnp.dot(attn_ref[...], w_buf[lax.rem(j, ahead)], preferred_element_type=F32)
    got = got.astype(BF16)
    if spans:
        total = got.astype(F32)
        for ref, (low, high) in zip(add_refs, spans):
            here = (j >= low) & (j < high)
            total = total + jnp.where(here, ref[...].astype(F32), 0.0)
        got = total.astype(BF16)
    out_ref[...] = got


def project(shared, weight, adds=()):
    parts = [x for group in shared for x in group]
    depth, cols = weight.shape
    heads = depth // HEAD_SIZE // len(shared)
    tile = 1024
    count = cols // tile
    ahead = min(4, count)
    streams = 4
    in_specs = [pl.BlockSpec(memory_space=pl.ANY)] * (len(parts) + 1)
    args = parts + [weight]
    spans = []
    for x, first in adds:
        low, n = first // tile, x.shape[1] // tile
        spans.append((low, low + n))
        in_specs.append(
            pl.BlockSpec((TOK, tile), lambda j, low=low, n=n: (0, jnp.clip(j - low, 0, n - 1)))
        )
        args.append(x)
    return pl.pallas_call(
        functools.partial(
            project_kernel, heads, [len(group) for group in shared], spans, streams, tile
        ),
        out_shape=jax.ShapeDtypeStruct((TOK, cols), BF16),
        grid=(count,),
        in_specs=in_specs,
        out_specs=pl.BlockSpec((TOK, tile), lambda j: (0, j)),
        scratch_shapes=[
            pltpu.VMEM((TOK, depth), BF16),
            pltpu.VMEM((len(parts),) + parts[0].shape, BF16),
            pltpu.VMEM((ahead, depth, tile), BF16),
            pltpu.SemaphoreType.DMA((len(parts),)),
            pltpu.SemaphoreType.DMA((ahead, streams)),
        ],
        compiler_params=pltpu.CompilerParams(vmem_limit_bytes=VMEM_LIMIT),
        cost_estimate=pl.CostEstimate(
            flops=2 * TOK * depth * cols,
            bytes_accessed=2 * depth * cols + 4 * TOK * cols,
            transcendentals=0,
        ),
        name="project",
    )(*args)


def shards(
    queries, new_key_values, key_value_store, o_weight, residual, hit_dev, hit_blk, prefix_len
):
    npool = lax.axis_size("pool")
    ntp = lax.axis_size("tp")
    me = lax.axis_index("pool")
    tp = lax.axis_index("tp")
    rdev = queries.shape[0] // TOK
    kv_local = key_value_store.shape[2] // (2 * HEAD_SIZE)
    nchips = npool // 2
    core = lax.rem(me, 2)
    chip = lax.div(me, 2)
    sibling = me + 1 - 2 * core
    ring = chip_ring(nchips)
    place = [ring.index(i) for i in range(nchips)]
    split_rows = ntp == rdev and rdev == 2

    swap_perm = [(p, p + 1 - 2 * (p % 2)) for p in range(npool)]
    cw_perm, ccw_perm = [], []
    for k in range(nchips):
        a, b = ring[k], ring[(k + 1) % nchips]
        for c in range(2):
            cw_perm.append((2 * a + c, 2 * b + c))
            ccw_perm.append((2 * b + c, 2 * a + c))

    starts = jnp.arange(MAXB, dtype=jnp.int32)[None, :] * PREFIX_BLOCK_LEN
    left = jnp.clip(prefix_len[:, None] - starts, 0, PREFIX_BLOCK_LEN)
    here, beside = hit_dev == me, hit_dev == sibling
    table = jnp.stack(
        [
            jnp.sum(jnp.where(at, x, 0), axis=1)
            for x, at in ((hit_blk, here), (hit_blk, beside), (left, here), (left, beside))
        ],
        axis=1,
    )
    half = nchips // 2
    steps = list(range(-half, half + 1))
    spot = jnp.asarray(place, jnp.int32)[chip]
    chips_at = jnp.asarray(ring, jnp.int32)[
        lax.rem(spot + nchips - jnp.asarray(steps, jnp.int32), nchips)
    ]
    slots = [1 - tp, tp] if split_rows else [jnp.int32(i) for i in range(rdev)]
    wanted = ((chips_at * 2 + core) * rdev)[None, :] + jnp.stack(slots)[:, None]
    plan = jnp.take(table, wanted.reshape(-1), axis=0, mode="clip").reshape(-1)
    sib = lax.ppermute(key_value_store, "pool", swap_perm)

    heads = queries.shape[1] // HEAD_SIZE
    nq = 2 if kv_local % 2 == 0 else 1
    width = heads // nq * HEAD_SIZE

    def travel(x, hops_cw, hops_ccw, held, key):
        for sign, perm, hops in ((1, cw_perm, hops_cw), (-1, ccw_perm, hops_ccw)):
            moving = x
            for t in range(1, hops + 1):
                moving = lax.ppermute(moving, "pool", perm)
                held[sign * t, key] = moving

    def after(x, *others):
        return lax.optimization_barrier((x,) + others)[0]

    def reach(flip):
        if nchips % 2:
            return half, half
        return (half - 1, half) if flip else (half, half - 1)

    q_of, fresh_of = [], []
    for order, slot in enumerate(slots):
        held = {}
        fresh_of.append(lax.dynamic_slice_in_dim(new_key_values, slot * TOK, TOK, 0))
        if order == 0:
            for part in range(nq):
                q = lax.dynamic_slice(queries, (slot * TOK, part * width), (TOK, width))
                held[0, part] = q
                travel(q, *reach(part % 2), held, part)
            for part in range(nq):
                far = [held[t, part] for t in (half, -half) if (t, part) in held]
                for t in (half, -half):
                    if far:
                        held.setdefault((t, part), far[0])
            q_of.append({t: [held.get((t, part)) for part in range(nq)] for t in steps})
        else:
            q = lax.dynamic_slice_in_dim(queries, slot * TOK, TOK, 0)
            travel(q, *reach(False), held, 0)
            q_of.append({t: [x] for (t, _), x in held.items()})
            q_of[order][0] = [q[:, part * width : (part + 1) * width] for part in range(nq)]

    last = [None]
    nouts = [1] + [nq] * (rdev - 1)

    def run(wanted, **more):
        calls = [order * len(steps) + steps.index(t) for order, t in wanted]
        table = plan if last[0] is None else after(plan, last[0])
        out = attend(
            calls, [nouts[order] for order, _ in wanted], nq, table,
            [q_of[order][t] for order, t in wanted], key_value_store, sib, kv_local, **more,
        )
        last[0] = out[0][0]
        return out

    carry = {}
    hops = dict(zip((1, -1), reach(False)))
    back = {1: ccw_perm, -1: cw_perm}
    early = {}
    own = run([(order, 0) for order in range(rdev)], fresh=fresh_of)
    for i in range(half):
        wanted = [(sign, hops[sign] - i) for sign in (1, -1) if hops[sign] > i]
        more = {"carry": [carry[sign] for sign, _ in wanted]} if i else {}
        got = run([(0, sign * t) for sign, t in wanted], **more)
        for (sign, _), (x,) in zip(wanted, got):
            carry[sign] = lax.ppermute(x, "pool", back[sign])
        reached = [i] if i < half - 1 else [half - 1, half]
        fill = [
            (order, sign * t)
            for order in range(1, rdev) for t in reached for sign in (1, -1)
            if t > 0 and sign * t in q_of[order]
        ]
        if fill:
            early.update(zip(fill, run(fill)))
    parts = [[own[0][0]] + list(carry.values())]
    parts[0][0] = after(parts[0][0], last[0])

    shares = heads // nq
    ends = []
    for order in range(1, rdev):
        for t in (half, -half):
            if (order, t) not in early and (order, -t) in early:
                early[order, t] = early[order, -t]
        ends.append([])
        for part in range(nq):
            counts = dict(zip((1, -1), reach(part % 2)))
            moving = {}
            for i in range(half):
                signs = [sign for sign in (1, -1) if counts[sign] > i]
                local = [early[order, sign * (counts[sign] - i)][part] for sign in signs]
                if i:
                    local = merge([(x, moving[sign]) for x, sign in zip(local, signs)], shares)
                for sign, x in zip(signs, local):
                    moving[sign] = lax.ppermute(x, "pool", back[sign])
            ends[-1].append([own[order][part]] + list(moving.values()))

    if split_rows:
        away = project([parts[0]], o_weight)
        got = lax.ppermute(away, "tp", [(0, 1), (1, 0)])
        return project(ends[0], o_weight, [(got, 0), (residual, 0)])
    rows = [project(x, o_weight) for x in [[parts[0]]] + ends]
    mine = lax.psum_scatter(
        jnp.concatenate(rows, axis=0), "tp", scatter_dimension=0, tiled=True
    )
    return (mine.astype(F32) + residual.astype(F32)).astype(BF16)


def solution(mesh):
    placed = (
        P("pool", "tp"),
        P("pool", "tp"),
        P("pool", None, "tp"),
        P("tp", None),
        P(("pool", "tp"), None),
        P(),
        P(),
        P(),
    )
    return jax.shard_map(
        shards, mesh=mesh, in_specs=placed, out_specs=P(("pool", "tp"), None), check_vma=False
    )
```

```python
import functools

import jax
import jax.numpy as jnp
from jax import lax
from jax.experimental import pallas as pl
from jax.experimental.pallas import tpu as pltpu
from jax.sharding import PartitionSpec as P

HEAD_SIZE = 128
NEW_TOKEN_COUNT = 128
PREFIX_BLOCK_LEN = 256
MAXB = 16
LOG2E = 1.4426950408889634
SCALE2 = HEAD_SIZE ** (-0.5) * LOG2E
NEG = -1e30
F32 = jnp.float32
BF16 = jnp.bfloat16
TOK = NEW_TOKEN_COUNT
VMEM_LIMIT = 64 * 1024 * 1024
CHUNK = 64
XPIECES = 4
GOT = {2: 0, 3: 1}


def dot_nt(a, b):
    return lax.dot_general(a, b, (((1,), (1,)), ((), ())), preferred_element_type=F32)


def chip_ring(nchips):
    if nchips % 2:
        return list(range(nchips))
    up = list(range(0, nchips, 2))
    return up + [chip + 1 for chip in reversed(up)]


def stat_rows(heads):
    return -(-3 * heads // 16) * 16


def part_rows(heads):
    return heads * HEAD_SIZE + stat_rows(heads)


def read_stat(ref, heads):
    s = ref[heads * HEAD_SIZE :, :].astype(F32)
    return s[:heads] + s[heads : 2 * heads] + s[2 * heads : 3 * heads]


def write_stat(ref, stat, heads):
    first = stat.astype(BF16).astype(F32)
    second = (stat - first).astype(BF16).astype(F32)
    third = stat - first - second
    terms = [first, second, third]
    extra = stat_rows(heads) - 3 * heads
    if extra:
        terms.append(jnp.zeros((extra, TOK), F32))
    ref[heads * HEAD_SIZE :, :] = jnp.concatenate(terms, axis=0).astype(BF16)


def attend_kernel(
    calls, nouts, nqs, shares, group, heads, ndeps, has_carry, has_fresh, plan_ref, *refs
):
    refs = list(refs)
    count = len(calls)
    kv = heads // group
    per_q = kv // shares
    pair = 2 * HEAD_SIZE
    width = group * HEAD_SIZE
    cols = group * TOK
    span = 2 * PREFIX_BLOCK_LEN + (TOK if has_fresh else 0)

    store_ref, sib_ref = refs.pop(0), refs.pop(0)
    q_refs = [[refs.pop(0) for _ in range(n)] for n in nqs]
    fresh_refs = [refs.pop(0) for _ in range(count)] if has_fresh else None
    carry_refs = [refs.pop(0) for _ in range(count)] if has_carry else None
    del refs[:ndeps]
    out_refs = [[refs.pop(0) for _ in range(n)] for n in nouts]
    q_buf, kv_buf, carry_buf, out_buf, bias_buf, s_buf, p_buf, in_sem, carry_sem, out_sem = refs

    def copies_in(r, part):
        at = slice(part * per_q * pair, (part + 1) * per_q * pair)
        cols = slice(part * per_q * width, (part + 1) * per_q * width)
        block, other = plan_ref[4 * calls[r]], plan_ref[4 * calls[r] + 1]
        q = q_refs[r][part] if len(q_refs[r]) > 1 else q_refs[r][0].at[:, cols]
        moves = [
            (q, q_buf.at[r, :, cols]),
            (store_ref.at[block, :, at], kv_buf.at[r, 0:PREFIX_BLOCK_LEN, at]),
            (sib_ref.at[other, :, at], kv_buf.at[r, PREFIX_BLOCK_LEN : 2 * PREFIX_BLOCK_LEN, at]),
        ]
        if has_fresh:
            moves.append((fresh_refs[r].at[:, at], kv_buf.at[r, 2 * PREFIX_BLOCK_LEN : span, at]))
        return [
            pltpu.make_async_copy(a, b, in_sem.at[r, part, i]) for i, (a, b) in enumerate(moves)
        ]

    def copy_carry(r):
        return pltpu.make_async_copy(carry_refs[r], carry_buf.at[r], carry_sem.at[r])

    def spot(r, head):
        share = heads // nouts[r]
        return head // share, head % share * HEAD_SIZE, head // share * part_rows(share)

    def copy_out(r, u):
        if u < kv:
            part, inner, base = spot(r, u * group)
            n = group * HEAD_SIZE
        else:
            part, share = u - kv, heads // nouts[r]
            inner, base, n = share * HEAD_SIZE, part * part_rows(share), stat_rows(share)
        return pltpu.make_async_copy(
            out_buf.at[r, base + inner : base + inner + n],
            out_refs[r][part].at[inner : inner + n],
            out_sem.at[r, u],
        )

    for r in range(count):
        for part in range(shares):
            for copy in copies_in(r, part):
                copy.start()
            if part == 0 and has_carry:
                copy_carry(r).start()

    for r in range(count):
        at = lax.broadcasted_iota(jnp.int32, (PREFIX_BLOCK_LEN, TOK), 0)
        for i in range(2):
            valid = at < plan_ref[4 * calls[r] + 2 + i]
            bias_buf[r, i * PREFIX_BLOCK_LEN : (i + 1) * PREFIX_BLOCK_LEN] = jnp.where(
                valid, 0.0, NEG
            ).astype(F32)
        if has_fresh:
            new = lax.broadcasted_iota(jnp.int32, (TOK, TOK), 0)
            tok = lax.broadcasted_iota(jnp.int32, (TOK, TOK), 1)
            bias_buf[r, 2 * PREFIX_BLOCK_LEN : span] = jnp.where(new <= tok, 0.0, NEG).astype(F32)

    jobs = [(r, u) for r in range(count) for u in range(kv)]
    slots = s_buf.shape[0]
    stats = [[] for _ in range(count)]

    def score(n):
        r, u = jobs[n]
        if u % per_q == 0:
            for copy in copies_in(r, u // per_q):
                copy.wait()
        at = u * width
        q = jnp.concatenate(
            [q_buf[r, :, at + g * HEAD_SIZE : at + (g + 1) * HEAD_SIZE] for g in range(group)],
            axis=0,
        )
        at = u * pair
        for low in range(0, span, PREFIX_BLOCK_LEN):
            rows = slice(low, min(low + PREFIX_BLOCK_LEN, span))
            s_buf[n % slots, rows] = dot_nt(kv_buf[r, rows, at : at + HEAD_SIZE], q)

    def soften(n):
        r, u = jobs[n]
        slot = n % slots

        def piece(at):
            bias = bias_buf[r, at : at + CHUNK]
            return s_buf[slot, at : at + CHUNK] + jnp.concatenate([bias] * group, axis=1)

        top = None
        for at in range(0, span, CHUNK):
            high = jnp.max(piece(at).reshape(CHUNK // 8, 8, cols), axis=0)
            top = high if top is None else jnp.maximum(top, high)
        top = jnp.max(top, axis=0, keepdims=True)
        total = None
        for at in range(0, span, CHUNK):
            ex = jnp.exp2((piece(at) - top) * SCALE2)
            p_buf[slot, at : at + CHUNK] = ex.astype(BF16)
            part = jnp.sum(ex.reshape(CHUNK // 8, 8, cols), axis=0)
            total = part if total is None else total + part
        return top * SCALE2, jnp.sum(total, axis=0, keepdims=True)

    def mix(n, base, total):
        r, u = jobs[n]
        mixed = lax.dot_general(
            kv_buf[r, :, u * pair + HEAD_SIZE : (u + 1) * pair],
            p_buf[n % slots],
            (((0,), (0,)), ((), ())),
            preferred_element_type=F32,
        )
        if has_carry and u == 0:
            copy_carry(r).wait()
        if has_carry:
            stat_in = read_stat(carry_buf.at[r], heads)
        for g in range(group):
            head = u * group + g
            at = slice(head * HEAD_SIZE, (head + 1) * HEAD_SIZE)
            part = slice(g * TOK, (g + 1) * TOK)
            o_g, sum_g, base_g = mixed[:, part], total[:, part], base[:, part]
            if has_carry:
                lse_c = stat_in[head : head + 1]
                high = jnp.maximum(base_g, lse_c)
                w_c = jnp.exp2(lse_c - high)
                w_g = jnp.exp2(base_g - high)
                sum_g = w_c + sum_g * w_g
                norm = 1.0 / sum_g
                out = carry_buf[r, at].astype(F32) * (w_c * norm) + o_g * (w_g * norm)
                base_g = high
            else:
                out = o_g * (1.0 / sum_g)
            _, inner, first = spot(r, head)
            out_buf[r, first + inner : first + inner + HEAD_SIZE] = out.astype(BF16)
            stats[r].append(base_g + jnp.log2(sum_g))
        copy_out(r, u).start()
        share = heads // nouts[r]
        if len(stats[r]) == share:
            part, _, first = spot(r, u * group)
            write_stat(
                out_buf.at[r, first : first + part_rows(share)],
                jnp.concatenate(stats[r], axis=0),
                share,
            )
            stats[r].clear()
            copy_out(r, kv + part).start()

    score(0)
    for n in range(len(jobs)):
        if n + 1 < len(jobs):
            score(n + 1)
        mix(n, *soften(n))
    for r in range(count):
        for u in range(kv + nouts[r]):
            copy_out(r, u).wait()


def attend(
    calls, nouts, shares, plan, q_parts, store, sib, kv_local, fresh=None, carry=None, deps=()
):
    count = len(calls)
    nqs = [len(parts) for parts in q_parts]
    heads = nqs[0] * q_parts[0][0].shape[1] // HEAD_SIZE
    group = heads // kv_local
    rows = part_rows(heads)
    sizes = [part_rows(heads // n) for n in nouts for _ in range(n)]
    room = max(n * part_rows(heads // n) for n in nouts)
    span = 2 * PREFIX_BLOCK_LEN + (TOK if fresh is not None else 0)
    args = [store, sib] + [x for parts in q_parts for x in parts]
    args += list(fresh or ()) + list(carry or ()) + list(deps)
    body = functools.partial(
        attend_kernel, calls, nouts, nqs, shares, group, heads, len(deps), carry is not None,
        fresh is not None,
    )
    any_spec = pl.BlockSpec(memory_space=pl.ANY)
    slots = 3
    out = pl.pallas_call(
        body,
        out_shape=[jax.ShapeDtypeStruct((n, TOK), BF16) for n in sizes],
        in_specs=[pl.BlockSpec(memory_space=pltpu.SMEM)] + [any_spec] * len(args),
        out_specs=[any_spec] * len(sizes),
        scratch_shapes=[
            pltpu.VMEM((count, TOK, heads * HEAD_SIZE), BF16),
            pltpu.VMEM((count, span, kv_local * 2 * HEAD_SIZE), BF16),
            pltpu.VMEM((count, rows, TOK), BF16),
            pltpu.VMEM((count, room, TOK), BF16),
            pltpu.VMEM((count, span, TOK), F32),
            pltpu.VMEM((slots, span, group * TOK), F32),
            pltpu.VMEM((slots, span, group * TOK), BF16),
            pltpu.SemaphoreType.DMA((count, shares, 4)),
            pltpu.SemaphoreType.DMA((count,)),
            pltpu.SemaphoreType.DMA((count, kv_local + max(nouts))),
        ],
        compiler_params=pltpu.CompilerParams(vmem_limit_bytes=VMEM_LIMIT),
        name="attend",
    )(plan, *args)
    out = list(out)
    return [[out.pop(0) for _ in range(n)] for n in nouts]


def merged_heads(heads, part_refs, emit):
    lses = [read_stat(ref, heads) for ref in part_refs]
    high = functools.reduce(jnp.maximum, lses)
    weights = [jnp.exp2(x - high) for x in lses]
    total = functools.reduce(jnp.add, weights)
    norm = 1.0 / total
    weights = [w * norm for w in weights]
    for head in range(heads):
        at = slice(head * HEAD_SIZE, (head + 1) * HEAD_SIZE)
        emit(
            head,
            functools.reduce(
                jnp.add,
                [w[head : head + 1] * ref[at, :].astype(F32) for w, ref in zip(weights, part_refs)],
            ),
        )
    return high + jnp.log2(total)


def merge_kernel(heads, count, *refs):
    refs = refs[: 2 * count] + refs[-count:]
    for i in range(count):
        a_ref, b_ref, out_ref = refs[2 * i], refs[2 * i + 1], refs[2 * count + i]

        def emit(head, value, out_ref=out_ref):
            out_ref[head * HEAD_SIZE : (head + 1) * HEAD_SIZE, :] = value.astype(BF16)

        write_stat(out_ref, merged_heads(heads, (a_ref, b_ref), emit), heads)


def merge(pairs, heads, deps=()):
    shape = pairs[0][0].shape
    spec = pl.BlockSpec(shape, lambda: (0, 0))
    args = [x for pair in pairs for x in pair]
    return pl.pallas_call(
        functools.partial(merge_kernel, heads, len(pairs)),
        out_shape=[jax.ShapeDtypeStruct(shape, BF16)] * len(pairs),
        in_specs=[spec] * len(args) + [pl.BlockSpec(memory_space=pl.ANY)] * len(deps),
        out_specs=[spec] * len(pairs),
        compiler_params=pltpu.CompilerParams(vmem_limit_bytes=VMEM_LIMIT),
        name="merge",
    )(*args, *deps)


def project_kernel(heads, counts, streams, tile, pieces, *refs):
    refs = list(refs)
    part_refs = [refs.pop(0) for _ in range(sum(counts))]
    w_ref = refs.pop(0)
    out_refs = refs[-6 - pieces + 1 : -5]
    attn_ref, parts_ref, w_buf, part_sem, w_sem = refs[-5:]
    j = pl.program_id(0)
    count = pl.num_programs(0)
    ahead = w_buf.shape[0]
    depth = w_buf.shape[1] // streams

    def weight_copies(t):
        slot = lax.rem(t, ahead)
        cols = pl.ds(pl.multiple_of(t * tile, tile), tile)
        return [
            pltpu.make_async_copy(
                w_ref.at[pl.ds(i * depth, depth), cols],
                w_buf.at[slot, pl.ds(i * depth, depth)],
                w_sem.at[slot, i],
            )
            for i in range(streams)
        ]

    @pl.when(j == 0)
    def _():
        copies = [
            pltpu.make_async_copy(ref, parts_ref.at[i], part_sem.at[i])
            for i, ref in enumerate(part_refs)
        ]
        for copy in copies:
            copy.start()
        for t in range(ahead - 1):
            for copy in weight_copies(t):
                copy.start()
        for copy in copies:
            copy.wait()

        first = 0
        for share, n in enumerate(counts):

            def emit(head, value, base=share * heads):
                cols = slice((base + head) * HEAD_SIZE, (base + head + 1) * HEAD_SIZE)
                attn_ref[:, cols] = value.T.astype(BF16)

            merged_heads(heads, [parts_ref.at[i] for i in range(first, first + n)], emit)
            first += n

    @pl.when(j + ahead - 1 < count)
    def _():
        for copy in weight_copies(j + ahead - 1):
            copy.start()

    for copy in weight_copies(j):
        copy.wait()
    got = jnp.dot(
        attn_ref[...], w_buf[lax.rem(j, ahead)], preferred_element_type=F32
    ).astype(BF16)
    for i, out_ref in enumerate(out_refs):

        @pl.when(j * pieces // count == i)
        def _(out_ref=out_ref):
            out_ref[...] = got


def project(shared, weight, pieces=1, deps=()):
    parts = [x for group in shared for x in group]
    depth, cols = weight.shape
    heads = depth // HEAD_SIZE // len(shared)
    tile = 1024
    count = cols // tile
    ahead = min(4, count)
    streams = 4
    each = count // pieces
    args = parts + [weight] + list(deps)
    in_specs = [pl.BlockSpec(memory_space=pl.ANY)] * len(args)
    return pl.pallas_call(
        functools.partial(
            project_kernel, heads, [len(group) for group in shared], streams, tile, pieces
        ),
        out_shape=[jax.ShapeDtypeStruct((TOK, cols // pieces), BF16)] * pieces,
        grid=(count,),
        in_specs=in_specs,
        out_specs=[
            pl.BlockSpec((TOK, tile), lambda j, i=i: (0, jnp.clip(j - i * each, 0, each - 1)))
            for i in range(pieces)
        ],
        scratch_shapes=[
            pltpu.VMEM((TOK, depth), BF16),
            pltpu.VMEM((len(parts),) + parts[0].shape, BF16),
            pltpu.VMEM((ahead, depth, tile), BF16),
            pltpu.SemaphoreType.DMA((len(parts),)),
            pltpu.SemaphoreType.DMA((ahead, streams)),
        ],
        compiler_params=pltpu.CompilerParams(vmem_limit_bytes=VMEM_LIMIT),
        name="project",
    )(*args)


def finish_kernel(tiles, pieces, mine_ref, rest_ref, *refs):
    j = pl.program_id(0)
    out_ref = refs[-1]
    for i, ref in enumerate(refs[:-1]):

        @pl.when(j * pieces // tiles == i)
        def _(ref=ref):
            total = ref[...].astype(F32) + mine_ref[...].astype(F32) + rest_ref[...].astype(F32)
            out_ref[...] = total.astype(BF16)


def finish(got, mine, residual):
    pieces, cols = len(got), mine.shape[1]
    tile = min(2048, cols // pieces)
    tiles = cols // tile
    each = tiles // pieces
    spec = pl.BlockSpec((TOK, tile), lambda j: (0, j))
    return pl.pallas_call(
        functools.partial(finish_kernel, tiles, pieces),
        out_shape=jax.ShapeDtypeStruct((TOK, cols), BF16),
        grid=(tiles,),
        in_specs=[spec, spec]
        + [
            pl.BlockSpec((TOK, tile), lambda j, i=i: (0, jnp.clip(j - i * each, 0, each - 1)))
            for i in range(pieces)
        ],
        out_specs=spec,
        compiler_params=pltpu.CompilerParams(vmem_limit_bytes=VMEM_LIMIT),
        name="finish",
    )(mine, residual, *got)


def shards(
    queries, new_key_values, key_value_store, o_weight, residual, hit_dev, hit_blk, prefix_len
):
    npool = lax.axis_size("pool")
    ntp = lax.axis_size("tp")
    me = lax.axis_index("pool")
    tp = lax.axis_index("tp")
    rdev = queries.shape[0] // TOK
    kv_local = key_value_store.shape[2] // (2 * HEAD_SIZE)
    nchips = npool // 2
    core = lax.rem(me, 2)
    chip = lax.div(me, 2)
    sibling = me + 1 - 2 * core
    ring = chip_ring(nchips)
    place = [ring.index(i) for i in range(nchips)]
    split_rows = ntp == rdev and rdev == 2

    swap_perm = [(p, p + 1 - 2 * (p % 2)) for p in range(npool)]
    cw_perm, ccw_perm = [], []
    for k in range(nchips):
        a, b = ring[k], ring[(k + 1) % nchips]
        for c in range(2):
            cw_perm.append((2 * a + c, 2 * b + c))
            ccw_perm.append((2 * b + c, 2 * a + c))

    starts = jnp.arange(MAXB, dtype=jnp.int32)[None, :] * PREFIX_BLOCK_LEN
    left = jnp.clip(prefix_len[:, None] - starts, 0, PREFIX_BLOCK_LEN)
    here, beside = hit_dev == me, hit_dev == sibling
    table = jnp.stack(
        [
            jnp.sum(jnp.where(at, x, 0), axis=1)
            for x, at in ((hit_blk, here), (hit_blk, beside), (left, here), (left, beside))
        ],
        axis=1,
    )
    half = nchips // 2
    steps = list(range(-half, half + 1))
    spot = jnp.asarray(place, jnp.int32)[chip]
    chips_at = jnp.asarray(ring, jnp.int32)[
        lax.rem(spot + nchips - jnp.asarray(steps, jnp.int32), nchips)
    ]
    slots = [1 - tp, tp] if split_rows else [jnp.int32(i) for i in range(rdev)]
    wanted = ((chips_at * 2 + core) * rdev)[None, :] + jnp.stack(slots)[:, None]
    plan = jnp.take(table, wanted.reshape(-1), axis=0, mode="clip").reshape(-1)
    sib = lax.ppermute(key_value_store, "pool", swap_perm)

    heads = queries.shape[1] // HEAD_SIZE
    nq = 2 if kv_local % 2 == 0 else 1
    width = heads // nq * HEAD_SIZE

    def travel(x, hops_cw, hops_ccw, held, key):
        for sign, perm, hops in ((1, cw_perm, hops_cw), (-1, ccw_perm, hops_ccw)):
            moving = x
            for t in range(1, hops + 1):
                moving = lax.ppermute(moving, "pool", perm)
                held[sign * t, key] = moving

    def reach(flip):
        if nchips % 2:
            return half, half
        return (half - 1, half) if flip else (half, half - 1)

    q_of, fresh_of = [], []
    for order, slot in enumerate(slots):
        held = {}
        fresh_of.append(lax.dynamic_slice_in_dim(new_key_values, slot * TOK, TOK, 0))
        if order == 0:
            for part in range(nq):
                q = lax.dynamic_slice(queries, (slot * TOK, part * width), (TOK, width))
                held[0, part] = q
                travel(q, *reach(part % 2), held, part)
            for part in range(nq):
                far = [held[t, part] for t in (half, -half) if (t, part) in held]
                for t in (half, -half):
                    if far:
                        held.setdefault((t, part), far[0])
            q_of.append({t: [held.get((t, part)) for part in range(nq)] for t in steps})
        else:
            q = lax.dynamic_slice_in_dim(queries, slot * TOK, TOK, 0)
            travel(q, *reach(False), held, 0)
            q_of.append({t: [x] for (t, _), x in held.items()})
            q_of[order][0] = [q[:, part * width : (part + 1) * width] for part in range(nq)]

    nouts = [1] + [nq] * (rdev - 1)

    def run(wanted, **more):
        calls = [order * len(steps) + steps.index(t) for order, t in wanted]
        return attend(
            calls, [nouts[order] for order, _ in wanted], nq, plan,
            [q_of[order][t] for order, t in wanted], key_value_store, sib, kv_local, **more,
        )

    carry = {}
    hops = dict(zip((1, -1), reach(False)))
    back = {1: ccw_perm, -1: cw_perm}
    early = {}
    own = run([(order, 0) for order in range(rdev)], fresh=fresh_of)
    ready = own[0] + [
        x for x in {id(x): x for t in steps if t for x in q_of[0][t] if x is not None}.values()
    ]

    def fill(i, deps):
        wanted = [
            (order, t) for order in range(1, rdev) for t in (i + 1, -i - 1) if t in q_of[order]
        ]
        got = run(wanted, deps=deps) if wanted else []
        early.update(zip(wanted, got))
        return [got[0][0]] if got else list(deps)

    for i in range(half):
        last_step = i == half - 1
        if last_step and i:
            ready = fill(i, ready)
        wanted = [(sign, hops[sign] - i) for sign in (1, -1) if hops[sign] > i]
        more = {"carry": [carry[sign] for sign, _ in wanted]} if i else {}
        coming = [
            q_of[order][t][0]
            for order in range(1, rdev) for t in (i + 1, -i - 1)
            if t in q_of[order] and not last_step
        ]
        got = run([(0, sign * t) for sign, t in wanted], deps=ready + coming, **more)
        for (sign, _), (x,) in zip(wanted, got):
            carry[sign] = lax.ppermute(x, "pool", back[sign])
        ready = [got[0][0]]
        if not (last_step and i):
            ready = fill(i, ready)
    parts = [[own[0][0]] + list(carry.values())]

    shares = heads // nq
    for order in range(1, rdev):
        for t in (half, -half):
            if (order, t) not in early and (order, -t) in early:
                early[order, t] = early[order, -t]
    moving = {}
    away, got = None, []
    for i in range(half):
        merged = []
        for order in range(1, rdev):
            for part in range(nq):
                counts = dict(zip((1, -1), reach(part % 2)))
                signs = [sign for sign in (1, -1) if counts[sign] > i]
                local = [early[order, sign * (counts[sign] - i)][part] for sign in signs]
                if i:
                    pairs = [(x, moving[order, part, sign]) for x, sign in zip(local, signs)]
                    local = merge(pairs, shares, deps=ready + got[: GOT.get(i, 0)] if got else ready)
                    merged.append(local[0])
                for sign, x in zip(signs, local):
                    moving[order, part, sign] = lax.ppermute(x, "pool", back[sign])
        if i == min(1, half - 1):
            away = project([parts[0]], o_weight, XPIECES if split_rows else 1, deps=merged)
            ready = [away[0]]
            if split_rows:
                got = [lax.ppermute(x, "tp", [(0, 1), (1, 0)]) for x in away]
    ends = [
        [
            [own[order][part]]
            + [moving[order, part, sign] for sign in (1, -1) if (order, part, sign) in moving]
            for part in range(nq)
        ]
        for order in range(1, rdev)
    ]

    others = [project(x, o_weight)[0] for x in ends]
    if split_rows:
        return finish(got, others[0], residual)
    mine = lax.psum_scatter(
        jnp.concatenate([*away, *others], axis=0), "tp", scatter_dimension=0, tiled=True
    )
    return (mine.astype(F32) + residual.astype(F32)).astype(BF16)


def solution(mesh):
    placed = (
        P("pool", "tp"),
        P("pool", "tp"),
        P("pool", None, "tp"),
        P("tp", None),
        P(("pool", "tp"), None),
        P(),
        P(),
        P(),
    )
    return jax.shard_map(
        shards, mesh=mesh, in_specs=placed, out_specs=P(("pool", "tp"), None), check_vma=False
    )
```

```python
import functools

import jax
import jax.numpy as jnp
from jax import lax
from jax.experimental import pallas as pl
from jax.experimental.pallas import tpu as pltpu
from jax.sharding import PartitionSpec as P

HEAD_SIZE = 128
NEW_TOKEN_COUNT = 128
PREFIX_BLOCK_LEN = 256
MAXB = 16
LOG2E = 1.4426950408889634
SCALE2 = HEAD_SIZE ** (-0.5) * LOG2E
NEG = -1e30
F32 = jnp.float32
BF16 = jnp.bfloat16
TOK = NEW_TOKEN_COUNT
VMEM_LIMIT = 64 * 1024 * 1024
CHUNK = 64
NOUT = 1
FIRST = 0


def dot_nt(a, b):
    return lax.dot_general(a, b, (((1,), (1,)), ((), ())), preferred_element_type=F32)


def chip_ring(nchips):
    if nchips % 2:
        return list(range(nchips))
    up = list(range(0, nchips, 2))
    return up + [chip + 1 for chip in reversed(up)]


def stat_rows(heads):
    return -(-3 * heads // 16) * 16


def part_rows(heads):
    return heads * HEAD_SIZE + stat_rows(heads)


def read_stat(ref, heads):
    s = ref[heads * HEAD_SIZE :, :].astype(F32)
    return s[:heads] + s[heads : 2 * heads] + s[2 * heads : 3 * heads]


def write_stat(ref, stat, heads):
    first = stat.astype(BF16).astype(F32)
    second = (stat - first).astype(BF16).astype(F32)
    third = stat - first - second
    terms = [first, second, third]
    extra = stat_rows(heads) - 3 * heads
    if extra:
        terms.append(jnp.zeros((extra, TOK), F32))
    ref[heads * HEAD_SIZE :, :] = jnp.concatenate(terms, axis=0).astype(BF16)


def attend_kernel(
    calls, nouts, nqs, shares, group, heads, ndeps, has_carry, has_fresh, plan_ref, *refs
):
    refs = list(refs)
    count = len(calls)
    kv = heads // group
    per_q = kv // shares
    pair = 2 * HEAD_SIZE
    width = group * HEAD_SIZE
    cols = group * TOK
    span = 2 * PREFIX_BLOCK_LEN + (TOK if has_fresh else 0)

    store_ref, sib_ref = refs.pop(0), refs.pop(0)
    q_refs = [[refs.pop(0) for _ in range(n)] for n in nqs]
    fresh_refs = [refs.pop(0) for _ in range(count)] if has_fresh else None
    carry_refs = [refs.pop(0) for _ in range(count)] if has_carry else None
    del refs[:ndeps]
    out_refs = [[refs.pop(0) for _ in range(n)] for n in nouts]
    q_buf, kv_buf, carry_buf, out_buf, bias_buf, s_buf, p_buf, in_sem, carry_sem, out_sem = refs

    def copies_in(r, part):
        at = slice(part * per_q * pair, (part + 1) * per_q * pair)
        cols = slice(part * per_q * width, (part + 1) * per_q * width)
        block, other = plan_ref[4 * calls[r]], plan_ref[4 * calls[r] + 1]
        q = q_refs[r][part] if len(q_refs[r]) > 1 else q_refs[r][0].at[:, cols]
        moves = [
            (q, q_buf.at[r, :, cols]),
            (store_ref.at[block, :, at], kv_buf.at[r, 0:PREFIX_BLOCK_LEN, at]),
            (sib_ref.at[other, :, at], kv_buf.at[r, PREFIX_BLOCK_LEN : 2 * PREFIX_BLOCK_LEN, at]),
        ]
        if has_fresh:
            moves.append((fresh_refs[r].at[:, at], kv_buf.at[r, 2 * PREFIX_BLOCK_LEN : span, at]))
        return [
            pltpu.make_async_copy(a, b, in_sem.at[r, part, i]) for i, (a, b) in enumerate(moves)
        ]

    def copy_carry(r):
        return pltpu.make_async_copy(carry_refs[r], carry_buf.at[r], carry_sem.at[r])

    def spot(r, head):
        share = heads // nouts[r]
        return head // share, head % share * HEAD_SIZE, head // share * part_rows(share)

    def copy_out(r, u):
        if u < kv:
            part, inner, base = spot(r, u * group)
            n = group * HEAD_SIZE
        else:
            part, share = u - kv, heads // nouts[r]
            inner, base, n = share * HEAD_SIZE, part * part_rows(share), stat_rows(share)
        return pltpu.make_async_copy(
            out_buf.at[r, base + inner : base + inner + n],
            out_refs[r][part].at[inner : inner + n],
            out_sem.at[r, u],
        )

    for r in range(count):
        for part in range(shares):
            for copy in copies_in(r, part):
                copy.start()
            if part == 0 and has_carry:
                copy_carry(r).start()

    for r in range(count):
        at = lax.broadcasted_iota(jnp.int32, (PREFIX_BLOCK_LEN, TOK), 0)
        for i in range(2):
            valid = at < plan_ref[4 * calls[r] + 2 + i]
            bias_buf[r, i * PREFIX_BLOCK_LEN : (i + 1) * PREFIX_BLOCK_LEN] = jnp.where(
                valid, 0.0, NEG
            ).astype(F32)
        if has_fresh:
            new = lax.broadcasted_iota(jnp.int32, (TOK, TOK), 0)
            tok = lax.broadcasted_iota(jnp.int32, (TOK, TOK), 1)
            bias_buf[r, 2 * PREFIX_BLOCK_LEN : span] = jnp.where(new <= tok, 0.0, NEG).astype(F32)

    jobs = [(r, u) for r in range(count) for u in range(kv)]
    slots = s_buf.shape[0]
    stats = [[] for _ in range(count)]

    def score(n):
        r, u = jobs[n]
        if u % per_q == 0:
            for copy in copies_in(r, u // per_q):
                copy.wait()
        at = u * width
        q = jnp.concatenate(
            [q_buf[r, :, at + g * HEAD_SIZE : at + (g + 1) * HEAD_SIZE] for g in range(group)],
            axis=0,
        )
        at = u * pair
        for low in range(0, span, PREFIX_BLOCK_LEN):
            rows = slice(low, min(low + PREFIX_BLOCK_LEN, span))
            s_buf[n % slots, rows] = dot_nt(kv_buf[r, rows, at : at + HEAD_SIZE], q)

    def soften(n):
        r, u = jobs[n]
        slot = n % slots

        def piece(at):
            bias = bias_buf[r, at : at + CHUNK]
            return s_buf[slot, at : at + CHUNK] + jnp.concatenate([bias] * group, axis=1)

        top = None
        for at in range(0, span, CHUNK):
            high = jnp.max(piece(at).reshape(CHUNK // 8, 8, cols), axis=0)
            top = high if top is None else jnp.maximum(top, high)
        top = jnp.max(top, axis=0, keepdims=True)
        total = None
        for at in range(0, span, CHUNK):
            ex = jnp.exp2((piece(at) - top) * SCALE2)
            p_buf[slot, at : at + CHUNK] = ex.astype(BF16)
            part = jnp.sum(ex.reshape(CHUNK // 8, 8, cols), axis=0)
            total = part if total is None else total + part
        return top * SCALE2, jnp.sum(total, axis=0, keepdims=True)

    def mix(n, base, total):
        r, u = jobs[n]
        mixed = lax.dot_general(
            kv_buf[r, :, u * pair + HEAD_SIZE : (u + 1) * pair],
            p_buf[n % slots],
            (((0,), (0,)), ((), ())),
            preferred_element_type=F32,
        )
        if has_carry and u == 0:
            copy_carry(r).wait()
        if has_carry:
            stat_in = read_stat(carry_buf.at[r], heads)
        for g in range(group):
            head = u * group + g
            at = slice(head * HEAD_SIZE, (head + 1) * HEAD_SIZE)
            part = slice(g * TOK, (g + 1) * TOK)
            o_g, sum_g, base_g = mixed[:, part], total[:, part], base[:, part]
            if has_carry:
                lse_c = stat_in[head : head + 1]
                high = jnp.maximum(base_g, lse_c)
                w_c = jnp.exp2(lse_c - high)
                w_g = jnp.exp2(base_g - high)
                sum_g = w_c + sum_g * w_g
                norm = 1.0 / sum_g
                out = carry_buf[r, at].astype(F32) * (w_c * norm) + o_g * (w_g * norm)
                base_g = high
            else:
                out = o_g * (1.0 / sum_g)
            _, inner, first = spot(r, head)
            out_buf[r, first + inner : first + inner + HEAD_SIZE] = out.astype(BF16)
            stats[r].append(base_g + jnp.log2(sum_g))
        copy_out(r, u).start()
        share = heads // nouts[r]
        if len(stats[r]) == share:
            part, _, first = spot(r, u * group)
            write_stat(
                out_buf.at[r, first : first + part_rows(share)],
                jnp.concatenate(stats[r], axis=0),
                share,
            )
            stats[r].clear()
            copy_out(r, kv + part).start()

    score(0)
    for n in range(len(jobs)):
        if n + 1 < len(jobs):
            score(n + 1)
        mix(n, *soften(n))
    for r in range(count):
        for u in range(kv + nouts[r]):
            copy_out(r, u).wait()


def attend(
    calls, nouts, shares, plan, q_parts, store, sib, kv_local, fresh=None, carry=None, deps=()
):
    count = len(calls)
    nqs = [len(parts) for parts in q_parts]
    heads = nqs[0] * q_parts[0][0].shape[1] // HEAD_SIZE
    group = heads // kv_local
    rows = part_rows(heads)
    sizes = [part_rows(heads // n) for n in nouts for _ in range(n)]
    room = max(n * part_rows(heads // n) for n in nouts)
    span = 2 * PREFIX_BLOCK_LEN + (TOK if fresh is not None else 0)
    args = [store, sib] + [x for parts in q_parts for x in parts]
    args += list(fresh or ()) + list(carry or ()) + list(deps)
    body = functools.partial(
        attend_kernel, calls, nouts, nqs, shares, group, heads, len(deps), carry is not None,
        fresh is not None,
    )
    any_spec = pl.BlockSpec(memory_space=pl.ANY)
    slots = 3
    out = pl.pallas_call(
        body,
        out_shape=[jax.ShapeDtypeStruct((n, TOK), BF16) for n in sizes],
        in_specs=[pl.BlockSpec(memory_space=pltpu.SMEM)] + [any_spec] * len(args),
        out_specs=[any_spec] * len(sizes),
        scratch_shapes=[
            pltpu.VMEM((count, TOK, heads * HEAD_SIZE), BF16),
            pltpu.VMEM((count, span, kv_local * 2 * HEAD_SIZE), BF16),
            pltpu.VMEM((count, rows, TOK), BF16),
            pltpu.VMEM((count, room, TOK), BF16),
            pltpu.VMEM((count, span, TOK), F32),
            pltpu.VMEM((slots, span, group * TOK), F32),
            pltpu.VMEM((slots, span, group * TOK), BF16),
            pltpu.SemaphoreType.DMA((count, shares, 4)),
            pltpu.SemaphoreType.DMA((count,)),
            pltpu.SemaphoreType.DMA((count, kv_local + max(nouts))),
        ],
        compiler_params=pltpu.CompilerParams(vmem_limit_bytes=VMEM_LIMIT),
        name="attend",
    )(plan, *args)
    out = list(out)
    return [[out.pop(0) for _ in range(n)] for n in nouts]


def merged_heads(heads, part_refs, emit):
    lses = [read_stat(ref, heads) for ref in part_refs]
    high = functools.reduce(jnp.maximum, lses)
    weights = [jnp.exp2(x - high) for x in lses]
    total = functools.reduce(jnp.add, weights)
    norm = 1.0 / total
    weights = [w * norm for w in weights]
    for head in range(heads):
        at = slice(head * HEAD_SIZE, (head + 1) * HEAD_SIZE)
        emit(
            head,
            functools.reduce(
                jnp.add,
                [w[head : head + 1] * ref[at, :].astype(F32) for w, ref in zip(weights, part_refs)],
            ),
        )
    return high + jnp.log2(total)


def merge_kernel(heads, count, *refs):
    refs = refs[: 2 * count] + refs[-count:]
    for i in range(count):
        a_ref, b_ref, out_ref = refs[2 * i], refs[2 * i + 1], refs[2 * count + i]

        def emit(head, value, out_ref=out_ref):
            out_ref[head * HEAD_SIZE : (head + 1) * HEAD_SIZE, :] = value.astype(BF16)

        write_stat(out_ref, merged_heads(heads, (a_ref, b_ref), emit), heads)


def merge(pairs, heads, deps=()):
    shape = pairs[0][0].shape
    spec = pl.BlockSpec(shape, lambda: (0, 0))
    args = [x for pair in pairs for x in pair]
    return pl.pallas_call(
        functools.partial(merge_kernel, heads, len(pairs)),
        out_shape=[jax.ShapeDtypeStruct(shape, BF16)] * len(pairs),
        in_specs=[spec] * len(args) + [pl.BlockSpec(memory_space=pl.ANY)] * len(deps),
        out_specs=[spec] * len(pairs),
        compiler_params=pltpu.CompilerParams(vmem_limit_bytes=VMEM_LIMIT),
        name="merge",
    )(*args, *deps)


def project_kernel(heads, counts, spans, streams, tile, *refs):
    refs = list(refs)
    part_refs = [refs.pop(0) for _ in range(sum(counts))]
    w_ref = refs.pop(0)
    add_refs = [refs.pop(0) for _ in spans]
    out_ref, attn_ref, parts_ref, w_buf, part_sem, w_sem = refs[-6:]
    j = pl.program_id(0)
    count = pl.num_programs(0)
    ahead = w_buf.shape[0]
    depth = w_buf.shape[1] // streams

    def weight_copies(t):
        slot = lax.rem(t, ahead)
        cols = pl.ds(pl.multiple_of(t * tile, tile), tile)
        return [
            pltpu.make_async_copy(
                w_ref.at[pl.ds(i * depth, depth), cols],
                w_buf.at[slot, pl.ds(i * depth, depth)],
                w_sem.at[slot, i],
            )
            for i in range(streams)
        ]

    @pl.when(j == 0)
    def _():
        copies = [
            pltpu.make_async_copy(ref, parts_ref.at[i], part_sem.at[i])
            for i, ref in enumerate(part_refs)
        ]
        for copy in copies:
            copy.start()
        for t in range(ahead - 1):
            for copy in weight_copies(t):
                copy.start()
        for copy in copies:
            copy.wait()

        first = 0
        for share, n in enumerate(counts):

            def emit(head, value, base=share * heads):
                cols = slice((base + head) * HEAD_SIZE, (base + head + 1) * HEAD_SIZE)
                attn_ref[:, cols] = value.T.astype(BF16)

            merged_heads(heads, [parts_ref.at[i] for i in range(first, first + n)], emit)
            first += n

    @pl.when(j + ahead - 1 < count)
    def _():
        for copy in weight_copies(j + ahead - 1):
            copy.start()

    for copy in weight_copies(j):
        copy.wait()
    got = jnp.dot(attn_ref[...], w_buf[lax.rem(j, ahead)], preferred_element_type=F32)
    got = got.astype(BF16)
    if spans:
        total = got.astype(F32)
        for ref, (low, high) in zip(add_refs, spans):
            here = (j >= low) & (j < high)
            total = total + jnp.where(here, ref[...].astype(F32), 0.0)
        got = total.astype(BF16)
    out_ref[...] = got


def project(shared, weight, adds=(), deps=()):
    parts = [x for group in shared for x in group]
    depth, cols = weight.shape
    heads = depth // HEAD_SIZE // len(shared)
    tile = 1024
    count = cols // tile
    ahead = min(4, count)
    streams = 4
    in_specs = [pl.BlockSpec(memory_space=pl.ANY)] * (len(parts) + 1)
    args = parts + [weight]
    spans = []
    for x, first in adds:
        low, n = first // tile, x.shape[1] // tile
        spans.append((low, low + n))
        in_specs.append(
            pl.BlockSpec((TOK, tile), lambda j, low=low, n=n: (0, jnp.clip(j - low, 0, n - 1)))
        )
        args.append(x)
    in_specs += [pl.BlockSpec(memory_space=pl.ANY)] * len(deps)
    args += deps
    return pl.pallas_call(
        functools.partial(
            project_kernel, heads, [len(group) for group in shared], spans, streams, tile
        ),
        out_shape=jax.ShapeDtypeStruct((TOK, cols), BF16),
        grid=(count,),
        in_specs=in_specs,
        out_specs=pl.BlockSpec((TOK, tile), lambda j: (0, j)),
        scratch_shapes=[
            pltpu.VMEM((TOK, depth), BF16),
            pltpu.VMEM((len(parts),) + parts[0].shape, BF16),
            pltpu.VMEM((ahead, depth, tile), BF16),
            pltpu.SemaphoreType.DMA((len(parts),)),
            pltpu.SemaphoreType.DMA((ahead, streams)),
        ],
        compiler_params=pltpu.CompilerParams(vmem_limit_bytes=VMEM_LIMIT),
        name="project",
    )(*args)


def shards(
    queries, new_key_values, key_value_store, o_weight, residual, hit_dev, hit_blk, prefix_len
):
    npool = lax.axis_size("pool")
    ntp = lax.axis_size("tp")
    me = lax.axis_index("pool")
    tp = lax.axis_index("tp")
    rdev = queries.shape[0] // TOK
    kv_local = key_value_store.shape[2] // (2 * HEAD_SIZE)
    nchips = npool // 2
    core = lax.rem(me, 2)
    chip = lax.div(me, 2)
    sibling = me + 1 - 2 * core
    ring = chip_ring(nchips)
    place = [ring.index(i) for i in range(nchips)]
    split_rows = ntp == rdev and rdev == 2

    swap_perm = [(p, p + 1 - 2 * (p % 2)) for p in range(npool)]
    cw_perm, ccw_perm = [], []
    for k in range(nchips):
        a, b = ring[k], ring[(k + 1) % nchips]
        for c in range(2):
            cw_perm.append((2 * a + c, 2 * b + c))
            ccw_perm.append((2 * b + c, 2 * a + c))

    starts = jnp.arange(MAXB, dtype=jnp.int32)[None, :] * PREFIX_BLOCK_LEN
    left = jnp.clip(prefix_len[:, None] - starts, 0, PREFIX_BLOCK_LEN)
    here, beside = hit_dev == me, hit_dev == sibling
    table = jnp.stack(
        [
            jnp.sum(jnp.where(at, x, 0), axis=1)
            for x, at in ((hit_blk, here), (hit_blk, beside), (left, here), (left, beside))
        ],
        axis=1,
    )
    half = nchips // 2
    steps = list(range(-half, half + 1))
    spot = jnp.asarray(place, jnp.int32)[chip]
    chips_at = jnp.asarray(ring, jnp.int32)[
        lax.rem(spot + nchips - jnp.asarray(steps, jnp.int32), nchips)
    ]
    slots = [1 - tp, tp] if split_rows else [jnp.int32(i) for i in range(rdev)]
    wanted = ((chips_at * 2 + core) * rdev)[None, :] + jnp.stack(slots)[:, None]
    plan = jnp.take(table, wanted.reshape(-1), axis=0, mode="clip").reshape(-1)
    sib = lax.ppermute(key_value_store, "pool", swap_perm)

    heads = queries.shape[1] // HEAD_SIZE
    nq = 2 if kv_local % 2 == 0 else 1
    width = heads // nq * HEAD_SIZE

    def travel(x, hops_cw, hops_ccw, held, key):
        for sign, perm, hops in ((1, cw_perm, hops_cw), (-1, ccw_perm, hops_ccw)):
            moving = x
            for t in range(1, hops + 1):
                moving = lax.ppermute(moving, "pool", perm)
                held[sign * t, key] = moving

    def reach(flip):
        if nchips % 2:
            return half, half
        return (half - 1, half) if flip else (half, half - 1)

    q_of, fresh_of = [], []
    for order, slot in enumerate(slots):
        held = {}
        fresh_of.append(lax.dynamic_slice_in_dim(new_key_values, slot * TOK, TOK, 0))
        if order == 0:
            for part in range(nq):
                q = lax.dynamic_slice(queries, (slot * TOK, part * width), (TOK, width))
                held[0, part] = q
                travel(q, *reach(part % 2), held, part)
            for part in range(nq):
                far = [held[t, part] for t in (half, -half) if (t, part) in held]
                for t in (half, -half):
                    if far:
                        held.setdefault((t, part), far[0])
            q_of.append({t: [held.get((t, part)) for part in range(nq)] for t in steps})
        else:
            q = lax.dynamic_slice_in_dim(queries, slot * TOK, TOK, 0)
            travel(q, *reach(False), held, 0)
            q_of.append({t: [x] for (t, _), x in held.items()})
            q_of[order][0] = [q[:, part * width : (part + 1) * width] for part in range(nq)]

    nouts = [1] + [NOUT] * (rdev - 1)

    def run(wanted, **more):
        calls = [order * len(steps) + steps.index(t) for order, t in wanted]
        return attend(
            calls, [nouts[order] for order, _ in wanted], nq, plan,
            [q_of[order][t] for order, t in wanted], key_value_store, sib, kv_local, **more,
        )

    carry = {}
    hops = dict(zip((1, -1), reach(False)))
    back = {1: ccw_perm, -1: cw_perm}
    early = {}
    own = run([(order, 0) for order in range(rdev)], fresh=fresh_of)
    ready = own[0] + list(
        {id(x): x for t in steps if t for x in q_of[0][t] if x is not None}.values()
    )
    for i in range(half):
        for sign in (1, -1):
            t = hops[sign] - i
            if t > 0:
                more = {"carry": [carry[sign]]} if i else {}
                ((x,),) = run([(0, sign * t)], deps=ready, **more)
                carry[sign] = lax.ppermute(x, "pool", back[sign])
                ready = [x]
        wanted = [
            (order, t) for order in range(1, rdev) for t in (i + 1, -i - 1) if t in q_of[order]
        ]
        if wanted:
            got = run(wanted, deps=ready)
            early.update(zip(wanted, got))
            ready = [got[0][0]]
    parts = [[own[0][0]] + list(carry.values())]

    shares = heads // NOUT
    for order in range(1, rdev):
        for t in (half, -half):
            if (order, t) not in early and (order, -t) in early:
                early[order, t] = early[order, -t]
    moving = {}
    away = None
    for i in range(half):
        merged = []
        for order in range(1, rdev):
            for part in range(NOUT):
                counts = dict(zip((1, -1), reach(part % 2)))
                for sign in (1, -1):
                    if counts[sign] <= i:
                        continue
                    x = early[order, sign * (counts[sign] - i)][part]
                    if i:
                        (x,) = merge([(x, moving[order, part, sign])], shares, deps=ready)
                        merged.append(x)
                    moving[order, part, sign] = lax.ppermute(x, "pool", back[sign])
        if i == min(FIRST, half - 1):
            away = project([parts[0]], o_weight, deps=merged)
            ready = [away]
    ends = [
        [
            [own[order][part]]
            + [moving[order, part, sign] for sign in (1, -1) if (order, part, sign) in moving]
            for part in range(NOUT)
        ]
        for order in range(1, rdev)
    ]
    if split_rows:
        got = lax.ppermute(away, "tp", [(0, 1), (1, 0)])
        return project(ends[0], o_weight, [(got, 0), (residual, 0)])
    rows = [away] + [project(x, o_weight) for x in ends]
    mine = lax.psum_scatter(
        jnp.concatenate(rows, axis=0), "tp", scatter_dimension=0, tiled=True
    )
    return (mine.astype(F32) + residual.astype(F32)).astype(BF16)


def solution(mesh):
    placed = (
        P("pool", "tp"),
        P("pool", "tp"),
        P("pool", None, "tp"),
        P("tp", None),
        P(("pool", "tp"), None),
        P(),
        P(),
        P(),
    )
    return jax.shard_map(
        shards, mesh=mesh, in_specs=placed, out_specs=P(("pool", "tp"), None), check_vma=False
    )
```

```python
import functools

import jax
import jax.numpy as jnp
from jax import lax
from jax.experimental import pallas as pl
from jax.experimental.pallas import tpu as pltpu
from jax.sharding import PartitionSpec as P

HEAD_SIZE = 128
NEW_TOKEN_COUNT = 128
PREFIX_BLOCK_LEN = 256
MAXB = 16
LOG2E = 1.4426950408889634
SCALE2 = HEAD_SIZE ** (-0.5) * LOG2E
NEG = -1e30
F32 = jnp.float32
BF16 = jnp.bfloat16
TOK = NEW_TOKEN_COUNT
VMEM_LIMIT = 64 * 1024 * 1024
CHUNK = 64
NOUT = 1
FIRST = 0


def dot_nt(a, b):
    return lax.dot_general(a, b, (((1,), (1,)), ((), ())), preferred_element_type=F32)


def chip_ring(nchips):
    if nchips % 2:
        return list(range(nchips))
    up = list(range(0, nchips, 2))
    return up + [chip + 1 for chip in reversed(up)]


def stat_rows(heads):
    return -(-3 * heads // 16) * 16


def part_rows(heads):
    return heads * HEAD_SIZE + stat_rows(heads)


def read_stat(ref, heads):
    s = ref[heads * HEAD_SIZE :, :].astype(F32)
    return s[:heads] + s[heads : 2 * heads] + s[2 * heads : 3 * heads]


def write_stat(ref, stat, heads):
    first = stat.astype(BF16).astype(F32)
    second = (stat - first).astype(BF16).astype(F32)
    third = stat - first - second
    terms = [first, second, third]
    extra = stat_rows(heads) - 3 * heads
    if extra:
        terms.append(jnp.zeros((extra, TOK), F32))
    ref[heads * HEAD_SIZE :, :] = jnp.concatenate(terms, axis=0).astype(BF16)


def attend_kernel(
    calls, nouts, nqs, shares, group, heads, ndeps, has_carry, has_fresh, plan_ref, *refs
):
    refs = list(refs)
    count = len(calls)
    kv = heads // group
    per_q = kv // shares
    pair = 2 * HEAD_SIZE
    width = group * HEAD_SIZE
    cols = group * TOK
    span = 2 * PREFIX_BLOCK_LEN + (TOK if has_fresh else 0)

    store_ref, sib_ref = refs.pop(0), refs.pop(0)
    q_refs = [[refs.pop(0) for _ in range(n)] for n in nqs]
    fresh_refs = [refs.pop(0) for _ in range(count)] if has_fresh else None
    carry_refs = [refs.pop(0) for _ in range(count)] if has_carry else None
    del refs[:ndeps]
    out_refs = [[refs.pop(0) for _ in range(n)] for n in nouts]
    q_buf, kv_buf, carry_buf, out_buf, bias_buf, s_buf, p_buf, in_sem, carry_sem, out_sem = refs

    def copies_in(r, part):
        at = slice(part * per_q * pair, (part + 1) * per_q * pair)
        cols = slice(part * per_q * width, (part + 1) * per_q * width)
        block, other = plan_ref[4 * calls[r]], plan_ref[4 * calls[r] + 1]
        q = q_refs[r][part] if len(q_refs[r]) > 1 else q_refs[r][0].at[:, cols]
        moves = [
            (q, q_buf.at[r, :, cols]),
            (store_ref.at[block, :, at], kv_buf.at[r, 0:PREFIX_BLOCK_LEN, at]),
            (sib_ref.at[other, :, at], kv_buf.at[r, PREFIX_BLOCK_LEN : 2 * PREFIX_BLOCK_LEN, at]),
        ]
        if has_fresh:
            moves.append((fresh_refs[r].at[:, at], kv_buf.at[r, 2 * PREFIX_BLOCK_LEN : span, at]))
        return [
            pltpu.make_async_copy(a, b, in_sem.at[r, part, i]) for i, (a, b) in enumerate(moves)
        ]

    def copy_carry(r):
        return pltpu.make_async_copy(carry_refs[r], carry_buf.at[r], carry_sem.at[r])

    def spot(r, head):
        share = heads // nouts[r]
        return head // share, head % share * HEAD_SIZE, head // share * part_rows(share)

    def copy_out(r, u):
        if u < kv:
            part, inner, base = spot(r, u * group)
            n = group * HEAD_SIZE
        else:
            part, share = u - kv, heads // nouts[r]
            inner, base, n = share * HEAD_SIZE, part * part_rows(share), stat_rows(share)
        return pltpu.make_async_copy(
            out_buf.at[r, base + inner : base + inner + n],
            out_refs[r][part].at[inner : inner + n],
            out_sem.at[r, u],
        )

    for r in range(count):
        for part in range(shares):
            for copy in copies_in(r, part):
                copy.start()
            if part == 0 and has_carry:
                copy_carry(r).start()

    for r in range(count):
        at = lax.broadcasted_iota(jnp.int32, (PREFIX_BLOCK_LEN, TOK), 0)
        for i in range(2):
            valid = at < plan_ref[4 * calls[r] + 2 + i]
            bias_buf[r, i * PREFIX_BLOCK_LEN : (i + 1) * PREFIX_BLOCK_LEN] = jnp.where(
                valid, 0.0, NEG
            ).astype(F32)
        if has_fresh:
            new = lax.broadcasted_iota(jnp.int32, (TOK, TOK), 0)
            tok = lax.broadcasted_iota(jnp.int32, (TOK, TOK), 1)
            bias_buf[r, 2 * PREFIX_BLOCK_LEN : span] = jnp.where(new <= tok, 0.0, NEG).astype(F32)

    jobs = [(r, u) for r in range(count) for u in range(kv)]
    slots = s_buf.shape[0]
    stats = [[] for _ in range(count)]

    def score(n):
        r, u = jobs[n]
        if u % per_q == 0:
            for copy in copies_in(r, u // per_q):
                copy.wait()
        at = u * width
        q = jnp.concatenate(
            [q_buf[r, :, at + g * HEAD_SIZE : at + (g + 1) * HEAD_SIZE] for g in range(group)],
            axis=0,
        )
        at = u * pair
        for low in range(0, span, PREFIX_BLOCK_LEN):
            rows = slice(low, min(low + PREFIX_BLOCK_LEN, span))
            s_buf[n % slots, rows] = dot_nt(kv_buf[r, rows, at : at + HEAD_SIZE], q)

    def soften(n):
        r, u = jobs[n]
        slot = n % slots

        def piece(at):
            bias = bias_buf[r, at : at + CHUNK]
            return s_buf[slot, at : at + CHUNK] + jnp.concatenate([bias] * group, axis=1)

        top = None
        for at in range(0, span, CHUNK):
            high = jnp.max(piece(at).reshape(CHUNK // 8, 8, cols), axis=0)
            top = high if top is None else jnp.maximum(top, high)
        top = jnp.max(top, axis=0, keepdims=True)
        total = None
        for at in range(0, span, CHUNK):
            ex = jnp.exp2((piece(at) - top) * SCALE2)
            p_buf[slot, at : at + CHUNK] = ex.astype(BF16)
            part = jnp.sum(ex.reshape(CHUNK // 8, 8, cols), axis=0)
            total = part if total is None else total + part
        return top * SCALE2, jnp.sum(total, axis=0, keepdims=True)

    def mix(n, base, total):
        r, u = jobs[n]
        mixed = lax.dot_general(
            kv_buf[r, :, u * pair + HEAD_SIZE : (u + 1) * pair],
            p_buf[n % slots],
            (((0,), (0,)), ((), ())),
            preferred_element_type=F32,
        )
        if has_carry and u == 0:
            copy_carry(r).wait()
        if has_carry:
            stat_in = read_stat(carry_buf.at[r], heads)
        for g in range(group):
            head = u * group + g
            at = slice(head * HEAD_SIZE, (head + 1) * HEAD_SIZE)
            part = slice(g * TOK, (g + 1) * TOK)
            o_g, sum_g, base_g = mixed[:, part], total[:, part], base[:, part]
            if has_carry:
                lse_c = stat_in[head : head + 1]
                high = jnp.maximum(base_g, lse_c)
                w_c = jnp.exp2(lse_c - high)
                w_g = jnp.exp2(base_g - high)
                sum_g = w_c + sum_g * w_g
                norm = 1.0 / sum_g
                out = carry_buf[r, at].astype(F32) * (w_c * norm) + o_g * (w_g * norm)
                base_g = high
            else:
                out = o_g * (1.0 / sum_g)
            _, inner, first = spot(r, head)
            out_buf[r, first + inner : first + inner + HEAD_SIZE] = out.astype(BF16)
            stats[r].append(base_g + jnp.log2(sum_g))
        copy_out(r, u).start()
        share = heads // nouts[r]
        if len(stats[r]) == share:
            part, _, first = spot(r, u * group)
            write_stat(
                out_buf.at[r, first : first + part_rows(share)],
                jnp.concatenate(stats[r], axis=0),
                share,
            )
            stats[r].clear()
            copy_out(r, kv + part).start()

    score(0)
    for n in range(len(jobs)):
        if n + 1 < len(jobs):
            score(n + 1)
        mix(n, *soften(n))
    for r in range(count):
        for u in range(kv + nouts[r]):
            copy_out(r, u).wait()


def attend(
    calls, nouts, shares, plan, q_parts, store, sib, kv_local, fresh=None, carry=None, deps=()
):
    count = len(calls)
    nqs = [len(parts) for parts in q_parts]
    heads = nqs[0] * q_parts[0][0].shape[1] // HEAD_SIZE
    group = heads // kv_local
    rows = part_rows(heads)
    sizes = [part_rows(heads // n) for n in nouts for _ in range(n)]
    room = max(n * part_rows(heads // n) for n in nouts)
    span = 2 * PREFIX_BLOCK_LEN + (TOK if fresh is not None else 0)
    args = [store, sib] + [x for parts in q_parts for x in parts]
    args += list(fresh or ()) + list(carry or ()) + list(deps)
    body = functools.partial(
        attend_kernel, calls, nouts, nqs, shares, group, heads, len(deps), carry is not None,
        fresh is not None,
    )
    any_spec = pl.BlockSpec(memory_space=pl.ANY)
    slots = 3
    out = pl.pallas_call(
        body,
        out_shape=[jax.ShapeDtypeStruct((n, TOK), BF16) for n in sizes],
        in_specs=[pl.BlockSpec(memory_space=pltpu.SMEM)] + [any_spec] * len(args),
        out_specs=[any_spec] * len(sizes),
        scratch_shapes=[
            pltpu.VMEM((count, TOK, heads * HEAD_SIZE), BF16),
            pltpu.VMEM((count, span, kv_local * 2 * HEAD_SIZE), BF16),
            pltpu.VMEM((count, rows, TOK), BF16),
            pltpu.VMEM((count, room, TOK), BF16),
            pltpu.VMEM((count, span, TOK), F32),
            pltpu.VMEM((slots, span, group * TOK), F32),
            pltpu.VMEM((slots, span, group * TOK), BF16),
            pltpu.SemaphoreType.DMA((count, shares, 4)),
            pltpu.SemaphoreType.DMA((count,)),
            pltpu.SemaphoreType.DMA((count, kv_local + max(nouts))),
        ],
        compiler_params=pltpu.CompilerParams(vmem_limit_bytes=VMEM_LIMIT),
        name="attend",
    )(plan, *args)
    out = list(out)
    return [[out.pop(0) for _ in range(n)] for n in nouts]


def merged_heads(heads, part_refs, emit):
    lses = [read_stat(ref, heads) for ref in part_refs]
    high = functools.reduce(jnp.maximum, lses)
    weights = [jnp.exp2(x - high) for x in lses]
    total = functools.reduce(jnp.add, weights)
    norm = 1.0 / total
    weights = [w * norm for w in weights]
    for head in range(heads):
        at = slice(head * HEAD_SIZE, (head + 1) * HEAD_SIZE)
        emit(
            head,
            functools.reduce(
                jnp.add,
                [w[head : head + 1] * ref[at, :].astype(F32) for w, ref in zip(weights, part_refs)],
            ),
        )
    return high + jnp.log2(total)


def merge_kernel(heads, count, *refs):
    refs = refs[: 2 * count] + refs[-count:]
    for i in range(count):
        a_ref, b_ref, out_ref = refs[2 * i], refs[2 * i + 1], refs[2 * count + i]

        def emit(head, value, out_ref=out_ref):
            out_ref[head * HEAD_SIZE : (head + 1) * HEAD_SIZE, :] = value.astype(BF16)

        write_stat(out_ref, merged_heads(heads, (a_ref, b_ref), emit), heads)


def merge(pairs, heads, deps=()):
    shape = pairs[0][0].shape
    spec = pl.BlockSpec(shape, lambda: (0, 0))
    args = [x for pair in pairs for x in pair]
    return pl.pallas_call(
        functools.partial(merge_kernel, heads, len(pairs)),
        out_shape=[jax.ShapeDtypeStruct(shape, BF16)] * len(pairs),
        in_specs=[spec] * len(args) + [pl.BlockSpec(memory_space=pl.ANY)] * len(deps),
        out_specs=[spec] * len(pairs),
        compiler_params=pltpu.CompilerParams(vmem_limit_bytes=VMEM_LIMIT),
        name="merge",
    )(*args, *deps)


def project_kernel(heads, counts, spans, streams, tile, *refs):
    refs = list(refs)
    part_refs = [refs.pop(0) for _ in range(sum(counts))]
    w_ref = refs.pop(0)
    add_refs = [refs.pop(0) for _ in spans]
    out_ref, attn_ref, parts_ref, w_buf, part_sem, w_sem = refs[-6:]
    j = pl.program_id(0)
    count = pl.num_programs(0)
    ahead = w_buf.shape[0]
    depth = w_buf.shape[1] // streams

    def weight_copies(t):
        slot = lax.rem(t, ahead)
        cols = pl.ds(pl.multiple_of(t * tile, tile), tile)
        return [
            pltpu.make_async_copy(
                w_ref.at[pl.ds(i * depth, depth), cols],
                w_buf.at[slot, pl.ds(i * depth, depth)],
                w_sem.at[slot, i],
            )
            for i in range(streams)
        ]

    @pl.when(j == 0)
    def _():
        copies = [
            pltpu.make_async_copy(ref, parts_ref.at[i], part_sem.at[i])
            for i, ref in enumerate(part_refs)
        ]
        for copy in copies:
            copy.start()
        for t in range(ahead - 1):
            for copy in weight_copies(t):
                copy.start()
        for copy in copies:
            copy.wait()

        first = 0
        for share, n in enumerate(counts):

            def emit(head, value, base=share * heads):
                cols = slice((base + head) * HEAD_SIZE, (base + head + 1) * HEAD_SIZE)
                attn_ref[:, cols] = value.T.astype(BF16)

            merged_heads(heads, [parts_ref.at[i] for i in range(first, first + n)], emit)
            first += n

    @pl.when(j + ahead - 1 < count)
    def _():
        for copy in weight_copies(j + ahead - 1):
            copy.start()

    for copy in weight_copies(j):
        copy.wait()
    got = jnp.dot(attn_ref[...], w_buf[lax.rem(j, ahead)], preferred_element_type=F32)
    got = got.astype(BF16)
    if spans:
        total = got.astype(F32)
        for ref, (low, high) in zip(add_refs, spans):
            here = (j >= low) & (j < high)
            total = total + jnp.where(here, ref[...].astype(F32), 0.0)
        got = total.astype(BF16)
    out_ref[...] = got


def project(shared, weight, adds=(), deps=()):
    parts = [x for group in shared for x in group]
    depth, cols = weight.shape
    heads = depth // HEAD_SIZE // len(shared)
    tile = 1024
    count = cols // tile
    ahead = min(4, count)
    streams = 4
    in_specs = [pl.BlockSpec(memory_space=pl.ANY)] * (len(parts) + 1)
    args = parts + [weight]
    spans = []
    for x, first in adds:
        low, n = first // tile, x.shape[1] // tile
        spans.append((low, low + n))
        in_specs.append(
            pl.BlockSpec((TOK, tile), lambda j, low=low, n=n: (0, jnp.clip(j - low, 0, n - 1)))
        )
        args.append(x)
    in_specs += [pl.BlockSpec(memory_space=pl.ANY)] * len(deps)
    args += deps
    return pl.pallas_call(
        functools.partial(
            project_kernel, heads, [len(group) for group in shared], spans, streams, tile
        ),
        out_shape=jax.ShapeDtypeStruct((TOK, cols), BF16),
        grid=(count,),
        in_specs=in_specs,
        out_specs=pl.BlockSpec((TOK, tile), lambda j: (0, j)),
        scratch_shapes=[
            pltpu.VMEM((TOK, depth), BF16),
            pltpu.VMEM((len(parts),) + parts[0].shape, BF16),
            pltpu.VMEM((ahead, depth, tile), BF16),
            pltpu.SemaphoreType.DMA((len(parts),)),
            pltpu.SemaphoreType.DMA((ahead, streams)),
        ],
        compiler_params=pltpu.CompilerParams(vmem_limit_bytes=VMEM_LIMIT),
        name="project",
    )(*args)


def shards(
    queries, new_key_values, key_value_store, o_weight, residual, hit_dev, hit_blk, prefix_len
):
    npool = lax.axis_size("pool")
    ntp = lax.axis_size("tp")
    me = lax.axis_index("pool")
    tp = lax.axis_index("tp")
    rdev = queries.shape[0] // TOK
    kv_local = key_value_store.shape[2] // (2 * HEAD_SIZE)
    nchips = npool // 2
    core = lax.rem(me, 2)
    chip = lax.div(me, 2)
    sibling = me + 1 - 2 * core
    ring = chip_ring(nchips)
    place = [ring.index(i) for i in range(nchips)]
    split_rows = ntp == rdev and rdev == 2

    swap_perm = [(p, p + 1 - 2 * (p % 2)) for p in range(npool)]
    cw_perm, ccw_perm = [], []
    for k in range(nchips):
        a, b = ring[k], ring[(k + 1) % nchips]
        for c in range(2):
            cw_perm.append((2 * a + c, 2 * b + c))
            ccw_perm.append((2 * b + c, 2 * a + c))

    starts = jnp.arange(MAXB, dtype=jnp.int32)[None, :] * PREFIX_BLOCK_LEN
    left = jnp.clip(prefix_len[:, None] - starts, 0, PREFIX_BLOCK_LEN)
    here, beside = hit_dev == me, hit_dev == sibling
    table = jnp.stack(
        [
            jnp.sum(jnp.where(at, x, 0), axis=1)
            for x, at in ((hit_blk, here), (hit_blk, beside), (left, here), (left, beside))
        ],
        axis=1,
    )
    half = nchips // 2
    steps = list(range(-half, half + 1))
    spot = jnp.asarray(place, jnp.int32)[chip]
    chips_at = jnp.asarray(ring, jnp.int32)[
        lax.rem(spot + nchips - jnp.asarray(steps, jnp.int32), nchips)
    ]
    slots = [1 - tp, tp] if split_rows else [jnp.int32(i) for i in range(rdev)]
    wanted = ((chips_at * 2 + core) * rdev)[None, :] + jnp.stack(slots)[:, None]
    plan = jnp.take(table, wanted.reshape(-1), axis=0, mode="clip").reshape(-1)
    sib = lax.ppermute(key_value_store, "pool", swap_perm)

    heads = queries.shape[1] // HEAD_SIZE
    nq = 2 if kv_local % 2 == 0 else 1
    width = heads // nq * HEAD_SIZE

    def travel(x, hops_cw, hops_ccw, held, key):
        for sign, perm, hops in ((1, cw_perm, hops_cw), (-1, ccw_perm, hops_ccw)):
            moving = x
            for t in range(1, hops + 1):
                moving = lax.ppermute(moving, "pool", perm)
                held[sign * t, key] = moving

    def reach(flip):
        if nchips % 2:
            return half, half
        return (half - 1, half) if flip else (half, half - 1)

    q_of, fresh_of = [], []
    for order, slot in enumerate(slots):
        held = {}
        fresh_of.append(lax.dynamic_slice_in_dim(new_key_values, slot * TOK, TOK, 0))
        if order == 0:
            for part in range(nq):
                q = lax.dynamic_slice(queries, (slot * TOK, part * width), (TOK, width))
                held[0, part] = q
                travel(q, *reach(part % 2), held, part)
            for part in range(nq):
                far = [held[t, part] for t in (half, -half) if (t, part) in held]
                for t in (half, -half):
                    if far:
                        held.setdefault((t, part), far[0])
            q_of.append({t: [held.get((t, part)) for part in range(nq)] for t in steps})
        else:
            q = lax.dynamic_slice_in_dim(queries, slot * TOK, TOK, 0)
            travel(q, *reach(False), held, 0)
            q_of.append({t: [x] for (t, _), x in held.items()})
            q_of[order][0] = [q[:, part * width : (part + 1) * width] for part in range(nq)]

    nouts = [1] + [NOUT] * (rdev - 1)

    def run(wanted, **more):
        calls = [order * len(steps) + steps.index(t) for order, t in wanted]
        return attend(
            calls, [nouts[order] for order, _ in wanted], nq, plan,
            [q_of[order][t] for order, t in wanted], key_value_store, sib, kv_local, **more,
        )

    carry = {}
    hops = dict(zip((1, -1), reach(False)))
    back = {1: ccw_perm, -1: cw_perm}
    early = {}
    ready = list({id(x): x for t in steps if t for x in q_of[0][t] if x is not None}.values())
    for i in range(half):
        for sign in (1, -1):
            t = hops[sign] - i
            if t > 0:
                more = {"carry": [carry[sign]]} if i else {}
                ((x,),) = run([(0, sign * t)], deps=ready, **more)
                carry[sign] = lax.ppermute(x, "pool", back[sign])
                ready = [x]
        if i == 0:
            own = run([(order, 0) for order in range(rdev)], fresh=fresh_of, deps=ready)
            ready = own[0]
        reached = [i] if i < half - 1 else [i, half]
        wanted = [
            (order, t) for order in range(1, rdev) for r in reached if r for t in (r, -r)
            if t in q_of[order]
        ]
        if wanted:
            got = run(wanted, deps=ready)
            early.update(zip(wanted, got))
            ready = [got[0][0]]
    parts = [[own[0][0]] + list(carry.values())]

    shares = heads // NOUT
    for order in range(1, rdev):
        for t in (half, -half):
            if (order, t) not in early and (order, -t) in early:
                early[order, t] = early[order, -t]
    moving = {}
    away = None
    for i in range(half):
        merged = []
        for order in range(1, rdev):
            for part in range(NOUT):
                counts = dict(zip((1, -1), reach(part % 2)))
                for sign in (1, -1):
                    if counts[sign] <= i:
                        continue
                    x = early[order, sign * (counts[sign] - i)][part]
                    if i:
                        (x,) = merge([(x, moving[order, part, sign])], shares, deps=ready)
                        merged.append(x)
                    moving[order, part, sign] = lax.ppermute(x, "pool", back[sign])
        if i == min(FIRST, half - 1):
            away = project([parts[0]], o_weight, deps=merged)
            ready = [away]
    ends = [
        [
            [own[order][part]]
            + [moving[order, part, sign] for sign in (1, -1) if (order, part, sign) in moving]
            for part in range(NOUT)
        ]
        for order in range(1, rdev)
    ]
    if split_rows:
        got = lax.ppermute(away, "tp", [(0, 1), (1, 0)])
        return project(ends[0], o_weight, [(got, 0), (residual, 0)])
    rows = [away] + [project(x, o_weight) for x in ends]
    mine = lax.psum_scatter(
        jnp.concatenate(rows, axis=0), "tp", scatter_dimension=0, tiled=True
    )
    return (mine.astype(F32) + residual.astype(F32)).astype(BF16)


def solution(mesh):
    placed = (
        P("pool", "tp"),
        P("pool", "tp"),
        P("pool", None, "tp"),
        P("tp", None),
        P(("pool", "tp"), None),
        P(),
        P(),
        P(),
    )
    return jax.shard_map(
        shards, mesh=mesh, in_specs=placed, out_specs=P(("pool", "tp"), None), check_vma=False
    )
```

```python
import functools

import jax
import jax.numpy as jnp
from jax import lax
from jax.experimental import pallas as pl
from jax.experimental.pallas import tpu as pltpu
from jax.sharding import PartitionSpec as P

HEAD_SIZE = 128
NEW_TOKEN_COUNT = 128
PREFIX_BLOCK_LEN = 256
MAXB = 16
LOG2E = 1.4426950408889634
SCALE2 = HEAD_SIZE ** (-0.5) * LOG2E
NEG = -1e30
F32 = jnp.float32
BF16 = jnp.bfloat16
TOK = NEW_TOKEN_COUNT
VMEM_LIMIT = 64 * 1024 * 1024
CHUNK = 64
NOUT = 1
AFTER_FIRST = ((2, -1), (3, 1))


def dot_nt(a, b):
    return lax.dot_general(a, b, (((1,), (1,)), ((), ())), preferred_element_type=F32)


def chip_ring(nchips):
    if nchips % 2:
        return list(range(nchips))
    up = list(range(0, nchips, 2))
    return up + [chip + 1 for chip in reversed(up)]


def stat_rows(heads):
    return -(-3 * heads // 16) * 16


def part_rows(heads):
    return heads * HEAD_SIZE + stat_rows(heads)


def read_stat(ref, heads):
    s = ref[heads * HEAD_SIZE :, :].astype(F32)
    return s[:heads] + s[heads : 2 * heads] + s[2 * heads : 3 * heads]


def write_stat(ref, stat, heads):
    first = stat.astype(BF16).astype(F32)
    second = (stat - first).astype(BF16).astype(F32)
    third = stat - first - second
    terms = [first, second, third]
    extra = stat_rows(heads) - 3 * heads
    if extra:
        terms.append(jnp.zeros((extra, TOK), F32))
    ref[heads * HEAD_SIZE :, :] = jnp.concatenate(terms, axis=0).astype(BF16)


def attend_kernel(
    calls, nouts, nqs, shares, group, heads, ndeps, has_carry, has_fresh, plan_ref, *refs
):
    refs = list(refs)
    count = len(calls)
    kv = heads // group
    per_q = kv // shares
    pair = 2 * HEAD_SIZE
    width = group * HEAD_SIZE
    cols = group * TOK
    span = 2 * PREFIX_BLOCK_LEN + (TOK if has_fresh else 0)

    store_ref, sib_ref = refs.pop(0), refs.pop(0)
    q_refs = [[refs.pop(0) for _ in range(n)] for n in nqs]
    fresh_refs = [refs.pop(0) for _ in range(count)] if has_fresh else None
    carry_refs = [refs.pop(0) for _ in range(count)] if has_carry else None
    del refs[:ndeps]
    out_refs = [[refs.pop(0) for _ in range(n)] for n in nouts]
    q_buf, kv_buf, carry_buf, out_buf, bias_buf, s_buf, p_buf, in_sem, carry_sem, out_sem = refs

    def copies_in(r, part):
        at = slice(part * per_q * pair, (part + 1) * per_q * pair)
        cols = slice(part * per_q * width, (part + 1) * per_q * width)
        block, other = plan_ref[4 * calls[r]], plan_ref[4 * calls[r] + 1]
        q = q_refs[r][part] if len(q_refs[r]) > 1 else q_refs[r][0].at[:, cols]
        moves = [
            (q, q_buf.at[r, :, cols]),
            (store_ref.at[block, :, at], kv_buf.at[r, 0:PREFIX_BLOCK_LEN, at]),
            (sib_ref.at[other, :, at], kv_buf.at[r, PREFIX_BLOCK_LEN : 2 * PREFIX_BLOCK_LEN, at]),
        ]
        if has_fresh:
            moves.append((fresh_refs[r].at[:, at], kv_buf.at[r, 2 * PREFIX_BLOCK_LEN : span, at]))
        return [
            pltpu.make_async_copy(a, b, in_sem.at[r, part, i]) for i, (a, b) in enumerate(moves)
        ]

    def copy_carry(r):
        return pltpu.make_async_copy(carry_refs[r], carry_buf.at[r], carry_sem.at[r])

    def spot(r, head):
        share = heads // nouts[r]
        return head // share, head % share * HEAD_SIZE, head // share * part_rows(share)

    def copy_out(r, u):
        if u < kv:
            part, inner, base = spot(r, u * group)
            n = group * HEAD_SIZE
        else:
            part, share = u - kv, heads // nouts[r]
            inner, base, n = share * HEAD_SIZE, part * part_rows(share), stat_rows(share)
        return pltpu.make_async_copy(
            out_buf.at[r, base + inner : base + inner + n],
            out_refs[r][part].at[inner : inner + n],
            out_sem.at[r, u],
        )

    for r in range(count):
        for part in range(shares):
            for copy in copies_in(r, part):
                copy.start()
            if part == 0 and has_carry:
                copy_carry(r).start()

    for r in range(count):
        at = lax.broadcasted_iota(jnp.int32, (PREFIX_BLOCK_LEN, TOK), 0)
        for i in range(2):
            valid = at < plan_ref[4 * calls[r] + 2 + i]
            bias_buf[r, i * PREFIX_BLOCK_LEN : (i + 1) * PREFIX_BLOCK_LEN] = jnp.where(
                valid, 0.0, NEG
            ).astype(F32)
        if has_fresh:
            new = lax.broadcasted_iota(jnp.int32, (TOK, TOK), 0)
            tok = lax.broadcasted_iota(jnp.int32, (TOK, TOK), 1)
            bias_buf[r, 2 * PREFIX_BLOCK_LEN : span] = jnp.where(new <= tok, 0.0, NEG).astype(F32)

    jobs = [(r, u) for r in range(count) for u in range(kv)]
    slots = s_buf.shape[0]
    stats = [[] for _ in range(count)]

    def score(n):
        r, u = jobs[n]
        if u % per_q == 0:
            for copy in copies_in(r, u // per_q):
                copy.wait()
        at = u * width
        q = jnp.concatenate(
            [q_buf[r, :, at + g * HEAD_SIZE : at + (g + 1) * HEAD_SIZE] for g in range(group)],
            axis=0,
        )
        at = u * pair
        for low in range(0, span, PREFIX_BLOCK_LEN):
            rows = slice(low, min(low + PREFIX_BLOCK_LEN, span))
            s_buf[n % slots, rows] = dot_nt(kv_buf[r, rows, at : at + HEAD_SIZE], q)

    def soften(n):
        r, u = jobs[n]
        slot = n % slots

        def piece(at):
            bias = bias_buf[r, at : at + CHUNK]
            return s_buf[slot, at : at + CHUNK] + jnp.concatenate([bias] * group, axis=1)

        top = None
        for at in range(0, span, CHUNK):
            high = jnp.max(piece(at).reshape(CHUNK // 8, 8, cols), axis=0)
            top = high if top is None else jnp.maximum(top, high)
        top = jnp.max(top, axis=0, keepdims=True)
        total = None
        for at in range(0, span, CHUNK):
            ex = jnp.exp2((piece(at) - top) * SCALE2)
            p_buf[slot, at : at + CHUNK] = ex.astype(BF16)
            part = jnp.sum(ex.reshape(CHUNK // 8, 8, cols), axis=0)
            total = part if total is None else total + part
        return top * SCALE2, jnp.sum(total, axis=0, keepdims=True)

    def mix(n, base, total):
        r, u = jobs[n]
        mixed = lax.dot_general(
            kv_buf[r, :, u * pair + HEAD_SIZE : (u + 1) * pair],
            p_buf[n % slots],
            (((0,), (0,)), ((), ())),
            preferred_element_type=F32,
        )
        if has_carry and u == 0:
            copy_carry(r).wait()
        if has_carry:
            stat_in = read_stat(carry_buf.at[r], heads)
        for g in range(group):
            head = u * group + g
            at = slice(head * HEAD_SIZE, (head + 1) * HEAD_SIZE)
            part = slice(g * TOK, (g + 1) * TOK)
            o_g, sum_g, base_g = mixed[:, part], total[:, part], base[:, part]
            if has_carry:
                lse_c = stat_in[head : head + 1]
                high = jnp.maximum(base_g, lse_c)
                w_c = jnp.exp2(lse_c - high)
                w_g = jnp.exp2(base_g - high)
                sum_g = w_c + sum_g * w_g
                norm = 1.0 / sum_g
                out = carry_buf[r, at].astype(F32) * (w_c * norm) + o_g * (w_g * norm)
                base_g = high
            else:
                out = o_g * (1.0 / sum_g)
            _, inner, first = spot(r, head)
            out_buf[r, first + inner : first + inner + HEAD_SIZE] = out.astype(BF16)
            stats[r].append(base_g + jnp.log2(sum_g))
        copy_out(r, u).start()
        share = heads // nouts[r]
        if len(stats[r]) == share:
            part, _, first = spot(r, u * group)
            write_stat(
                out_buf.at[r, first : first + part_rows(share)],
                jnp.concatenate(stats[r], axis=0),
                share,
            )
            stats[r].clear()
            copy_out(r, kv + part).start()

    score(0)
    for n in range(len(jobs)):
        if n + 1 < len(jobs):
            score(n + 1)
        mix(n, *soften(n))
    for r in range(count):
        for u in range(kv + nouts[r]):
            copy_out(r, u).wait()


def attend(
    calls, nouts, shares, plan, q_parts, store, sib, kv_local, fresh=None, carry=None, deps=()
):
    count = len(calls)
    nqs = [len(parts) for parts in q_parts]
    heads = nqs[0] * q_parts[0][0].shape[1] // HEAD_SIZE
    group = heads // kv_local
    rows = part_rows(heads)
    sizes = [part_rows(heads // n) for n in nouts for _ in range(n)]
    room = max(n * part_rows(heads // n) for n in nouts)
    span = 2 * PREFIX_BLOCK_LEN + (TOK if fresh is not None else 0)
    args = [store, sib] + [x for parts in q_parts for x in parts]
    args += list(fresh or ()) + list(carry or ()) + list(deps)
    body = functools.partial(
        attend_kernel, calls, nouts, nqs, shares, group, heads, len(deps), carry is not None,
        fresh is not None,
    )
    any_spec = pl.BlockSpec(memory_space=pl.ANY)
    slots = 3
    out = pl.pallas_call(
        body,
        out_shape=[jax.ShapeDtypeStruct((n, TOK), BF16) for n in sizes],
        in_specs=[pl.BlockSpec(memory_space=pltpu.SMEM)] + [any_spec] * len(args),
        out_specs=[any_spec] * len(sizes),
        scratch_shapes=[
            pltpu.VMEM((count, TOK, heads * HEAD_SIZE), BF16),
            pltpu.VMEM((count, span, kv_local * 2 * HEAD_SIZE), BF16),
            pltpu.VMEM((count, rows, TOK), BF16),
            pltpu.VMEM((count, room, TOK), BF16),
            pltpu.VMEM((count, span, TOK), F32),
            pltpu.VMEM((slots, span, group * TOK), F32),
            pltpu.VMEM((slots, span, group * TOK), BF16),
            pltpu.SemaphoreType.DMA((count, shares, 4)),
            pltpu.SemaphoreType.DMA((count,)),
            pltpu.SemaphoreType.DMA((count, kv_local + max(nouts))),
        ],
        compiler_params=pltpu.CompilerParams(vmem_limit_bytes=VMEM_LIMIT),
        name="attend",
    )(plan, *args)
    out = list(out)
    return [[out.pop(0) for _ in range(n)] for n in nouts]


def merged_heads(heads, part_refs, emit):
    lses = [read_stat(ref, heads) for ref in part_refs]
    high = functools.reduce(jnp.maximum, lses)
    weights = [jnp.exp2(x - high) for x in lses]
    total = functools.reduce(jnp.add, weights)
    norm = 1.0 / total
    weights = [w * norm for w in weights]
    for head in range(heads):
        at = slice(head * HEAD_SIZE, (head + 1) * HEAD_SIZE)
        emit(
            head,
            functools.reduce(
                jnp.add,
                [w[head : head + 1] * ref[at, :].astype(F32) for w, ref in zip(weights, part_refs)],
            ),
        )
    return high + jnp.log2(total)


def merge_kernel(heads, count, *refs):
    refs = refs[: 2 * count] + refs[-count:]
    for i in range(count):
        a_ref, b_ref, out_ref = refs[2 * i], refs[2 * i + 1], refs[2 * count + i]

        def emit(head, value, out_ref=out_ref):
            out_ref[head * HEAD_SIZE : (head + 1) * HEAD_SIZE, :] = value.astype(BF16)

        write_stat(out_ref, merged_heads(heads, (a_ref, b_ref), emit), heads)


def merge(pairs, heads, deps=()):
    shape = pairs[0][0].shape
    spec = pl.BlockSpec(shape, lambda: (0, 0))
    args = [x for pair in pairs for x in pair]
    return pl.pallas_call(
        functools.partial(merge_kernel, heads, len(pairs)),
        out_shape=[jax.ShapeDtypeStruct(shape, BF16)] * len(pairs),
        in_specs=[spec] * len(args) + [pl.BlockSpec(memory_space=pl.ANY)] * len(deps),
        out_specs=[spec] * len(pairs),
        compiler_params=pltpu.CompilerParams(vmem_limit_bytes=VMEM_LIMIT),
        name="merge",
    )(*args, *deps)


def project_kernel(heads, counts, spans, streams, tile, col0, *refs):
    refs = list(refs)
    part_refs = [refs.pop(0) for _ in range(sum(counts))]
    w_ref = refs.pop(0)
    add_refs = [refs.pop(0) for _ in spans]
    out_ref, attn_ref, parts_ref, w_buf, part_sem, w_sem = refs[-6:]
    j = pl.program_id(0)
    count = pl.num_programs(0)
    ahead = w_buf.shape[0]
    depth = w_buf.shape[1] // streams

    def weight_copies(t):
        slot = lax.rem(t, ahead)
        cols = pl.ds(pl.multiple_of(col0 + t * tile, tile), tile)
        return [
            pltpu.make_async_copy(
                w_ref.at[pl.ds(i * depth, depth), cols],
                w_buf.at[slot, pl.ds(i * depth, depth)],
                w_sem.at[slot, i],
            )
            for i in range(streams)
        ]

    @pl.when(j == 0)
    def _():
        copies = [
            pltpu.make_async_copy(ref, parts_ref.at[i], part_sem.at[i])
            for i, ref in enumerate(part_refs)
        ]
        for copy in copies:
            copy.start()
        for t in range(ahead - 1):
            for copy in weight_copies(t):
                copy.start()
        for copy in copies:
            copy.wait()

        first = 0
        for share, n in enumerate(counts):

            def emit(head, value, base=share * heads):
                cols = slice((base + head) * HEAD_SIZE, (base + head + 1) * HEAD_SIZE)
                attn_ref[:, cols] = value.T.astype(BF16)

            merged_heads(heads, [parts_ref.at[i] for i in range(first, first + n)], emit)
            first += n

    @pl.when(j + ahead - 1 < count)
    def _():
        for copy in weight_copies(j + ahead - 1):
            copy.start()

    for copy in weight_copies(j):
        copy.wait()
    got = jnp.dot(attn_ref[...], w_buf[lax.rem(j, ahead)], preferred_element_type=F32)
    got = got.astype(BF16)
    if spans:
        total = got.astype(F32)
        for ref, (low, high) in zip(add_refs, spans):
            here = (j >= low) & (j < high)
            total = total + jnp.where(here, ref[...].astype(F32), 0.0)
        got = total.astype(BF16)
    out_ref[...] = got


def project(shared, weight, adds=(), deps=(), col0=0, cols=None):
    parts = [x for group in shared for x in group]
    depth = weight.shape[0]
    cols = weight.shape[1] if cols is None else cols
    heads = depth // HEAD_SIZE // len(shared)
    tile = 1024
    count = cols // tile
    ahead = min(4, count)
    streams = 4
    in_specs = [pl.BlockSpec(memory_space=pl.ANY)] * (len(parts) + 1)
    args = parts + [weight]
    spans = []
    for x, first in adds:
        low, n = first // tile, x.shape[1] // tile
        spans.append((low, low + n))
        in_specs.append(
            pl.BlockSpec((TOK, tile), lambda j, low=low, n=n: (0, jnp.clip(j - low, 0, n - 1)))
        )
        args.append(x)
    in_specs += [pl.BlockSpec(memory_space=pl.ANY)] * len(deps)
    args += deps
    return pl.pallas_call(
        functools.partial(
            project_kernel, heads, [len(group) for group in shared], spans, streams, tile, col0
        ),
        out_shape=jax.ShapeDtypeStruct((TOK, cols), BF16),
        grid=(count,),
        in_specs=in_specs,
        out_specs=pl.BlockSpec((TOK, tile), lambda j: (0, j)),
        scratch_shapes=[
            pltpu.VMEM((TOK, depth), BF16),
            pltpu.VMEM((len(parts),) + parts[0].shape, BF16),
            pltpu.VMEM((ahead, depth, tile), BF16),
            pltpu.SemaphoreType.DMA((len(parts),)),
            pltpu.SemaphoreType.DMA((ahead, streams)),
        ],
        compiler_params=pltpu.CompilerParams(vmem_limit_bytes=VMEM_LIMIT),
        name="project",
    )(*args)


def shards(
    queries, new_key_values, key_value_store, o_weight, residual, hit_dev, hit_blk, prefix_len
):
    npool = lax.axis_size("pool")
    ntp = lax.axis_size("tp")
    me = lax.axis_index("pool")
    tp = lax.axis_index("tp")
    rdev = queries.shape[0] // TOK
    kv_local = key_value_store.shape[2] // (2 * HEAD_SIZE)
    nchips = npool // 2
    core = lax.rem(me, 2)
    chip = lax.div(me, 2)
    sibling = me + 1 - 2 * core
    ring = chip_ring(nchips)
    place = [ring.index(i) for i in range(nchips)]
    split_rows = ntp == rdev and rdev == 2

    swap_perm = [(p, p + 1 - 2 * (p % 2)) for p in range(npool)]
    cw_perm, ccw_perm = [], []
    for k in range(nchips):
        a, b = ring[k], ring[(k + 1) % nchips]
        for c in range(2):
            cw_perm.append((2 * a + c, 2 * b + c))
            ccw_perm.append((2 * b + c, 2 * a + c))

    starts = jnp.arange(MAXB, dtype=jnp.int32)[None, :] * PREFIX_BLOCK_LEN
    left = jnp.clip(prefix_len[:, None] - starts, 0, PREFIX_BLOCK_LEN)
    here, beside = hit_dev == me, hit_dev == sibling
    table = jnp.stack(
        [
            jnp.sum(jnp.where(at, x, 0), axis=1)
            for x, at in ((hit_blk, here), (hit_blk, beside), (left, here), (left, beside))
        ],
        axis=1,
    )
    half = nchips // 2
    steps = list(range(-half, half + 1))
    spot = jnp.asarray(place, jnp.int32)[chip]
    chips_at = jnp.asarray(ring, jnp.int32)[
        lax.rem(spot + nchips - jnp.asarray(steps, jnp.int32), nchips)
    ]
    slots = [1 - tp, tp] if split_rows else [jnp.int32(i) for i in range(rdev)]
    wanted = ((chips_at * 2 + core) * rdev)[None, :] + jnp.stack(slots)[:, None]
    plan = jnp.take(table, wanted.reshape(-1), axis=0, mode="clip").reshape(-1)
    sib = lax.ppermute(key_value_store, "pool", swap_perm)

    heads = queries.shape[1] // HEAD_SIZE
    nq = 2 if kv_local % 2 == 0 else 1
    width = heads // nq * HEAD_SIZE

    def travel(x, hops_cw, hops_ccw, held, key):
        for sign, perm, hops in ((1, cw_perm, hops_cw), (-1, ccw_perm, hops_ccw)):
            moving = x
            for t in range(1, hops + 1):
                moving = lax.ppermute(moving, "pool", perm)
                held[sign * t, key] = moving

    def reach(flip):
        if nchips % 2:
            return half, half
        return (half - 1, half) if flip else (half, half - 1)

    q_of, fresh_of = [], []
    for order, slot in enumerate(slots):
        held = {}
        fresh_of.append(lax.dynamic_slice_in_dim(new_key_values, slot * TOK, TOK, 0))
        if order == 0:
            for part in range(nq):
                q = lax.dynamic_slice(queries, (slot * TOK, part * width), (TOK, width))
                held[0, part] = q
                travel(q, *reach(part % 2), held, part)
            for part in range(nq):
                far = [held[t, part] for t in (half, -half) if (t, part) in held]
                for t in (half, -half):
                    if far:
                        held.setdefault((t, part), far[0])
            q_of.append({t: [held.get((t, part)) for part in range(nq)] for t in steps})
        else:
            q = lax.dynamic_slice_in_dim(queries, slot * TOK, TOK, 0)
            travel(q, *reach(False), held, 0)
            q_of.append({t: [x] for (t, _), x in held.items()})
            q_of[order][0] = [q[:, part * width : (part + 1) * width] for part in range(nq)]

    nouts = [1] + [NOUT] * (rdev - 1)

    def run(wanted, **more):
        calls = [order * len(steps) + steps.index(t) for order, t in wanted]
        return attend(
            calls, [nouts[order] for order, _ in wanted], nq, plan,
            [q_of[order][t] for order, t in wanted], key_value_store, sib, kv_local, **more,
        )

    carry = {}
    hops = dict(zip((1, -1), reach(False)))
    back = {1: ccw_perm, -1: cw_perm}
    early = {}
    ready = list({id(x): x for t in steps if t for x in q_of[0][t] if x is not None}.values())
    for i in range(half):
        for sign in (1, -1):
            t = hops[sign] - i
            if t > 0:
                more = {"carry": [carry[sign]]} if i else {}
                ((x,),) = run([(0, sign * t)], deps=ready, **more)
                carry[sign] = lax.ppermute(x, "pool", back[sign])
                ready = [x]
        if i == 0:
            own = run([(order, 0) for order in range(rdev)], fresh=fresh_of, deps=ready)
            ready = own[0]
        reached = [i] if i < half - 1 else [i, half]
        wanted = [
            (order, t) for order in range(1, rdev) for r in reached if r for t in (r, -r)
            if t in q_of[order]
        ]
        if wanted:
            got = run(wanted, deps=ready)
            early.update(zip(wanted, got))
            ready = [got[0][0]]
    parts = [[own[0][0]] + list(carry.values())]

    shares = heads // NOUT
    for order in range(1, rdev):
        for t in (half, -half):
            if (order, t) not in early and (order, -t) in early:
                early[order, t] = early[order, -t]
    moving = {}
    away = []
    model = o_weight.shape[1]

    got = []

    def project_half(deps):
        at = len(away) * (model // 2)
        away.append(project([parts[0]], o_weight, deps=deps, col0=at, cols=model // 2))
        if split_rows:
            got.append((lax.ppermute(away[-1], "tp", [(0, 1), (1, 0)]), at))
        return [away[-1]]

    ready = project_half(ready)
    for i in range(half):
        for order in range(1, rdev):
            for part in range(NOUT):
                counts = dict(zip((1, -1), reach(part % 2)))
                for sign in (1, -1):
                    if counts[sign] <= i:
                        continue
                    x = early[order, sign * (counts[sign] - i)][part]
                    if i:
                        wait = [y for y, _ in got[:1]] if (i, sign) in AFTER_FIRST else []
                        (x,) = merge([(x, moving[order, part, sign])], shares, deps=ready + wait)
                        if len(away) == 1:
                            ready = project_half([x])
                    moving[order, part, sign] = lax.ppermute(x, "pool", back[sign])
    if len(away) == 1:
        project_half(ready)
    ends = [
        [
            [own[order][part]]
            + [moving[order, part, sign] for sign in (1, -1) if (order, part, sign) in moving]
            for part in range(NOUT)
        ]
        for order in range(1, rdev)
    ]
    if split_rows:
        return project(ends[0], o_weight, got + [(residual, 0)])
    rows = [jnp.concatenate(away, axis=1)] + [project(x, o_weight) for x in ends]
    mine = lax.psum_scatter(
        jnp.concatenate(rows, axis=0), "tp", scatter_dimension=0, tiled=True
    )
    return (mine.astype(F32) + residual.astype(F32)).astype(BF16)


def solution(mesh):
    placed = (
        P("pool", "tp"),
        P("pool", "tp"),
        P("pool", None, "tp"),
        P("tp", None),
        P(("pool", "tp"), None),
        P(),
        P(),
        P(),
    )
    return jax.shard_map(
        shards, mesh=mesh, in_specs=placed, out_specs=P(("pool", "tp"), None), check_vma=False
    )
```

```python
import functools

import jax
import jax.numpy as jnp
from jax import lax
from jax.experimental import pallas as pl
from jax.experimental.pallas import tpu as pltpu
from jax.sharding import PartitionSpec as P

HEAD_SIZE = 128
NEW_TOKEN_COUNT = 128
PREFIX_BLOCK_LEN = 256
MAXB = 16
LOG2E = 1.4426950408889634
SCALE2 = HEAD_SIZE ** (-0.5) * LOG2E
NEG = -1e30
F32 = jnp.float32
BF16 = jnp.bfloat16
TOK = NEW_TOKEN_COUNT
VMEM_LIMIT = 64 * 1024 * 1024
CHUNK = 64
NOUT = 1
AFTER_FIRST = ((2, -1), (3, 1))


def dot_nt(a, b):
    return lax.dot_general(a, b, (((1,), (1,)), ((), ())), preferred_element_type=F32)


def chip_ring(nchips):
    if nchips % 2:
        return list(range(nchips))
    up = list(range(0, nchips, 2))
    return up + [chip + 1 for chip in reversed(up)]


def stat_rows(heads):
    return -(-3 * heads // 16) * 16


def part_rows(heads):
    return heads * HEAD_SIZE + stat_rows(heads)


def read_stat(ref, heads):
    s = ref[heads * HEAD_SIZE :, :].astype(F32)
    return s[:heads] + s[heads : 2 * heads] + s[2 * heads : 3 * heads]


def write_stat(ref, stat, heads):
    first = stat.astype(BF16).astype(F32)
    second = (stat - first).astype(BF16).astype(F32)
    third = stat - first - second
    terms = [first, second, third]
    extra = stat_rows(heads) - 3 * heads
    if extra:
        terms.append(jnp.zeros((extra, TOK), F32))
    ref[heads * HEAD_SIZE :, :] = jnp.concatenate(terms, axis=0).astype(BF16)


def take_kernel(slot_ref, x_ref, *refs):
    refs[-1][...] = x_ref[...]


def take_rows(x, slot, deps):
    cols = x.shape[1]
    return pl.pallas_call(
        take_kernel,
        out_shape=jax.ShapeDtypeStruct((TOK, cols), x.dtype),
        grid_spec=pltpu.PrefetchScalarGridSpec(
            num_scalar_prefetch=1,
            grid=(1,),
            in_specs=[pl.BlockSpec((TOK, cols), lambda i, slot: (slot[0], 0))]
            + [pl.BlockSpec(memory_space=pl.ANY)] * len(deps),
            out_specs=pl.BlockSpec((TOK, cols), lambda i, slot: (0, 0)),
        ),
        compiler_params=pltpu.CompilerParams(vmem_limit_bytes=VMEM_LIMIT),
        name="take_rows",
    )(jnp.asarray(slot, jnp.int32).reshape(1), x, *deps)


def attend_kernel(
    calls, nouts, nqs, shares, group, heads, ndeps, has_carry, has_fresh, plan_ref, *refs
):
    refs = list(refs)
    count = len(calls)
    kv = heads // group
    per_q = kv // shares
    pair = 2 * HEAD_SIZE
    width = group * HEAD_SIZE
    cols = group * TOK
    span = 2 * PREFIX_BLOCK_LEN + (TOK if has_fresh else 0)

    store_ref, sib_ref = refs.pop(0), refs.pop(0)
    q_refs = [[refs.pop(0) for _ in range(n)] for n in nqs]
    fresh_refs = [refs.pop(0) for _ in range(count)] if has_fresh else None
    carry_refs = [refs.pop(0) for _ in range(count)] if has_carry else None
    del refs[:ndeps]
    out_refs = [[refs.pop(0) for _ in range(n)] for n in nouts]
    q_buf, kv_buf, carry_buf, out_buf, bias_buf, s_buf, p_buf, in_sem, carry_sem, out_sem = refs

    def copies_in(r, part):
        at = slice(part * per_q * pair, (part + 1) * per_q * pair)
        cols = slice(part * per_q * width, (part + 1) * per_q * width)
        block, other = plan_ref[4 * calls[r]], plan_ref[4 * calls[r] + 1]
        q = q_refs[r][part] if len(q_refs[r]) > 1 else q_refs[r][0].at[:, cols]
        moves = [
            (q, q_buf.at[r, :, cols]),
            (store_ref.at[block, :, at], kv_buf.at[r, 0:PREFIX_BLOCK_LEN, at]),
            (sib_ref.at[other, :, at], kv_buf.at[r, PREFIX_BLOCK_LEN : 2 * PREFIX_BLOCK_LEN, at]),
        ]
        if has_fresh:
            moves.append((fresh_refs[r].at[:, at], kv_buf.at[r, 2 * PREFIX_BLOCK_LEN : span, at]))
        return [
            pltpu.make_async_copy(a, b, in_sem.at[r, part, i]) for i, (a, b) in enumerate(moves)
        ]

    def copy_carry(r):
        return pltpu.make_async_copy(carry_refs[r], carry_buf.at[r], carry_sem.at[r])

    def spot(r, head):
        share = heads // nouts[r]
        return head // share, head % share * HEAD_SIZE, head // share * part_rows(share)

    def copy_out(r, u):
        if u < kv:
            part, inner, base = spot(r, u * group)
            n = group * HEAD_SIZE
        else:
            part, share = u - kv, heads // nouts[r]
            inner, base, n = share * HEAD_SIZE, part * part_rows(share), stat_rows(share)
        return pltpu.make_async_copy(
            out_buf.at[r, base + inner : base + inner + n],
            out_refs[r][part].at[inner : inner + n],
            out_sem.at[r, u],
        )

    for r in range(count):
        for part in range(shares):
            for copy in copies_in(r, part):
                copy.start()
            if part == 0 and has_carry:
                copy_carry(r).start()

    for r in range(count):
        at = lax.broadcasted_iota(jnp.int32, (PREFIX_BLOCK_LEN, TOK), 0)
        for i in range(2):
            valid = at < plan_ref[4 * calls[r] + 2 + i]
            bias_buf[r, i * PREFIX_BLOCK_LEN : (i + 1) * PREFIX_BLOCK_LEN] = jnp.where(
                valid, 0.0, NEG
            ).astype(F32)
        if has_fresh:
            new = lax.broadcasted_iota(jnp.int32, (TOK, TOK), 0)
            tok = lax.broadcasted_iota(jnp.int32, (TOK, TOK), 1)
            bias_buf[r, 2 * PREFIX_BLOCK_LEN : span] = jnp.where(new <= tok, 0.0, NEG).astype(F32)

    jobs = [(r, u) for r in range(count) for u in range(kv)]
    slots = s_buf.shape[0]
    stats = [[] for _ in range(count)]

    def score(n):
        r, u = jobs[n]
        if u % per_q == 0:
            for copy in copies_in(r, u // per_q):
                copy.wait()
        at = u * width
        q = jnp.concatenate(
            [q_buf[r, :, at + g * HEAD_SIZE : at + (g + 1) * HEAD_SIZE] for g in range(group)],
            axis=0,
        )
        at = u * pair
        for low in range(0, span, PREFIX_BLOCK_LEN):
            rows = slice(low, min(low + PREFIX_BLOCK_LEN, span))
            s_buf[n % slots, rows] = dot_nt(kv_buf[r, rows, at : at + HEAD_SIZE], q)

    def soften(n):
        r, u = jobs[n]
        slot = n % slots

        def piece(at):
            bias = bias_buf[r, at : at + CHUNK]
            return s_buf[slot, at : at + CHUNK] + jnp.concatenate([bias] * group, axis=1)

        top = None
        for at in range(0, span, CHUNK):
            high = jnp.max(piece(at).reshape(CHUNK // 8, 8, cols), axis=0)
            top = high if top is None else jnp.maximum(top, high)
        top = jnp.max(top, axis=0, keepdims=True)
        total = None
        for at in range(0, span, CHUNK):
            ex = jnp.exp2((piece(at) - top) * SCALE2)
            p_buf[slot, at : at + CHUNK] = ex.astype(BF16)
            part = jnp.sum(ex.reshape(CHUNK // 8, 8, cols), axis=0)
            total = part if total is None else total + part
        return top * SCALE2, jnp.sum(total, axis=0, keepdims=True)

    def mix(n, base, total):
        r, u = jobs[n]
        mixed = lax.dot_general(
            kv_buf[r, :, u * pair + HEAD_SIZE : (u + 1) * pair],
            p_buf[n % slots],
            (((0,), (0,)), ((), ())),
            preferred_element_type=F32,
        )
        if has_carry and u == 0:
            copy_carry(r).wait()
        if has_carry:
            stat_in = read_stat(carry_buf.at[r], heads)
        for g in range(group):
            head = u * group + g
            at = slice(head * HEAD_SIZE, (head + 1) * HEAD_SIZE)
            part = slice(g * TOK, (g + 1) * TOK)
            o_g, sum_g, base_g = mixed[:, part], total[:, part], base[:, part]
            if has_carry:
                lse_c = stat_in[head : head + 1]
                high = jnp.maximum(base_g, lse_c)
                w_c = jnp.exp2(lse_c - high)
                w_g = jnp.exp2(base_g - high)
                sum_g = w_c + sum_g * w_g
                norm = 1.0 / sum_g
                out = carry_buf[r, at].astype(F32) * (w_c * norm) + o_g * (w_g * norm)
                base_g = high
            else:
                out = o_g * (1.0 / sum_g)
            _, inner, first = spot(r, head)
            out_buf[r, first + inner : first + inner + HEAD_SIZE] = out.astype(BF16)
            stats[r].append(base_g + jnp.log2(sum_g))
        copy_out(r, u).start()
        share = heads // nouts[r]
        if len(stats[r]) == share:
            part, _, first = spot(r, u * group)
            write_stat(
                out_buf.at[r, first : first + part_rows(share)],
                jnp.concatenate(stats[r], axis=0),
                share,
            )
            stats[r].clear()
            copy_out(r, kv + part).start()

    score(0)
    for n in range(len(jobs)):
        if n + 1 < len(jobs):
            score(n + 1)
        mix(n, *soften(n))
    for r in range(count):
        for u in range(kv + nouts[r]):
            copy_out(r, u).wait()


def attend(
    calls, nouts, shares, plan, q_parts, store, sib, kv_local, fresh=None, carry=None, deps=()
):
    count = len(calls)
    nqs = [len(parts) for parts in q_parts]
    heads = nqs[0] * q_parts[0][0].shape[1] // HEAD_SIZE
    group = heads // kv_local
    rows = part_rows(heads)
    sizes = [part_rows(heads // n) for n in nouts for _ in range(n)]
    room = max(n * part_rows(heads // n) for n in nouts)
    span = 2 * PREFIX_BLOCK_LEN + (TOK if fresh is not None else 0)
    args = [store, sib] + [x for parts in q_parts for x in parts]
    args += list(fresh or ()) + list(carry or ()) + list(deps)
    body = functools.partial(
        attend_kernel, calls, nouts, nqs, shares, group, heads, len(deps), carry is not None,
        fresh is not None,
    )
    any_spec = pl.BlockSpec(memory_space=pl.ANY)
    slots = 3
    out = pl.pallas_call(
        body,
        out_shape=[jax.ShapeDtypeStruct((n, TOK), BF16) for n in sizes],
        in_specs=[pl.BlockSpec(memory_space=pltpu.SMEM)] + [any_spec] * len(args),
        out_specs=[any_spec] * len(sizes),
        scratch_shapes=[
            pltpu.VMEM((count, TOK, heads * HEAD_SIZE), BF16),
            pltpu.VMEM((count, span, kv_local * 2 * HEAD_SIZE), BF16),
            pltpu.VMEM((count, rows, TOK), BF16),
            pltpu.VMEM((count, room, TOK), BF16),
            pltpu.VMEM((count, span, TOK), F32),
            pltpu.VMEM((slots, span, group * TOK), F32),
            pltpu.VMEM((slots, span, group * TOK), BF16),
            pltpu.SemaphoreType.DMA((count, shares, 4)),
            pltpu.SemaphoreType.DMA((count,)),
            pltpu.SemaphoreType.DMA((count, kv_local + max(nouts))),
        ],
        compiler_params=pltpu.CompilerParams(vmem_limit_bytes=VMEM_LIMIT),
        name="attend",
    )(plan, *args)
    out = list(out)
    return [[out.pop(0) for _ in range(n)] for n in nouts]


def merged_heads(heads, part_refs, emit):
    lses = [read_stat(ref, heads) for ref in part_refs]
    high = functools.reduce(jnp.maximum, lses)
    weights = [jnp.exp2(x - high) for x in lses]
    total = functools.reduce(jnp.add, weights)
    norm = 1.0 / total
    weights = [w * norm for w in weights]
    for head in range(heads):
        at = slice(head * HEAD_SIZE, (head + 1) * HEAD_SIZE)
        emit(
            head,
            functools.reduce(
                jnp.add,
                [w[head : head + 1] * ref[at, :].astype(F32) for w, ref in zip(weights, part_refs)],
            ),
        )
    return high + jnp.log2(total)


def merge_kernel(heads, count, *refs):
    refs = refs[: 2 * count] + refs[-count:]
    for i in range(count):
        a_ref, b_ref, out_ref = refs[2 * i], refs[2 * i + 1], refs[2 * count + i]

        def emit(head, value, out_ref=out_ref):
            out_ref[head * HEAD_SIZE : (head + 1) * HEAD_SIZE, :] = value.astype(BF16)

        write_stat(out_ref, merged_heads(heads, (a_ref, b_ref), emit), heads)


def merge(pairs, heads, deps=()):
    shape = pairs[0][0].shape
    spec = pl.BlockSpec(shape, lambda: (0, 0))
    args = [x for pair in pairs for x in pair]
    return pl.pallas_call(
        functools.partial(merge_kernel, heads, len(pairs)),
        out_shape=[jax.ShapeDtypeStruct(shape, BF16)] * len(pairs),
        in_specs=[spec] * len(args) + [pl.BlockSpec(memory_space=pl.ANY)] * len(deps),
        out_specs=[spec] * len(pairs),
        compiler_params=pltpu.CompilerParams(vmem_limit_bytes=VMEM_LIMIT),
        name="merge",
    )(*args, *deps)


def project_kernel(heads, counts, spans, streams, tile, col0, *refs):
    refs = list(refs)
    part_refs = [refs.pop(0) for _ in range(sum(counts))]
    w_ref = refs.pop(0)
    add_refs = [refs.pop(0) for _ in spans]
    out_ref, attn_ref, parts_ref, w_buf, part_sem, w_sem = refs[-6:]
    j = pl.program_id(0)
    count = pl.num_programs(0)
    ahead = w_buf.shape[0]
    depth = w_buf.shape[1] // streams

    def weight_copies(t):
        slot = lax.rem(t, ahead)
        cols = pl.ds(pl.multiple_of(col0 + t * tile, tile), tile)
        return [
            pltpu.make_async_copy(
                w_ref.at[pl.ds(i * depth, depth), cols],
                w_buf.at[slot, pl.ds(i * depth, depth)],
                w_sem.at[slot, i],
            )
            for i in range(streams)
        ]

    @pl.when(j == 0)
    def _():
        copies = [
            pltpu.make_async_copy(ref, parts_ref.at[i], part_sem.at[i])
            for i, ref in enumerate(part_refs)
        ]
        for copy in copies:
            copy.start()
        for t in range(ahead - 1):
            for copy in weight_copies(t):
                copy.start()
        for copy in copies:
            copy.wait()

        first = 0
        for share, n in enumerate(counts):

            def emit(head, value, base=share * heads):
                cols = slice((base + head) * HEAD_SIZE, (base + head + 1) * HEAD_SIZE)
                attn_ref[:, cols] = value.T.astype(BF16)

            merged_heads(heads, [parts_ref.at[i] for i in range(first, first + n)], emit)
            first += n

    @pl.when(j + ahead - 1 < count)
    def _():
        for copy in weight_copies(j + ahead - 1):
            copy.start()

    for copy in weight_copies(j):
        copy.wait()
    got = jnp.dot(attn_ref[...], w_buf[lax.rem(j, ahead)], preferred_element_type=F32)
    got = got.astype(BF16)
    if spans:
        total = got.astype(F32)
        for ref, (low, high) in zip(add_refs, spans):
            here = (j >= low) & (j < high)
            total = total + jnp.where(here, ref[...].astype(F32), 0.0)
        got = total.astype(BF16)
    out_ref[...] = got


def project(shared, weight, adds=(), deps=(), col0=0, cols=None):
    parts = [x for group in shared for x in group]
    depth = weight.shape[0]
    cols = weight.shape[1] if cols is None else cols
    heads = depth // HEAD_SIZE // len(shared)
    tile = 1024
    count = cols // tile
    ahead = min(4, count)
    streams = 4
    in_specs = [pl.BlockSpec(memory_space=pl.ANY)] * (len(parts) + 1)
    args = parts + [weight]
    spans = []
    for x, first in adds:
        low, n = first // tile, x.shape[1] // tile
        spans.append((low, low + n))
        in_specs.append(
            pl.BlockSpec((TOK, tile), lambda j, low=low, n=n: (0, jnp.clip(j - low, 0, n - 1)))
        )
        args.append(x)
    in_specs += [pl.BlockSpec(memory_space=pl.ANY)] * len(deps)
    args += deps
    return pl.pallas_call(
        functools.partial(
            project_kernel, heads, [len(group) for group in shared], spans, streams, tile, col0
        ),
        out_shape=jax.ShapeDtypeStruct((TOK, cols), BF16),
        grid=(count,),
        in_specs=in_specs,
        out_specs=pl.BlockSpec((TOK, tile), lambda j: (0, j)),
        scratch_shapes=[
            pltpu.VMEM((TOK, depth), BF16),
            pltpu.VMEM((len(parts),) + parts[0].shape, BF16),
            pltpu.VMEM((ahead, depth, tile), BF16),
            pltpu.SemaphoreType.DMA((len(parts),)),
            pltpu.SemaphoreType.DMA((ahead, streams)),
        ],
        compiler_params=pltpu.CompilerParams(vmem_limit_bytes=VMEM_LIMIT),
        name="project",
    )(*args)


def shards(
    queries, new_key_values, key_value_store, o_weight, residual, hit_dev, hit_blk, prefix_len
):
    npool = lax.axis_size("pool")
    ntp = lax.axis_size("tp")
    me = lax.axis_index("pool")
    tp = lax.axis_index("tp")
    rdev = queries.shape[0] // TOK
    kv_local = key_value_store.shape[2] // (2 * HEAD_SIZE)
    nchips = npool // 2
    core = lax.rem(me, 2)
    chip = lax.div(me, 2)
    sibling = me + 1 - 2 * core
    ring = chip_ring(nchips)
    place = [ring.index(i) for i in range(nchips)]
    split_rows = ntp == rdev and rdev == 2

    swap_perm = [(p, p + 1 - 2 * (p % 2)) for p in range(npool)]
    cw_perm, ccw_perm = [], []
    for k in range(nchips):
        a, b = ring[k], ring[(k + 1) % nchips]
        for c in range(2):
            cw_perm.append((2 * a + c, 2 * b + c))
            ccw_perm.append((2 * b + c, 2 * a + c))

    starts = jnp.arange(MAXB, dtype=jnp.int32)[None, :] * PREFIX_BLOCK_LEN
    left = jnp.clip(prefix_len[:, None] - starts, 0, PREFIX_BLOCK_LEN)
    here, beside = hit_dev == me, hit_dev == sibling
    table = jnp.stack(
        [
            jnp.sum(jnp.where(at, x, 0), axis=1)
            for x, at in ((hit_blk, here), (hit_blk, beside), (left, here), (left, beside))
        ],
        axis=1,
    )
    half = nchips // 2
    steps = list(range(-half, half + 1))
    spot = jnp.asarray(place, jnp.int32)[chip]
    chips_at = jnp.asarray(ring, jnp.int32)[
        lax.rem(spot + nchips - jnp.asarray(steps, jnp.int32), nchips)
    ]
    slots = [1 - tp, tp] if split_rows else [jnp.int32(i) for i in range(rdev)]
    wanted = ((chips_at * 2 + core) * rdev)[None, :] + jnp.stack(slots)[:, None]
    plan = jnp.take(table, wanted.reshape(-1), axis=0, mode="clip").reshape(-1)
    sib = lax.ppermute(key_value_store, "pool", swap_perm)

    heads = queries.shape[1] // HEAD_SIZE
    nq = 2 if kv_local % 2 == 0 else 1
    width = heads // nq * HEAD_SIZE

    def travel(x, hops_cw, hops_ccw, held, key):
        for sign, perm, hops in ((1, cw_perm, hops_cw), (-1, ccw_perm, hops_ccw)):
            moving = x
            for t in range(1, hops + 1):
                moving = lax.ppermute(moving, "pool", perm)
                held[sign * t, key] = moving

    def reach(flip):
        if nchips % 2:
            return half, half
        return (half - 1, half) if flip else (half, half - 1)

    q_of, fresh_of = [], []
    for order, slot in enumerate(slots):
        held = {}
        fresh_of.append(lax.dynamic_slice_in_dim(new_key_values, slot * TOK, TOK, 0))
        if order == 0:
            for part in range(nq):
                q = lax.dynamic_slice(queries, (slot * TOK, part * width), (TOK, width))
                held[0, part] = q
                travel(q, *reach(part % 2), held, part)
            before = [
                held[t, part] for t in (half - 1, 1 - half) for part in range(nq) if half > 1
            ]
            for part in range(nq):
                far = [held[t, part] for t in (half, -half) if (t, part) in held]
                for t in (half, -half):
                    if far:
                        held.setdefault((t, part), far[0])
            q_of.append({t: [held.get((t, part)) for part in range(nq)] for t in steps})
        else:
            q = take_rows(queries, slot, before)
            travel(q, *reach(False), held, 0)
            held[0, 0] = q
            q_of.append({t: [x] for (t, _), x in held.items()})

    nouts = [1] + [NOUT] * (rdev - 1)

    def run(wanted, **more):
        calls = [order * len(steps) + steps.index(t) for order, t in wanted]
        return attend(
            calls, [nouts[order] for order, _ in wanted], nq, plan,
            [q_of[order][t] for order, t in wanted], key_value_store, sib, kv_local, **more,
        )

    carry = {}
    hops = dict(zip((1, -1), reach(False)))
    back = {1: ccw_perm, -1: cw_perm}
    early = {}
    ready = list({id(x): x for t in steps if t for x in q_of[0][t] if x is not None}.values())
    for i in range(half):
        for sign in (1, -1):
            t = hops[sign] - i
            if t > 0:
                more = {"carry": [carry[sign]]} if i else {}
                ((x,),) = run([(0, sign * t)], deps=ready, **more)
                carry[sign] = lax.ppermute(x, "pool", back[sign])
                ready = [x]
        if i == 0:
            own = run([(order, 0) for order in range(rdev)], fresh=fresh_of, deps=ready)
            ready = own[0]
        reached = [i] if i < half - 1 else [i, half]
        wanted = [
            (order, t) for order in range(1, rdev) for r in reached if r for t in (r, -r)
            if t in q_of[order]
        ]
        if wanted:
            got = run(wanted, deps=ready)
            early.update(zip(wanted, got))
            ready = [got[0][0]]
    parts = [[own[0][0]] + list(carry.values())]

    shares = heads // NOUT
    for order in range(1, rdev):
        for t in (half, -half):
            if (order, t) not in early and (order, -t) in early:
                early[order, t] = early[order, -t]
    moving = {}
    away = []
    model = o_weight.shape[1]

    got = []

    def project_half(deps):
        at = len(away) * (model // 2)
        away.append(project([parts[0]], o_weight, deps=deps, col0=at, cols=model // 2))
        if split_rows:
            got.append((lax.ppermute(away[-1], "tp", [(0, 1), (1, 0)]), at))
        return [away[-1]]

    ready = project_half(ready)
    for i in range(half):
        for order in range(1, rdev):
            for part in range(NOUT):
                counts = dict(zip((1, -1), reach(part % 2)))
                for sign in (1, -1):
                    if counts[sign] <= i:
                        continue
                    x = early[order, sign * (counts[sign] - i)][part]
                    if i:
                        wait = [y for y, _ in got[:1]] if (i, sign) in AFTER_FIRST else []
                        (x,) = merge([(x, moving[order, part, sign])], shares, deps=ready + wait)
                        if len(away) == 1:
                            ready = project_half([x])
                    moving[order, part, sign] = lax.ppermute(x, "pool", back[sign])
    if len(away) == 1:
        project_half(ready)
    ends = [
        [
            [own[order][part]]
            + [moving[order, part, sign] for sign in (1, -1) if (order, part, sign) in moving]
            for part in range(NOUT)
        ]
        for order in range(1, rdev)
    ]
    if split_rows:
        return project(ends[0], o_weight, got + [(residual, 0)])
    rows = [jnp.concatenate(away, axis=1)] + [project(x, o_weight) for x in ends]
    mine = lax.psum_scatter(
        jnp.concatenate(rows, axis=0), "tp", scatter_dimension=0, tiled=True
    )
    return (mine.astype(F32) + residual.astype(F32)).astype(BF16)


def solution(mesh):
    placed = (
        P("pool", "tp"),
        P("pool", "tp"),
        P("pool", None, "tp"),
        P("tp", None),
        P(("pool", "tp"), None),
        P(),
        P(),
        P(),
    )
    return jax.shard_map(
        shards, mesh=mesh, in_specs=placed, out_specs=P(("pool", "tp"), None), check_vma=False
    )
```
